32 devices in a mesh: section: 4 (over x, core), dp: 4 (over z), tensor: 2 (over y).
Axes of the slice: x: 2, y: 2, z: 4, core: 2. Of those that a mesh axis runs over, the one named last changes fastest.
Arguments:
- inputs: bfloat16 [8, 1024, 768], P('dp', ('section', 'tensor')), may hold values from -6 to 6
- cotangent: bfloat16 [8, 1024, 768], P('dp', ('section', 'tensor')), may hold values from -6 to 6
- subset_ids: int32 [8], P('dp'), may hold values from 0 to 21
- subset_weight: float32 [22], replicated, may hold values from 0.25 to 4
- ln_gain: float32 [4, 2, 2, 768], P('section'), may hold values from 0.5 to 1.5
- ln_bias: float32 [4, 2, 2, 768], P('section'), may hold values from -2 to 2
- w_query: bfloat16 [4, 2, 768, 768], P('section', None, None, 'tensor'), may hold values from -0.21875 to 0.21875
- b_query: float32 [4, 2, 768], P('section', None, 'tensor'), may hold values from -2 to 2
- w_kv: bfloat16 [4, 768, 128], P('section'), may hold values from -0.21875 to 0.21875
- b_kv: float32 [4, 128], P('section'), may hold values from -2 to 2
- w_out: bfloat16 [4, 2, 768, 768], P('section', None, 'tensor'), may hold values from -0.75 to 0.75
- out_bias: float32 [4, 2, 2, 768], P('section'), may hold values from -2 to 2
- w_in: bfloat16 [4, 2, 768, 3072], P('section', None, None, 'tensor'), may hold values from -0.21875 to 0.21875
- b_in: float32 [4, 2, 3072], P('section', None, 'tensor'), may hold values from -2 to 2
- w_hid_out: bfloat16 [4, 2, 3072, 768], P('section', None, 'tensor'), may hold values from -0.109375 to 0.109375
Outputs:
- final: bfloat16 [8, 1024, 768], P('dp', ('section', 'tensor'))
- input_grad: float32 [8, 1024, 768], P('dp', ('section', 'tensor'))
- grad_ln_gain: float32 [4, 2, 2, 768], P('section')
- grad_ln_bias: float32 [4, 2, 2, 768], P('section')
- grad_w_query: float32 [4, 2, 768, 768], P('section', None, None, 'tensor')
- grad_b_query: float32 [4, 2, 768], P('section', None, 'tensor')
- grad_w_kv: float32 [4, 768, 128], P('section')
- grad_b_kv: float32 [4, 128], P('section')
- grad_w_out: float32 [4, 2, 768, 768], P('section', None, 'tensor')
- grad_out_bias: float32 [4, 2, 2, 768], P('section')
- grad_w_in: float32 [4, 2, 768, 3072], P('section', None, None, 'tensor')
- grad_b_in: float32 [4, 2, 3072], P('section', None, 'tensor')
- grad_w_hid_out: float32 [4, 2, 3072, 768], P('section', None, 'tensor')
The draws below stay inside these ranges and needn't reach their ends.
All inputs are finite; a program needn't handle non-finite values.
Results may differ from the reference program's by a relative error of at most 0.025.
Values may be sent and summed in bfloat16 or wider, within the bound.
No kernel may reach another device: no remote copies, remote signals or barrier semaphores. Data moves between devices by JAX's collectives and lax.ppermute only.
A program may use at most 320 MiB of HBM per device.

```python
import math
import jax
import jax.numpy as jnp
from jax import lax

D = 768
HEADS = 12
HD = 64
ROT = 16
FF = 3072
LEN = 1024
SUBSETS = 22
SEQS = 8
N_SECTION = 4


def touch_ends(values, key, low, high):
    place = [jax.random.randint(jax.random.fold_in(key, axis), (), 0, length) for axis, length in enumerate(values.shape)]
    main_axis = values.shape.index(max(values.shape))
    neighbour = place[:main_axis] + [(place[main_axis] + 1) % values.shape[main_axis]] + place[main_axis + 1:]
    return values.at[tuple(place)].set(low).at[tuple(neighbour)].set(high)


def block_scale(rng, extent, shards, smallest, largest):
    level, own = 1.0, jax.random.fold_in(rng, 6)
    for dim, blocks in shards:
        steps = jnp.exp(jax.random.uniform(jax.random.fold_in(own, dim), (blocks,), jnp.float32, smallest / len(shards), largest / len(shards)))
        level = level * jnp.repeat(steps, extent[dim] // blocks).reshape([-1 if axis == dim else 1 for axis in range(len(extent))])
    return level


def gaussian(rng, shape, scale, bound, cuts=(), held_as=jnp.bfloat16):
    level = block_scale(rng, shape, cuts, -0.22, 0.18) if cuts else 1.0
    entries = jax.random.normal(rng, shape, jnp.float32) * scale * level
    return jnp.minimum(jnp.maximum(entries, -bound), bound).astype(held_as)


def setup_inputs(seed: int = 0) -> dict:
    splits = jax.random.split(jax.random.key(seed), 16)
    return {
        "inputs": gaussian(splits[0], (SEQS, LEN, D), 1.0, 6.0, ((0, 4), (1, 8))),
        "cotangent": gaussian(splits[1], (SEQS, LEN, D), 1.0, 6.0, ((0, 4), (1, 8))),
        "subset_ids": touch_ends(jax.random.randint(splits[2], (SEQS,), 0, SUBSETS), jax.random.fold_in(splits[2], 1), 0, SUBSETS - 1).astype(jnp.int32),
        "subset_weight": jnp.clip(jnp.exp(jax.random.uniform(splits[3], (SUBSETS,), jnp.float32, math.log(0.25), math.log(4.0))), 0.25, 4.0),
        "ln_gain": jnp.clip(1.0 + 0.1 * jax.random.normal(splits[4], (N_SECTION, 2, 2, D), jnp.float32), 0.5, 1.5),
        "ln_bias": gaussian(splits[5], (N_SECTION, 2, 2, D), 0.3, 2.0, ((0, 4),), jnp.float32),
        "w_query": gaussian(splits[6], (N_SECTION, 2, D, HEADS * HD), D ** -0.5, 0.21875, ((0, 4), (3, 2))),
        "b_query": gaussian(splits[7], (N_SECTION, 2, HEADS * HD), 0.3, 2.0, ((0, 4), (2, 2)), jnp.float32),
        "w_kv": gaussian(splits[8], (N_SECTION, D, 2 * HD), D ** -0.5, 0.21875, ((0, 4),)),
        "b_kv": gaussian(splits[9], (N_SECTION, 2 * HD), 0.3, 2.0, ((0, 4),), jnp.float32),
        "w_out": gaussian(splits[10], (N_SECTION, 2, HEADS * HD, D), HD ** -0.5, 0.75, ((0, 4), (2, 2))),
        "out_bias": gaussian(splits[11], (N_SECTION, 2, 2, D), 0.3, 2.0, ((0, 4),), jnp.float32),
        "w_in": gaussian(splits[12], (N_SECTION, 2, D, FF), D ** -0.5, 0.21875, ((0, 4), (3, 2))),
        "b_in": gaussian(splits[13], (N_SECTION, 2, FF), 0.3, 2.0, ((0, 4), (2, 2)), jnp.float32),
        "w_hid_out": gaussian(splits[14], (N_SECTION, 2, FF, D), FF ** -0.5, 0.109375, ((0, 4), (2, 2))),
    }


EPS = 1e-05
HIGH = lax.Precision.HIGHEST

@jax.custom_vjp
def low(v):
    return lax.optimization_barrier(v.astype(jnp.bfloat16)).astype(jnp.float32)

@jax.custom_vjp
def low_back(v):
    return v

def low_keep(v):
    return (low(v), None)

def low_pass(kept, grad):
    return (grad,)

def back_keep(v):
    return (v, None)

def back_low(kept, grad):
    return (low(grad),)
low.defvjp(low_keep, low_pass)
low_back.defvjp(back_keep, back_low)

def product(left, right):
    return jnp.dot(left, right, precision=HIGH, preferred_element_type=jnp.float32)

def layer_norm(hidden, gain, bias):
    centre = lax.optimization_barrier(jnp.mean(hidden, axis=-1, keepdims=True))
    centred = hidden - centre
    spread = lax.optimization_barrier(jnp.mean(centred * centred, axis=-1, keepdims=True))
    return centred * lax.rsqrt(spread + EPS) * gain + bias

def rope_tables(length, width):
    column = jnp.arange(width) % HD
    half = ROT // 2
    freq = jnp.power(10000.0, -2.0 * (column % half).astype(jnp.float32) / ROT)
    angle = jnp.arange(length).astype(jnp.float32)[:, None] * freq[None, :]
    turning = (column < ROT)[None, :]
    return (jnp.where(turning, jnp.cos(angle), 1.0), jnp.where(turning, jnp.sin(angle), 0.0))

def rotate(values, cosines, sines):
    column = jnp.arange(values.shape[-1]) % HD
    half = ROT // 2
    ahead = jnp.roll(values, -half, axis=-1)
    behind = jnp.roll(values, half, axis=-1)
    turned = jnp.where(column < half, -ahead, jnp.where(column < ROT, behind, 0.0))
    return values * cosines + turned * sines

def attend_block(query_rows, keys, values, first, heads):
    block = query_rows.shape[0]
    reach = keys.shape[0]
    rows = query_rows.reshape(block * heads, HD)
    scores = low_back(jnp.dot(rows, keys.T, precision=HIGH) * HD ** (-0.5))
    query_pos = first + jnp.arange(block * heads) // heads
    visible = jnp.arange(reach)[None, :] <= query_pos[:, None]
    scores = jnp.where(visible, scores, -1e+30)
    top = lax.optimization_barrier(jnp.max(scores, axis=1, keepdims=True))
    expo = jnp.exp(scores - top)
    probs = expo / lax.optimization_barrier(jnp.sum(expo, axis=1, keepdims=True))
    return product(low(probs), values).reshape(block, heads * HD)

def attend(query, keys, values):
    length = query.shape[0]
    heads = query.shape[1] // HD
    block = min(length, 512)
    pieces = []
    for number in range(length // block):
        reach = (number + 1) * block
        pieces.append(jax.checkpoint(attend_block, static_argnums=(3, 4))(query[number * block:reach], keys[:reach], values[:reach], number * block, heads))
    return jnp.concatenate(pieces, axis=0)

def layer(hidden, slot, shared, kv_weights, tables):
    gains, biases, w_q, b_q, w_o, o_bias, w_i, b_i, w_h = slot
    first = low(layer_norm(hidden, gains[0], biases[0]))
    second = low(layer_norm(hidden, gains[1], biases[1]))
    if kv_weights is not None:
        kv_lin = product(first, kv_weights[0]) + kv_weights[1]
        shared = (low(rotate(low_back(kv_lin[:, :HD]), tables[2], tables[3])), low(low_back(kv_lin[:, HD:])))
    query = low(rotate(low_back(product(first, w_q) + b_q), tables[0], tables[1]))
    attended = low(low_back(attend(query, shared[0], shared[1])))
    act = low(jax.nn.gelu(low_back(product(second, w_i) + b_i), approximate=False))
    branch = low_back(product(attended, w_o) + product(act, w_h))
    return (hidden + branch + o_bias[0] + o_bias[1], shared)

def sequence_forward(hidden, params):
    ln_gain, ln_bias, w_query, b_query, w_kv, b_kv, w_out, out_bias, w_in, b_in, w_hid_out = params
    length = hidden.shape[0]
    tables = rope_tables(length, HEADS * HD) + rope_tables(length, HD)
    for section in range(N_SECTION):
        if section > 0:
            hidden = low_back(low(hidden))
        slots = [(ln_gain[section, slot], ln_bias[section, slot], w_query[section, slot], b_query[section, slot], w_out[section, slot], out_bias[section, slot], w_in[section, slot], b_in[section, slot], w_hid_out[section, slot]) for slot in range(2)]
        hidden, shared = layer(hidden, slots[0], None, (w_kv[section], b_kv[section]), tables)
        hidden, unused = layer(hidden, slots[1], shared, None, tables)
    return hidden

def reference(inputs, cotangent, subset_ids, subset_weight, ln_gain, ln_bias, w_query, b_query, w_kv, b_kv, w_out, out_bias, w_in, b_in, w_hid_out):
    floats = tuple((item.astype(jnp.float32) for item in (ln_gain, ln_bias, w_query, b_query, w_kv, b_kv, w_out, out_bias, w_in, b_in, w_hid_out)))
    table = subset_weight.astype(jnp.float32)
    subjects = jnp.arange(SUBSETS).astype(jnp.int32)

    def one(totals, item):
        seq_in, seq_cot, seq_id = item
        weight = jnp.sum(jnp.where(subjects == seq_id.astype(jnp.int32), table, 0.0))
        result, pull = jax.vjp(sequence_forward, seq_in.astype(jnp.float32), floats)
        grad_in, grad_params = pull(seq_cot.astype(jnp.float32) * weight)
        totals = jax.tree.map(jnp.add, totals, grad_params)
        return (totals, (result.astype(jnp.bfloat16), grad_in))
    start = jax.tree.map(jnp.zeros_like, floats)
    grads, outputs = lax.scan(one, start, (inputs, cotangent, subset_ids))
    return (outputs[0], outputs[1], grads[0], grads[1], grads[2], grads[3], grads[4], grads[5], grads[6], grads[7], grads[8], grads[9], grads[10])
```

```python
import functools
import jax
import jax.numpy as jnp
from jax import lax
from jax.experimental import pallas as pl
from jax.experimental.pallas import tpu as pltpu
from jax.sharding import PartitionSpec as P

HD = 64
ROT = 16
EPS = 1e-05
LANES = 128
TILE = 256
ROWS = 256
VMEM_LIMIT = 56 * 2**20
ANY = pl.BlockSpec(memory_space=pl.ANY)
SMEM = pl.BlockSpec(memory_space=pltpu.SMEM)
VMEM = pl.BlockSpec(memory_space=pltpu.VMEM)
BF16, F32 = jnp.bfloat16, jnp.float32


def dot(left, right, dims=((1,), (0,))):
    return lax.dot_general(left, right, (dims, ((), ())), preferred_element_type=F32)


def dot_nt(left, right):
    return dot(left, right, ((1,), (1,)))


def turn(values, cosines, ahead, behind):
    return (
        values * cosines
        + pltpu.roll(values, LANES - ROT // 2, axis=1) * ahead
        + pltpu.roll(values, ROT // 2, axis=1) * behind
    )


def normalized(rows):
    centred = rows - jnp.mean(rows, axis=-1, keepdims=True)
    scale = lax.rsqrt(jnp.mean(centred * centred, axis=-1, keepdims=True) + EPS)
    return centred * scale, scale


def split_pair(block):
    low = lax.broadcasted_iota(jnp.int32, block.shape, 1) < HD
    zero = jnp.zeros_like(block)
    return jnp.where(low, block, zero), jnp.where(low, zero, block)


def visible(rows):
    key = lax.broadcasted_iota(jnp.int32, (rows, rows), 0)
    return key <= lax.broadcasted_iota(jnp.int32, (rows, rows), 1)


class Copies:
    def __init__(self, sems):
        self.sems, self.used, self.open = sems, 0, []

    def start(self, source, target):
        copy = pltpu.make_async_copy(source, target, self.sems.at[self.used])
        self.used += 1
        copy.start()
        return copy

    def later(self, source, target):
        self.open.append(self.start(source, target))

    def finish(self):
        for copy in self.open:
            copy.wait()
        self.open = []


FWD_STATE = ("x0", "x1", "h1a", "h1b", "h2a", "h2b", "qa", "qb", "oa", "ob", "aa", "ab", "ga", "gb", "la", "lb", "kd", "vd", "kt", "vt", "y")
BWD_STATE = ("dba", "dbb", "dua", "dub", "dqa", "dqb", "dkv", "dkw", "dvw", "acc", "gin")


def state_shapes(length, width, hidden):
    pairs = width // LANES
    row, ff = ((length, width), BF16), ((length, hidden), BF16)
    lse, wide, tall = ((pairs, 8, length), F32), ((length, LANES), BF16), ((HD, length), BF16)
    fwd = dict(x0=row, x1=((length, width), F32), h1a=row, h1b=row, h2a=row, h2b=row, qa=row, qb=row, oa=row, ob=row, aa=ff, ab=ff, ga=ff, gb=ff, la=lse, lb=lse, kd=wide, vd=wide, kt=tall, vt=tall, y=row)
    total = ((length, LANES), F32)
    bwd = dict(dba=row, dbb=row, dua=ff, dub=ff, dqa=row, dqb=row, dkv=wide, dkw=total, dvw=total, acc=((24, width), F32), gin=row)
    return fwd, bwd


def make_struct(item):
    return jax.ShapeDtypeStruct(*item)


def fwd_kernel(rows, chunks, fresh, *refs):
    n_state = len(FWD_STATE)
    sc, hop_in, seq_in, common, bq_m, bq_t, bi_m, bi_t, cos, ahead, behind, wkv = refs[:12]
    weights = refs[12:20]
    at = 20 if fresh else 20 + n_state
    st = dict(zip(FWD_STATE, refs[at : at + n_state]))
    hop_out = refs[at + n_state]
    (x_s, xf_s, h1_s, h2_s, q_s, o_s, a_s, g_s, l_s, kd_s, vd_s, kt_s, vt_s, vtc_s, wq_s, wo_s, wi_s, wh_s, sems, wsems) = refs[at + n_state + 1 :]
    width = xf_s.shape[1]
    half, hid = wq_s.shape[3], wi_s.shape[3]
    biases = ((bq_m, bi_m), (bq_t, bi_t))

    @pl.when(sc[0] == 1)
    def _():
        m = sc[1]
        place = pl.ds(pl.multiple_of(m * rows, rows), rows)
        copies, loads = Copies(sems), Copies(wsems)

        @pl.when(sc[2] == 1)
        def _():
            pltpu.make_async_copy(seq_in.at[place], x_s, sems.at[50]).start()

        @pl.when(sc[2] == 0)
        def _():
            pltpu.make_async_copy(hop_in, x_s, sems.at[50]).start()

        kd_in = copies.start(st["kd"], kd_s)
        vt_in = copies.start(st["vt"], vt_s)
        got = {}
        for j in range(2):
            for n, (name, buf) in enumerate((("q", wq_s), ("o", wo_s), ("i", wi_s), ("h", wh_s))):
                for k in range(2):
                    got[name, k, j] = loads.start(weights[2 * n + k].at[j], buf.at[k, j])
        pltpu.make_async_copy(hop_in, x_s, sems.at[50]).wait()
        xf_s[...] = x_s[...].astype(F32)
        copies.later(x_s, st["x0"].at[place])
        tables = (cos[place, :], ahead[place, :], behind[place, :])
        for j in range(2):
            for r in range(0, rows, 64):
                hat, _ = normalized(xf_s[r : r + 64, :])
                h1_s[j, r : r + 64, :] = (hat * common[2 * j : 2 * j + 1, :] + common[4 + 2 * j : 5 + 2 * j, :]).astype(BF16)
                h2_s[j, r : r + 64, :] = (hat * common[2 * j + 1 : 2 * j + 2, :] + common[5 + 2 * j : 6 + 2 * j, :]).astype(BF16)
            copies.later(h1_s.at[j], st["h1" + "ab"[j]].at[place])
            copies.later(h2_s.at[j], st["h2" + "ab"[j]].at[place])
            h1 = h1_s[j]
            if j == 0:
                kv = dot(h1, wkv[...]) + common[12:13, :TILE]
                keys, values = turn(kv[:, :LANES], *tables), kv[:, LANES:]
                kd_in.wait()
                vt_in.wait()
                kd_s[place, :] = keys.astype(BF16)
                vd_s[...] = values.astype(BF16)
                kt_s[...] = jnp.transpose(keys)[:HD].astype(BF16)
                vtc_s[...] = jnp.transpose(values)[:HD].astype(BF16)
                vt_s[:, place] = vtc_s[...]
                copies.later(kd_s.at[place], st["kd"].at[place])
                copies.later(vd_s, st["vd"].at[place])
                copies.later(kt_s, st["kt"].at[:, place])
                copies.later(vtc_s, st["vt"].at[:, place])
            for k in range(2):
                got["q", k, j].wait()
                query = dot(h1, wq_s[k, j]) + biases[k][0][j : j + 1, :]
                for b in range(half // LANES):
                    block = turn(query[:, b * LANES : (b + 1) * LANES], *tables) * HD**-0.5
                    col = k * half + b * LANES
                    q_s[j, :, col : col + LANES] = block.astype(BF16)
            copies.later(q_s.at[j], st["q" + "ab"[j]].at[place])

            def attend(before):
                def pair(i, _):
                    cols = pl.ds(pl.multiple_of(i * LANES, LANES), LANES)
                    outs = []
                    for n, query in enumerate(split_pair(q_s[j, :, cols])):
                        diag = dot_nt(kd_s[before : before + rows, :], query)
                        diag = jnp.where(visible(rows), diag, -1e30)
                        top = jnp.max(diag, axis=0, keepdims=True)
                        if before:
                            past = dot_nt(kd_s[:before, :], query)
                            top = jnp.maximum(top, jnp.max(past, axis=0, keepdims=True))
                        expo = jnp.exp(diag - top)
                        summed = jnp.sum(expo, axis=0, keepdims=True)
                        out = dot(vt_s[:, before : before + rows], expo.astype(BF16))
                        if before:
                            expo = jnp.exp(past - top)
                            summed += jnp.sum(expo, axis=0, keepdims=True)
                            out += dot(vt_s[:, :before], expo.astype(BF16))
                        outs.append(out / summed)
                        l_s[j, i, n : n + 1, :] = top + jnp.log(summed)
                    o_s[j, :, cols] = jnp.transpose(jnp.concatenate(outs, axis=0)).astype(BF16)
                    return 0

                lax.fori_loop(0, width // LANES, pair, 0)

            for c in range(chunks):
                pl.when(m == c)(functools.partial(attend, c * rows))
            copies.later(o_s.at[j], st["o" + "ab"[j]].at[place])
            copies.later(l_s.at[j], st["l" + "ab"[j]].at[:, :, place])
            for k in range(2):
                got["i", k, j].wait()
                for n in range(hid // TILE):
                    cols = slice(n * TILE, (n + 1) * TILE)
                    before = dot(h2_s[j], wi_s[k, j, :, cols]) + biases[k][1][j : j + 1, cols]
                    normal = 0.5 + 0.5 * lax.erf(before * 0.5**0.5)
                    col = k * hid + n * TILE
                    a_s[j, :, col : col + TILE] = (before * normal).astype(BF16)
                    slope = normal + before * (jnp.exp(-0.5 * before * before) * 0.3989422804014327)
                    g_s[j, :, col : col + TILE] = slope.astype(BF16)
            copies.later(a_s.at[j], st["a" + "ab"[j]].at[place])
            copies.later(g_s.at[j], st["g" + "ab"[j]].at[place])
            for k in range(2):
                got["o", k, j].wait()
                got["h", k, j].wait()
                branch = dot(o_s[j, :, k * half : (k + 1) * half], wo_s[k, j])
                branch += dot(a_s[j, :, k * hid : (k + 1) * hid], wh_s[k, j])
                if k == 0:
                    branch += common[8 + 2 * j : 9 + 2 * j, :] + common[9 + 2 * j : 10 + 2 * j, :]
                if j == 1 and k == 0:
                    x1_out.wait()
                xf_s[...] += branch
            if j == 0:
                x1_out = copies.start(xf_s, st["x1"].at[place])
        copies.finish()
        x_s[...] = xf_s[...].astype(BF16)
        copies.later(x_s, st["y"].at[place])
        copies.later(x_s, hop_out)
        copies.finish()


def fwd_call(rows, chunks, state, sc, hop, seq, params, weights):
    common, bq_m, bq_t, bi_m, bi_t, cos, ahead, behind, wkv = params
    length, width = seq.shape
    half, hid = weights[0].shape[2], weights[4].shape[2]
    hidden = 2 * hid
    shapes, _ = state_shapes(length, width, hidden)
    fresh = state is None
    n = len(FWD_STATE)
    scratch = [
        pltpu.VMEM((rows, width), BF16),
        pltpu.VMEM((rows, width), F32),
        pltpu.VMEM((2, rows, width), BF16),
        pltpu.VMEM((2, rows, width), BF16),
        pltpu.VMEM((2, rows, width), BF16),
        pltpu.VMEM((2, rows, width), BF16),
        pltpu.VMEM((2, rows, hidden), BF16),
        pltpu.VMEM((2, rows, hidden), BF16),
        pltpu.VMEM((2, width // LANES, 8, rows), F32),
        pltpu.VMEM((length, LANES), BF16),
        pltpu.VMEM((rows, LANES), BF16),
        pltpu.VMEM((HD, rows), BF16),
        pltpu.VMEM((HD, length), BF16),
        pltpu.VMEM((HD, rows), BF16),
        pltpu.VMEM((2, 2, width, half), BF16),
        pltpu.VMEM((2, 2, half, width), BF16),
        pltpu.VMEM((2, 2, width, hid), BF16),
        pltpu.VMEM((2, 2, hid, width), BF16),
        pltpu.SemaphoreType.DMA((51,)),
        pltpu.SemaphoreType.DMA((16,)),
    ]
    outs = pl.pallas_call(
        functools.partial(fwd_kernel, rows, chunks, fresh),
        out_shape=[make_struct(shapes[k]) for k in FWD_STATE] + [jax.ShapeDtypeStruct((rows, width), BF16)],
        in_specs=[SMEM, ANY, ANY] + [VMEM] * 9 + [ANY] * (8 + (0 if fresh else n)),
        out_specs=[ANY] * (n + 1),
        scratch_shapes=scratch,
        input_output_aliases={} if fresh else {20 + i: i for i in range(n)},
        compiler_params=pltpu.CompilerParams(vmem_limit_bytes=VMEM_LIMIT),
        name="section_forward",
    )(sc, hop, seq, common, bq_m, bq_t, bi_m, bi_t, cos, ahead, behind, wkv, *weights, *([] if fresh else state))
    return outs[:n], outs[n]


READ = ("x0", "x1", "qa", "qb", "oa", "ob", "ga", "gb", "la", "lb", "kd", "vd", "kt")


def bwd_kernel(rows, chunks, fresh, *refs):
    n_read, n_state = len(READ), len(BWD_STATE)
    sc, scale, hop_in, cot, common, cos, ahead, behind, wkv = refs[:9]
    weights = refs[9:17]
    rd = dict(zip(READ, refs[17 : 17 + n_read]))
    at = 17 + n_read + (0 if fresh else n_state)
    st = dict(zip(BWD_STATE, refs[at : at + n_state]))
    hop_out = refs[at + n_state]
    (in_s, dy_s, x0_s, x1_s, q_s, o_s, g_s, l_s, kd_s, vd_s, kt_s, db_s, do_s, du_s, dql_s, dkv_s, dkw_s, dvw_s, dh1_s, dh2_s, acc_s, wq_s, wo_s, wi_s, wh_s, sems, wsems) = refs[at + n_state + 1 :]
    width = dy_s.shape[1]
    half, hid = wq_s.shape[3], wi_s.shape[3]

    @pl.when(sc[0] == 1)
    def _():
        m = sc[1]
        place = pl.ds(pl.multiple_of(m * rows, rows), rows)
        copies, loads = Copies(sems), Copies(wsems)

        @pl.when(sc[2] == 1)
        def _():
            pltpu.make_async_copy(cot.at[place], in_s, sems.at[50]).start()

        @pl.when(sc[2] == 0)
        def _():
            pltpu.make_async_copy(hop_in, in_s, sems.at[50]).start()

        got = {}
        for j in (1, 0):
            s = "ab"[j]
            for n, (name, buf) in enumerate((("q", wq_s), ("o", wo_s), ("i", wi_s), ("h", wh_s))[::-1]):
                for k in range(2):
                    got[name, k, j] = loads.start(weights[2 * (3 - n) + k].at[j], buf.at[k, j])
            got["g", j] = copies.start(rd["g" + s].at[place], g_s.at[j])
            got["o", j] = copies.start(rd["o" + s].at[place], o_s.at[j])
            got["q", j] = copies.start(rd["q" + s].at[place], q_s.at[j])
            got["l", j] = copies.start(rd["l" + s].at[:, :, place], l_s.at[j])
            if j == 1:
                early = [copies.start(rd["kd"], kd_s), copies.start(rd["vd"], vd_s), copies.start(rd["kt"], kt_s)]
                got["x", 1] = copies.start(rd["x1"].at[place], x1_s)
            else:
                got["x", 0] = copies.start(rd["x0"].at[place], x0_s)

        @pl.when(m == chunks - 1)
        def _():
            dkw_s[...] = jnp.zeros_like(dkw_s)
            dvw_s[...] = jnp.zeros_like(dvw_s)
            acc_s[...] = jnp.zeros_like(acc_s)

        @pl.when(m < chunks - 1)
        def _():
            for i, (source, target) in enumerate(((st["dkw"], dkw_s), (st["dvw"], dvw_s), (st["acc"], acc_s))):
                pltpu.make_async_copy(source, target, sems.at[47 + i]).start()
            for i, (source, target) in enumerate(((st["dkw"], dkw_s), (st["dvw"], dvw_s), (st["acc"], acc_s))):
                pltpu.make_async_copy(source, target, sems.at[47 + i]).wait()

        pltpu.make_async_copy(hop_in, in_s, sems.at[50]).wait()
        dy_s[...] = in_s[...].astype(F32) * scale[0]
        tables = (cos[place, :], -ahead[place, :], -behind[place, :])
        for j in (1, 0):
            base = 10 * j
            grad = dy_s[...]
            db_s[j] = grad.astype(BF16)
            acc_s[base : base + 1, :] += jnp.sum(grad, axis=0, keepdims=True)
            copies.later(db_s.at[j], st["db" + "ab"[j]].at[place])
            got["g", j].wait()
            for k in range(2):
                got["h", k, j].wait()
                for n in range(hid // TILE):
                    slope_col = k * hid + n * TILE
                    back = dot_nt(db_s[j], wh_s[k, j, n * TILE : (n + 1) * TILE, :])
                    back = (back * g_s[j, :, slope_col : slope_col + TILE].astype(F32)).astype(BF16)
                    du_s[j, :, slope_col : slope_col + TILE] = back
                    row, col = base + 6 + slope_col // width, slope_col % width
                    acc_s[row : row + 1, col : col + TILE] += jnp.sum(back.astype(F32), axis=0, keepdims=True)
            copies.later(du_s.at[j], st["du" + "ab"[j]].at[place])
            for k in range(2):
                got["i", k, j].wait()
                part = dot_nt(du_s[j, :, k * hid : (k + 1) * hid], wi_s[k, j])
                dh2_s[...] = part if k == 0 else dh2_s[...] + part
            for k in range(2):
                got["o", k, j].wait()
                do_s[:, k * half : (k + 1) * half] = dot_nt(db_s[j], wo_s[k, j]).astype(BF16)
            for name in ("o", "q", "l"):
                got[name, j].wait()
            if j == 1:
                for copy in early:
                    copy.wait()

            def attend(before):
                def pair(i, _):
                    cols = pl.ds(pl.multiple_of(i * LANES, LANES), LANES)
                    out_grad = do_s[:, cols]
                    inner = jnp.transpose(out_grad.astype(F32) * o_s[j, :, cols].astype(F32))
                    queries, grads = split_pair(q_s[j, :, cols]), split_pair(out_grad)
                    back = []
                    spans = ((before, before + rows, True),) + (((0, before, False),) if before else ())
                    sums = {}
                    for n in range(2):
                        lse = l_s[j, i, n : n + 1, :]
                        mean = jnp.sum(inner[n * HD : (n + 1) * HD], axis=0, keepdims=True)
                        total = None
                        for low, high, masked in spans:
                            scores = dot_nt(kd_s[low:high, :], queries[n])
                            probs = jnp.exp(scores - lse)
                            if masked:
                                probs = jnp.where(visible(rows), probs, 0.0)
                            prob_grad = dot_nt(vd_s[low:high, :], grads[n])
                            score_grad = (probs * (prob_grad - mean)).astype(BF16)
                            key_part = dot(score_grad, queries[n])
                            value_part = dot(probs.astype(BF16), grads[n])
                            query_part = dot(kt_s[:, low:high], score_grad)
                            total = query_part if total is None else total + query_part
                            if n == 0:
                                sums[low] = (key_part, value_part)
                            else:
                                dkw_s[low:high, :] += sums[low][0] + key_part
                                dvw_s[low:high, :] += sums[low][1] + value_part
                        back.append(total * HD**-0.5)
                    turned = turn(jnp.transpose(jnp.concatenate(back, axis=0)), *tables)
                    dql_s[j, :, cols] = turned.astype(BF16)
                    return 0

                lax.fori_loop(0, width // LANES, pair, 0)

            for c in range(chunks):
                pl.when(m == c)(functools.partial(attend, c * rows))
            copies.later(dql_s.at[j], st["dq" + "ab"[j]].at[place])
            acc_s[base + 5 : base + 6, :] += jnp.sum(dql_s[j].astype(F32), axis=0, keepdims=True)
            for k in range(2):
                got["q", k, j].wait()
                part = dot_nt(dql_s[j, :, k * half : (k + 1) * half], wq_s[k, j])
                dh1_s[...] = part if k == 0 else dh1_s[...] + part
            if j == 0:
                key_grad, value_grad = dkw_s[place, :], dvw_s[place, :]
                key_grad = turn(key_grad + pltpu.roll(key_grad, HD, axis=1), *tables)
                value_grad = value_grad + pltpu.roll(value_grad, HD, axis=1)
                low = lax.broadcasted_iota(jnp.int32, key_grad.shape, 1) < HD
                both = jnp.where(low, key_grad, value_grad).astype(BF16)
                dkv_s[...] = both
                copies.later(dkv_s, st["dkv"].at[place])
                acc_s[20:21, :LANES] += jnp.sum(both.astype(F32), axis=0, keepdims=True)
                dh1_s[...] += dot_nt(both, wkv[...])
            got["x", j].wait()
            gain1, gain2 = common[2 * j : 2 * j + 1, :], common[2 * j + 1 : 2 * j + 2, :]
            totals = None
            for r in range(0, rows, 64):
                span = slice(r, r + 64)
                hat, spread = normalized((x1_s if j else x0_s)[span, :].astype(F32))
                first, second = dh1_s[span, :], dh2_s[span, :]
                parts = [jnp.sum(v, axis=0, keepdims=True) for v in (first * hat, first, second * hat, second)]
                totals = parts if totals is None else [a + b for a, b in zip(totals, parts)]
                inside = first * gain1 + second * gain2
                shift = jnp.mean(inside, axis=-1, keepdims=True)
                tilt = jnp.mean(inside * hat, axis=-1, keepdims=True)
                dy_s[span, :] += spread * (inside - shift - hat * tilt)
            for i, v in enumerate(totals):
                acc_s[base + 1 + i : base + 2 + i, :] += v
        in_s[...] = dy_s[...].astype(BF16)
        copies.later(in_s, st["gin"].at[place])
        copies.later(in_s, hop_out)
        copies.later(dkw_s, st["dkw"])
        copies.later(dvw_s, st["dvw"])
        copies.later(acc_s, st["acc"])
        copies.finish()


def bwd_call(rows, chunks, state, sc, scale, hop, cot, params, weights, fwd):
    common, cos, ahead, behind, wkv = params
    length, width = cot.shape
    half, hid = weights[0].shape[2], weights[4].shape[2]
    hidden = 2 * hid
    _, shapes = state_shapes(length, width, hidden)
    fresh = state is None
    n = len(BWD_STATE)
    saved = dict(zip(FWD_STATE, fwd))
    scratch = [
        pltpu.VMEM((rows, width), BF16),
        pltpu.VMEM((rows, width), F32),
        pltpu.VMEM((rows, width), BF16),
        pltpu.VMEM((rows, width), F32),
        pltpu.VMEM((2, rows, width), BF16),
        pltpu.VMEM((2, rows, width), BF16),
        pltpu.VMEM((2, rows, hidden), BF16),
        pltpu.VMEM((2, width // LANES, 8, rows), F32),
        pltpu.VMEM((length, LANES), BF16),
        pltpu.VMEM((length, LANES), BF16),
        pltpu.VMEM((HD, length), BF16),
        pltpu.VMEM((2, rows, width), BF16),
        pltpu.VMEM((rows, width), BF16),
        pltpu.VMEM((2, rows, hidden), BF16),
        pltpu.VMEM((2, rows, width), BF16),
        pltpu.VMEM((rows, LANES), BF16),
        pltpu.VMEM((length, LANES), F32),
        pltpu.VMEM((length, LANES), F32),
        pltpu.VMEM((rows, width), F32),
        pltpu.VMEM((rows, width), F32),
        pltpu.VMEM((24, width), F32),
        pltpu.VMEM((2, 2, width, half), BF16),
        pltpu.VMEM((2, 2, half, width), BF16),
        pltpu.VMEM((2, 2, width, hid), BF16),
        pltpu.VMEM((2, 2, hid, width), BF16),
        pltpu.SemaphoreType.DMA((51,)),
        pltpu.SemaphoreType.DMA((16,)),
    ]
    first_state = 17 + len(READ)
    outs = pl.pallas_call(
        functools.partial(bwd_kernel, rows, chunks, fresh),
        out_shape=[make_struct(shapes[k]) for k in BWD_STATE] + [jax.ShapeDtypeStruct((rows, width), BF16)],
        in_specs=[SMEM, SMEM, ANY, ANY] + [VMEM] * 5 + [ANY] * (8 + len(READ) + (0 if fresh else n)),
        out_specs=[ANY] * (n + 1),
        scratch_shapes=scratch,
        input_output_aliases={} if fresh else {first_state + i: i for i in range(n)},
        compiler_params=pltpu.CompilerParams(vmem_limit_bytes=VMEM_LIMIT),
        name="section_backward",
    )(sc, scale, hop, cot, common, cos, ahead, behind, wkv, *weights, *[saved[k] for k in READ], *([] if fresh else state))
    return outs[:n], outs[n]


def turn_tables(length):
    column = jnp.arange(LANES) % HD
    half = ROT // 2
    freq = jnp.power(10000.0, -2.0 * (column % half).astype(F32) / ROT)
    angle = jnp.arange(length).astype(F32)[:, None] * freq[None, :]
    cosines = jnp.where((column < ROT)[None, :], jnp.cos(angle), 1.0)
    sines = jnp.sin(angle)
    ahead = jnp.where((column < half)[None, :], -sines, 0.0)
    behind = jnp.where(((column >= half) & (column < ROT))[None, :], sines, 0.0)
    return cosines, ahead, behind


def stage_place(stage):
    across = stage // 2
    return across, (stage % 2 if across == 0 else 1 - stage % 2)


def device(across, core, tensor):
    return (2 * across + core) * 2 + tensor


PLANE = ("section", "tensor")
SWAP = [(0, 1), (1, 0), (2, 3), (3, 2)]


def plane_routes():
    fetch, ahead = [], []
    for stage in range(4):
        across, tensor = stage_place(stage)
        for core in range(2):
            fetch.append((device(across, stage % 2, core), device(across, core, tensor)))
            if stage < 3:
                after, turned = stage_place(stage + 1)
                ahead.append((device(across, core, tensor), device(after, core, turned)))
    return fetch, [(b, a) for a, b in fetch], ahead, [(b, a) for a, b in ahead]


FETCH, DELIVER, AHEAD, BEHIND = plane_routes()


def other_core(value):
    return lax.ppermute(value, "section", SWAP)


def added(left, right):
    return (left.astype(F32) + right.astype(F32)).astype(BF16)


def after(value, *others):
    return lax.optimization_barrier((value, *others))[0]


def summed_over_line(pieces, make):
    position = lax.axis_index("dp")
    at_end = (position == 0) | (position == 3)
    first, second, third, done = [], [], [], []
    for r in range(len(pieces) + 3):
        if r < len(pieces):
            term = make(pieces[r])
            ties = [chain[-1] for chain in (first[:-1], second[:-1], third[:-1]) if chain]
            if ties:
                term = after(term, *ties)
            first.append(added(term, lax.ppermute(term, "dp", [(0, 1), (3, 2)])))
        if 0 <= r - 1 < len(pieces):
            part = first[r - 1]
            second.append(added(part, lax.ppermute(part, "dp", [(1, 2), (2, 1)])))
        if 0 <= r - 2 < len(pieces):
            whole = second[r - 2]
            third.append(jnp.where(at_end, lax.ppermute(whole, "dp", [(1, 0), (2, 3)]), whole))
        if 0 <= r - 3 < len(pieces):
            done.append(lax.ppermute(third[r - 3], PLANE, DELIVER))
    return done


def local(
    inputs,
    cotangent,
    subset_ids,
    subset_weight,
    ln_gain,
    ln_bias,
    w_query,
    b_query,
    w_kv,
    b_kv,
    w_out,
    out_bias,
    w_in,
    b_in,
    w_hid_out,
):
    section, tensor = lax.axis_index("section"), lax.axis_index("tensor")
    across, core = section // 2, section % 2
    stage = 2 * across + jnp.where(across == 0, tensor, 1 - tensor)
    micro, part, width = inputs.shape
    length = part * lax.axis_size(PLANE)
    half, hid = w_query.shape[3], w_in.shape[3]
    chunks = length // ROWS
    ticks = chunks + 3

    mine = [lax.ppermute(w[0], PLANE, FETCH) for w in (w_query, w_out, w_in, w_hid_out)]
    small = jnp.concatenate([v.reshape(-1) for v in (ln_gain, ln_bias, out_bias, b_kv, b_query, b_in)]).reshape(-1, LANES)
    small = lax.ppermute(small, PLANE, FETCH)
    own_kv = lax.ppermute(w_kv[0], PLANE, FETCH)
    weights = [w for pair in zip(mine, [other_core(w) for w in mine]) for w in pair]
    flat, flat_other = small.reshape(-1), other_core(small).reshape(-1)
    edge = 12 * width + LANES
    bkv = flat[12 * width : edge]
    bkv = jnp.concatenate([bkv[:HD], bkv[:HD], bkv[HD:], bkv[HD:]])
    common = jnp.concatenate([flat[: 12 * width].reshape(12, width), jnp.pad(bkv, (0, width - TILE))[None], jnp.zeros((3, width), F32)])
    bq = [f[edge : edge + 2 * half].reshape(2, half) for f in (flat, flat_other)]
    bi = [f[edge + 2 * half :].reshape(2, hid) for f in (flat, flat_other)]
    wide_kv = jnp.concatenate([own_kv[:, :HD], own_kv[:, :HD], own_kv[:, HD:], own_kv[:, HD:]], axis=1)

    whole_in = lax.all_gather(inputs, PLANE, axis=1, tiled=True)
    whole_cot = lax.all_gather(cotangent, PLANE, axis=1, tiled=True)
    my_in = lax.dynamic_index_in_dim(whole_in, core, 0, keepdims=False)
    my_cot = lax.dynamic_index_in_dim(whole_cot, core, 0, keepdims=False)
    my_id = lax.dynamic_index_in_dim(subset_ids, core, 0, keepdims=False)
    matches = my_id == jnp.arange(subset_weight.shape[0], dtype=jnp.int32)
    weight = jnp.sum(jnp.where(matches, subset_weight, 0.0))
    is_first, is_last = stage == 0, stage == 3
    scale = jnp.where(is_last, weight, 1.0).reshape(1)

    tables = turn_tables(length)
    forward_params = (common, *bq, *bi, *tables, wide_kv)
    hop = jnp.zeros((ROWS, width), BF16)
    saved = None
    for tick in range(ticks):
        number = tick - stage
        valid = (number >= 0) & (number < chunks)
        sc = jnp.stack([valid.astype(jnp.int32), jnp.clip(number, 0, chunks - 1), is_first.astype(jnp.int32)])
        saved, hop = fwd_call(ROWS, chunks, saved, sc, hop, my_in, forward_params, weights)
        if tick < ticks - 1:
            hop = lax.ppermute(hop, PLANE, AHEAD)
    kept = dict(zip(FWD_STATE, saved))

    def spread(mine_only, here):
        rows = jnp.where(here, mine_only, jnp.zeros_like(mine_only))[None]
        canvas = jnp.where((jnp.arange(micro) == core)[:, None, None], rows, jnp.zeros_like(rows))
        return lax.psum_scatter(canvas, PLANE, scatter_dimension=1, tiled=True)

    final = spread(kept["y"], is_last)

    backward_params = (common, *tables, own_kv)
    back = None
    for tick in range(ticks):
        number = chunks - 1 - tick + (3 - stage)
        valid = (number >= 0) & (number < chunks)
        sc = jnp.stack([valid.astype(jnp.int32), jnp.clip(number, 0, chunks - 1), is_last.astype(jnp.int32)])
        back, hop = bwd_call(ROWS, chunks, back, sc, scale, hop, my_cot, backward_params, weights, saved)
        if tick < ticks - 1:
            hop = lax.ppermute(hop, PLANE, BEHIND)
    got = dict(zip(BWD_STATE, back))
    input_grad = spread(got["gin"], is_first).astype(F32)

    def product(left, left_cols, right, right_cols):
        return dot(left[:, left_cols], right[:, right_cols], ((0,), (0,))).astype(BF16)

    everything = slice(None)

    def term(piece):
        name, slot, start, size = piece
        s = "ab"[slot]
        both = []
        for k in range(2):
            if name == "h":
                at = k * hid + start
                both.append(product(kept["a" + s], slice(at, at + size), got["db" + s], everything))
            elif name == "i":
                at = k * hid + start
                both.append(product(kept["h2" + s], everything, got["du" + s], slice(at, at + size)))
            elif name == "o":
                at = k * half + start
                both.append(product(kept["o" + s], slice(at, at + size), got["db" + s], everything))
            elif name == "q":
                at = k * half + start
                both.append(product(kept["h1" + s], everything, got["dq" + s], slice(at, at + size)))
        if name == "kv":
            one = product(kept["h1a"], everything, got["dkv"], everything)
            return added(one, other_core(one))
        return added(both[0], other_core(both[1]))

    pieces = []
    for slot in (1, 0):
        pieces.append(("o", slot, 0, half))
        pieces += [("h", slot, at, hid // 2) for at in (0, hid // 2)]
        pieces += [("i", slot, at, hid // 2) for at in (0, hid // 2)]
        pieces.append(("q", slot, 0, half))
    pieces.append(("kv", 0, 0, 0))
    if lax.axis_size("dp") == 4:
        done = summed_over_line(pieces, term)
    else:
        done = [lax.ppermute(lax.psum(term(piece), "dp"), PLANE, DELIVER) for piece in pieces]
    done = dict(zip(pieces, done))

    def joined(name, size, axis):
        slots = []
        for slot in range(2):
            parts = [done[p].astype(F32) for p in pieces if p[:2] == (name, slot)]
            slots.append(jnp.concatenate(parts, axis=axis))
        return jnp.stack(slots)[None]

    acc = got["acc"]
    rows = []
    for slot in range(2):
        base = 10 * slot
        query, first, second = acc[base + 5], acc[base + 6 : base + 8], acc[base + 8 : base + 10]
        query = jnp.where(core == 0, query, jnp.roll(query, half))
        rows += [acc[base : base + 5], query[None]]
        rows += [jnp.where(core == 0, first, second), jnp.where(core == 0, second, first)]
    rows.append(acc[20:])
    acc = jnp.concatenate(rows)
    acc = acc + other_core(acc)
    acc = lax.ppermute(lax.psum(acc, "dp"), PLANE, DELIVER)

    def per_slot(pick):
        return jnp.stack([pick(0), pick(10)])[None]

    gain_grad = per_slot(lambda b: jnp.stack([acc[b + 1], acc[b + 3]]))
    bias_grad = per_slot(lambda b: jnp.stack([acc[b + 2], acc[b + 4]]))
    out_bias_grad = per_slot(lambda b: jnp.stack([acc[b], acc[b]]))
    bq_grad = per_slot(lambda b: lax.dynamic_slice_in_dim(acc[b + 5], tensor * half, half))
    bi_grad = per_slot(lambda b: lax.dynamic_slice_in_dim(acc[b + 6 : b + 10].reshape(-1), tensor * hid, hid))
    return (
        final,
        input_grad,
        gain_grad,
        bias_grad,
        joined("q", half, 1),
        bq_grad,
        done["kv", 0, 0, 0].astype(F32)[None],
        acc[20, : 2 * HD][None],
        joined("o", half, 0),
        out_bias_grad,
        joined("i", hid, 1),
        bi_grad,
        joined("h", hid, 0),
    )


def solution(mesh):
    assert mesh.shape["section"] == 4 and mesh.shape["tensor"] == 2
    rows = P("dp", PLANE, None)
    weights = (
        P("section", None, None, None),
        P("section", None, None, None),
        P("section", None, None, "tensor"),
        P("section", None, "tensor"),
        P("section", None, None),
        P("section", None),
        P("section", None, "tensor", None),
        P("section", None, None, None),
        P("section", None, None, "tensor"),
        P("section", None, "tensor"),
        P("section", None, "tensor", None),
    )
    return jax.shard_map(
        local,
        mesh=mesh,
        in_specs=(rows, rows, P("dp"), P(), *weights),
        out_specs=(rows, rows, *weights),
        check_vma=False,
    )
```

```python
import functools
import jax
import jax.numpy as jnp
from jax import lax
from jax.experimental import pallas as pl
from jax.experimental.pallas import tpu as pltpu
from jax.sharding import PartitionSpec as P

HD = 64
ROT = 16
EPS = 1e-05
LANES = 128
ROWS = 256
NORM_ROWS = 64
SPAN = 512
VMEM_LIMIT = 60 * 2**20
ANY = pl.BlockSpec(memory_space=pl.ANY)
SMEM = pl.BlockSpec(memory_space=pltpu.SMEM)
VMEM = pl.BlockSpec(memory_space=pltpu.VMEM)
BF16, F32 = jnp.bfloat16, jnp.float32


def dot(left, right, dims=((1,), (0,))):
    return lax.dot_general(left, right, (dims, ((), ())), preferred_element_type=F32)


def dot_nt(left, right):
    return dot(left, right, ((1,), (1,)))


def turn(values, cosines, ahead, behind):
    return (
        values * cosines
        + pltpu.roll(values, LANES - ROT // 2, axis=1) * ahead
        + pltpu.roll(values, ROT // 2, axis=1) * behind
    )


def normalized(rows):
    centred = rows - jnp.mean(rows, axis=-1, keepdims=True)
    scale = lax.rsqrt(jnp.mean(centred * centred, axis=-1, keepdims=True) + EPS)
    return centred * scale, scale


def hidden_from(span, rows, m):
    key = lax.broadcasted_iota(jnp.int32, (SPAN, 2 * rows), 0)
    query = lax.broadcasted_iota(jnp.int32, (SPAN, 2 * rows), 1) & (rows - 1)
    return key > query + (m * rows - span * SPAN)


def side_by_side(pair):
    return jnp.concatenate([pair[:HD], pair[HD:]], axis=1)


def staged(total, stages):
    def turns(t):
        for half in range(2):
            for k, stage in enumerate(stages):
                u = 2 * t + half - k
                stage(jnp.clip(u, 0, total - 1), (half - k) % 2, u >= 0)

    steps((total + len(stages)) // 2, turns)


def fold(values):
    return jnp.sum(values.reshape(values.shape[0] // 8, 8, values.shape[1]), axis=0)


def steps(size, body):
    def step(i, _):
        body(i)
        return 0

    lax.fori_loop(0, size, step, 0)


def block_of(i, size):
    return pl.ds(pl.multiple_of(i * size, size), size)


FWD_STATE = ("x", "h1", "h2", "q", "qt", "o", "ot", "a", "g", "l", "kd", "vd", "kt", "vt", "y")
BWD_STATE = ("db", "du", "dq", "dkv", "dkw", "acc", "accu", "gin")
READ = ("x", "q", "qt", "ot", "g", "l", "kd", "vd", "kt")
N_W = 8


def state_shapes(length, width, hidden):
    pairs, tiles = width // LANES, hidden // width
    row, ff, one = ((2, length, width), BF16), ((2, length, hidden), BF16), ((length, width), BF16)
    full, chunks = ((2, length, width), F32), length // ROWS
    lse, turned = ((2, chunks, pairs, 1, 2 * ROWS), F32), (2, chunks, pairs, HD, 2 * ROWS)
    wide, tall, total = ((length, LANES), BF16), ((HD, length), BF16), ((length, LANES), F32)
    fwd = dict(x=full, h1=row, h2=row, q=row, qt=(turned, BF16), o=row, ot=(turned, F32), a=ff, g=ff, l=lse, kd=wide, vd=wide, kt=tall, vt=tall, y=one)
    bwd = dict(db=row, du=ff, dq=row, dkv=wide, dkw=total, acc=((2, 8, 8, width), F32), accu=((2, tiles, 8, width), F32), gin=one)
    return fwd, bwd


def weight_copies(stored, weights, wsems, slot):
    copies = {}
    for n, name in enumerate("qoih"):
        copies[name] = [pltpu.make_async_copy(stored[2 * n + k].at[slot], weights[2 * n + k].at[slot], wsems.at[slot, 2 * n + k]) for k in range(2)]
    return copies


def weight_scratch(weights):
    return [pltpu.VMEM(w.shape, BF16) for w in weights]


def make_struct(item):
    return jax.ShapeDtypeStruct(*item)


def fwd_kernel(rows, fresh, *refs):
    n_state = len(FWD_STATE)
    sc, hop_in, seq_in, small, bi, cos, ahead, behind, wkv = refs[:9]
    stored = refs[9 : 9 + N_W]
    at = 9 + N_W + (0 if fresh else n_state)
    st = dict(zip(FWD_STATE, refs[at : at + n_state]))
    hop_out = refs[at + n_state]
    (x_s, xf_s, h1_s, h2_s, q_s, qt_s, o_s, ot_s, a_s, g_s, l_s, kd_s, vd_s, kt_s, vt_s, vtc_s, s0_s, s1_s, e0_s, e1_s, top_s, sum_s, part_s, *weights, sems, once, wsems) = refs[at + n_state + 1 :]
    wq, wo, wi, wh = (weights[2 * i : 2 * i + 2] for i in range(4))
    width = xf_s.shape[2]
    half, hid = wq[0].shape[2], wi[0].shape[2]
    pairs, tiles, length = width // LANES, hid // width, kd_s.shape[0]

    @pl.when(sc[0] == 1)
    def _():
        m = sc[1]
        place = block_of(m, rows)

        @pl.when(sc[2] == 1)
        def _():
            pltpu.make_async_copy(seq_in.at[place], x_s, once.at[0]).start()

        @pl.when(sc[2] == 0)
        def _():
            pltpu.make_async_copy(hop_in, x_s, once.at[0]).start()

        for j in range(2):
            copies = weight_copies(stored, weights, wsems, j ^ sc[3])
            for name in "qioh":
                for copy in copies[name]:
                    copy.start()
        kd_in = pltpu.make_async_copy(st["kd"], kd_s, once.at[1])
        vt_in = pltpu.make_async_copy(st["vt"], vt_s, once.at[2])
        kd_in.start()
        vt_in.start()
        pltpu.make_async_copy(hop_in, x_s, once.at[0]).wait()
        xf_s[0] = x_s[...].astype(F32)
        tables = (cos[place, :], ahead[place, :], behind[place, :])

        def saves(j):
            pairs_of = (("x", xf_s), ("h1", h1_s), ("h2", h2_s), ("q", q_s), ("o", o_s), ("a", a_s), ("g", g_s))
            out = {n: pltpu.make_async_copy(b.at[j], st[n].at[j, place], sems.at[j, i]) for i, (n, b) in enumerate(pairs_of)}
            for i, (n, b) in enumerate((("l", l_s), ("qt", qt_s), ("ot", ot_s))):
                out[n] = pltpu.make_async_copy(b.at[j], st[n].at[j, m], sems.at[j, 7 + i])
            return out

        kv_saves = (
            pltpu.make_async_copy(kd_s.at[place], st["kd"].at[place], once.at[3]),
            pltpu.make_async_copy(vd_s, st["vd"].at[place], once.at[4]),
            pltpu.make_async_copy(kt_s, st["kt"].at[:, place], once.at[5]),
            pltpu.make_async_copy(vtc_s, st["vt"].at[:, place], once.at[6]),
        )

        def layer(j):
            w = j ^ sc[3]
            loads = weight_copies(stored, weights, wsems, w)
            save = saves(j)
            save["x"].start()

            def norm(r):
                span = block_of(r, NORM_ROWS)
                hat, _ = normalized(xf_s[j, span, :])
                h1_s[j, span, :] = (hat * small[j, 0:1, :] + small[j, 2:3, :]).astype(BF16)
                h2_s[j, span, :] = (hat * small[j, 1:2, :] + small[j, 3:4, :]).astype(BF16)

            steps(rows // NORM_ROWS, norm)
            save["h1"].start()
            save["h2"].start()

            @pl.when(j == 0)
            def _():
                kv = dot(h1_s[j], wkv[...]) + small[j, 7:8, : 2 * LANES]
                keys, values = turn(kv[:, :LANES], *tables), kv[:, LANES:]
                kd_in.wait()
                vt_in.wait()
                kd_s[place, :] = keys.astype(BF16)
                vd_s[...] = values.astype(BF16)
                kt_s[...] = jnp.transpose(keys)[:HD].astype(BF16)
                vtc_s[...] = jnp.transpose(values)[:HD].astype(BF16)
                vt_s[:, place] = vtc_s[...]
                for c in range(1, length // rows):

                    @pl.when(m < c)
                    def _():
                        vt_s[:, c * rows : (c + 1) * rows] = jnp.zeros((HD, rows), BF16)

                for copy in kv_saves:
                    copy.start()

            for k in range(2):
                loads["q"][k].wait()
                query = dot(h1_s[j], wq[k][w]) + small[j, 6:7, k * half : (k + 1) * half]
                for b in range(half // LANES):
                    block = turn(query[:, b * LANES : (b + 1) * LANES], *tables) * HD**-0.5
                    col = k * half + b * LANES
                    q_s[j, :, col : col + LANES] = block.astype(BF16)
                    qt_s[j, col // LANES] = side_by_side(jnp.transpose(block)).astype(BF16)
            save["q"].start()
            save["qt"].start()

            many = m * rows >= SPAN

            def unit(u):
                return (u >= pairs).astype(jnp.int32), jnp.where(u >= pairs, u - pairs, u)

            def scores(u, slot, live):
                span, i = unit(u)
                (s0_s, s1_s)[slot][...] = dot(kd_s[block_of(span, SPAN), :HD], qt_s[j, i])

            def soften(u, slot, live):
                span, i = unit(u)
                score = jnp.where(hidden_from(span, rows, m), -1e30, (s0_s, s1_s)[slot][...])
                top = jnp.max(score, axis=0, keepdims=True)
                expo = jnp.exp(score - top)
                top_s[u] = top
                sum_s[u] = jnp.sum(expo, axis=0, keepdims=True)
                (e0_s, e1_s)[slot][...] = expo.astype(BF16)

            def weigh(u, slot, live):
                span, i = unit(u)
                part_s[u] = dot(vt_s[:, block_of(span, SPAN)], (e0_s, e1_s)[slot][...])

            staged(jnp.where(many, 2 * pairs, pairs), (scores, soften, weigh))

            def gather(i):
                first, second = top_s[i], jnp.where(many, top_s[pairs + i], -1e30)
                top = jnp.maximum(first, second)
                first, second = jnp.exp(first - top), jnp.exp(second - top)
                summed = first * sum_s[i] + jnp.where(many, second * sum_s[pairs + i], 0.0)
                out = first * part_s[i] + jnp.where(many, second * part_s[pairs + i], 0.0)
                out = out / summed
                l_s[j, i] = top + jnp.log(summed)
                ot_s[j, i] = out
                out = jnp.concatenate([out[:, :rows], out[:, rows:]], axis=0)
                o_s[j, :, block_of(i, LANES)] = jnp.transpose(out).astype(BF16)

            steps(pairs, gather)
            for name in ("o", "ot", "l"):
                save[name].start()

            for copy in loads["i"]:
                copy.wait()

            def hidden(t):
                for k in range(2):
                    before = dot(h2_s[j], wi[k][w, :, block_of(t, width)]) + bi[j, k * tiles + t]
                    normal = 0.5 + 0.5 * lax.erf(before * 0.5**0.5)
                    cols = pl.ds(pl.multiple_of(k * hid + t * width, width), width)
                    a_s[j, :, cols] = (before * normal).astype(BF16)
                    slope = normal + before * (jnp.exp(-0.5 * before * before) * 0.3989422804014327)
                    g_s[j, :, cols] = slope.astype(BF16)

            steps(tiles, hidden)
            save["a"].start()
            save["g"].start()
            for copy in loads["o"] + loads["h"]:
                copy.wait()
            branch = dot(a_s[j, :, :hid], wh[0][w]) + dot(a_s[j, :, hid:], wh[1][w])
            branch += dot(o_s[j, :, :half], wo[0][w]) + dot(o_s[j, :, half:], wo[1][w])
            xf_s[j + 1] = xf_s[j] + (branch + small[j, 4:5, :] + small[j, 5:6, :])

        steps(2, layer)
        x_s[...] = xf_s[2].astype(BF16)
        ends = (
            pltpu.make_async_copy(x_s, st["y"].at[place], once.at[7]),
            pltpu.make_async_copy(x_s, hop_out, once.at[8]),
        )
        for copy in ends:
            copy.start()
        for j in range(2):
            for copy in saves(j).values():
                copy.wait()
        for copy in kv_saves + ends:
            copy.wait()


def fwd_call(rows, state, sc, hop, seq, params, weights):
    small, bi, cos, ahead, behind, wkv = params
    length, width = seq.shape
    half, hid = weights[0].shape[2], weights[4].shape[2]
    hidden, pairs = 2 * hid, width // LANES
    shapes, _ = state_shapes(length, width, hidden)
    fresh = state is None
    n = len(FWD_STATE)
    scratch = [
        pltpu.VMEM((rows, width), BF16),
        pltpu.VMEM((3, rows, width), F32),
        pltpu.VMEM((2, rows, width), BF16),
        pltpu.VMEM((2, rows, width), BF16),
        pltpu.VMEM((2, rows, width), BF16),
        pltpu.VMEM((2, pairs, HD, 2 * rows), BF16),
        pltpu.VMEM((2, rows, width), BF16),
        pltpu.VMEM((2, pairs, HD, 2 * rows), F32),
        pltpu.VMEM((2, rows, hidden), BF16),
        pltpu.VMEM((2, rows, hidden), BF16),
        pltpu.VMEM((2, pairs, 1, 2 * rows), F32),
        pltpu.VMEM((length, LANES), BF16),
        pltpu.VMEM((rows, LANES), BF16),
        pltpu.VMEM((HD, rows), BF16),
        pltpu.VMEM((HD, length), BF16),
        pltpu.VMEM((HD, rows), BF16),
        pltpu.VMEM((SPAN, 2 * rows), F32),
        pltpu.VMEM((SPAN, 2 * rows), F32),
        pltpu.VMEM((SPAN, 2 * rows), BF16),
        pltpu.VMEM((SPAN, 2 * rows), BF16),
        pltpu.VMEM((2 * pairs, 1, 2 * rows), F32),
        pltpu.VMEM((2 * pairs, 1, 2 * rows), F32),
        pltpu.VMEM((2 * pairs, HD, 2 * rows), F32),
        *weight_scratch(weights),
        pltpu.SemaphoreType.DMA((2, 10)),
        pltpu.SemaphoreType.DMA((9,)),
        pltpu.SemaphoreType.DMA((2, N_W)),
    ]
    outs = pl.pallas_call(
        functools.partial(fwd_kernel, rows, fresh),
        out_shape=[make_struct(shapes[k]) for k in FWD_STATE] + [jax.ShapeDtypeStruct((rows, width), BF16)],
        in_specs=[SMEM, ANY, ANY] + [VMEM] * 6 + [ANY] * (N_W + (0 if fresh else n)),
        out_specs=[ANY] * (n + 1),
        scratch_shapes=scratch,
        input_output_aliases={} if fresh else {9 + N_W + i: i for i in range(n)},
        compiler_params=pltpu.CompilerParams(vmem_limit_bytes=VMEM_LIMIT),
        name="section_forward",
    )(sc, hop, seq, small, bi, cos, ahead, behind, wkv, *weights, *([] if fresh else state))
    return outs[:n], outs[n]


def bwd_kernel(rows, chunks, fresh, *refs):
    n_read, n_state = len(READ), len(BWD_STATE)
    sc, scale, hop_in, cot, small, cos, ahead, behind, wkv = refs[:9]
    stored = refs[9 : 9 + N_W]
    at = 9 + N_W
    rd = dict(zip(READ, refs[at : at + n_read]))
    at += n_read + (0 if fresh else n_state)
    st = dict(zip(BWD_STATE, refs[at : at + n_state]))
    hop_out = refs[at + n_state]
    (in_s, dy_s, x_s, q_s, qt_s, ot_s, g_s, l_s, kd_s, vd_s, kt_s, db_s, do_s, du_s, dq_s, dqt_s, dkv_s, dkw_s, dh1_s, dh2_s, acc_s, accu_s, two_s, dot_s, d_s, s0_s, s1_s, dp0_s, dp1_s, both0_s, both1_s, *weights, sems, outs, once, wsems) = refs[at + n_state + 1 :]
    wq, wo, wi, wh = (weights[2 * i : 2 * i + 2] for i in range(4))
    width = dy_s.shape[1]
    half, hid = wq[0].shape[2], wi[0].shape[2]
    pairs, tiles, length = width // LANES, hid // width, kd_s.shape[0]

    @pl.when(sc[0] == 1)
    def _():
        m = sc[1]
        place = block_of(m, rows)

        @pl.when(sc[2] == 1)
        def _():
            pltpu.make_async_copy(cot.at[place], in_s, once.at[0]).start()

        @pl.when(sc[2] == 0)
        def _():
            pltpu.make_async_copy(hop_in, in_s, once.at[0]).start()

        def gets(j):
            named = (("g", g_s), ("q", q_s), ("x", x_s))
            got = {n: pltpu.make_async_copy(rd[n].at[j, place], b.at[j], sems.at[j, i]) for i, (n, b) in enumerate(named)}
            for i, (n, b) in enumerate((("l", l_s), ("qt", qt_s), ("ot", ot_s))):
                got[n] = pltpu.make_async_copy(rd[n].at[j, m], b.at[j], sems.at[j, 3 + i])
            return got

        shared = [pltpu.make_async_copy(rd[n], b, once.at[1 + i]) for i, (n, b) in enumerate((("kd", kd_s), ("vd", vd_s), ("kt", kt_s)))]
        for j in (1, 0):
            copies = weight_copies(stored, weights, wsems, j ^ sc[3])
            for copy in copies["o"] + list(gets(j).values()):
                copy.start()
            for copy in shared if j == 1 else ():
                copy.start()
            for copy in copies["q"] + copies["h"] + copies["i"]:
                copy.start()
        running = (("dkw", dkw_s), ("acc", acc_s), ("accu", accu_s))

        @pl.when(m == chunks - 1)
        def _():
            for _, buf in running:
                buf[...] = jnp.zeros_like(buf)

        @pl.when(m < chunks - 1)
        def _():
            copies = [pltpu.make_async_copy(st[n], b, once.at[4 + i]) for i, (n, b) in enumerate(running)]
            for copy in copies:
                copy.start()
            for copy in copies:
                copy.wait()

        pltpu.make_async_copy(hop_in, in_s, once.at[0]).wait()
        dy_s[...] = in_s[...].astype(F32) * scale[0]
        tables = (cos[place, :], -ahead[place, :], -behind[place, :])

        def saves(j):
            named = (("db", db_s), ("du", du_s), ("dq", dq_s))
            return {n: pltpu.make_async_copy(b.at[j], st[n].at[j, place], outs.at[j, i]) for i, (n, b) in enumerate(named)}

        kv_save = pltpu.make_async_copy(dkv_s, st["dkv"].at[place], once.at[8])

        def layer(step):
            j = 1 - step
            w = j ^ sc[3]
            loads = weight_copies(stored, weights, wsems, w)
            got, save = gets(j), saves(j)
            grad = dy_s[...]
            db_s[j] = grad.astype(BF16)
            acc_s[j, 0] += fold(grad)
            save["db"].start()
            for k in range(2):
                loads["o"][k].wait()
                do_s[:, k * half : (k + 1) * half] = dot_nt(db_s[j], wo[k][w]).astype(BF16)
            for name in ("ot", "q", "qt", "l"):
                got[name].wait()

            @pl.when(j == 1)
            def _():
                for copy in shared:
                    copy.wait()

            def ready(i):
                cols = block_of(i, LANES)
                out_grad = do_s[:, cols].astype(F32)
                turned = side_by_side(jnp.transpose(out_grad))
                d_s[i] = jnp.sum(turned * ot_s[j, i], axis=0, keepdims=True)
                dot_s[i] = turned.astype(BF16)
                query = q_s[j, :, cols].astype(F32)
                low = lax.broadcasted_iota(jnp.int32, query.shape, 1) < HD
                parts = (
                    jnp.where(low, query, 0.0),
                    jnp.where(low, pltpu.roll(query, HD, axis=1), 0.0),
                    jnp.where(low, 0.0, pltpu.roll(out_grad, HD, axis=1)),
                    jnp.where(low, 0.0, out_grad),
                )
                for n, part in enumerate(parts):
                    two_s[i, n * rows : (n + 1) * rows, :] = part.astype(BF16)

            steps(pairs, ready)

            def unit(u):
                return (u >= pairs).astype(jnp.int32), jnp.where(u >= pairs, u - pairs, u)

            def scores(u, slot, live):
                span, i = unit(u)
                (s0_s, s1_s)[slot][...] = dot(kd_s[block_of(span, SPAN), :HD], qt_s[j, i])
                (dp0_s, dp1_s)[slot][...] = dot(vd_s[block_of(span, SPAN), :HD], dot_s[i])

            def soften(u, slot, live):
                span, i = unit(u)
                probs = jnp.where(hidden_from(span, rows, m), 0.0, jnp.exp((s0_s, s1_s)[slot][...] - l_s[j, i]))
                both = (both0_s, both1_s)[slot]
                both[:, : 2 * rows] = (probs * ((dp0_s, dp1_s)[slot][...] - d_s[i])).astype(BF16)
                both[:, 2 * rows :] = probs.astype(BF16)

            def weigh(u, slot, live):
                span, i = unit(u)
                place = block_of(span, SPAN)
                dqt_s[u] = dot(kt_s[:, place], (both0_s, both1_s)[slot][:, : 2 * rows])
                part = dot((both0_s, both1_s)[slot][...], two_s[i])

                dkw_s[place, :] += jnp.where(live, part, 0.0)

            many = m * rows >= SPAN
            staged(jnp.where(many, 2 * pairs, pairs), (scores, soften, weigh))

            def finish(i):
                grad = dqt_s[i] + jnp.where(many, dqt_s[pairs + i], 0.0)
                grad = jnp.concatenate([grad[:, :rows], grad[:, rows:]], axis=0)
                turned = turn(jnp.transpose(grad) * HD**-0.5, *tables)
                dq_s[j, :, block_of(i, LANES)] = turned.astype(BF16)

            steps(pairs, finish)
            save["dq"].start()
            acc_s[j, 5] += fold(dq_s[j].astype(F32))
            for copy in loads["q"]:
                copy.wait()
            dh1_s[...] = dot_nt(dq_s[j, :, :half], wq[0][w]) + dot_nt(dq_s[j, :, half:], wq[1][w])

            @pl.when(j == 0)
            def _():
                both = dkw_s[place, :]
                low = lax.broadcasted_iota(jnp.int32, both.shape, 1) < HD
                both = jnp.where(low, turn(both, *tables), both).astype(BF16)
                dkv_s[...] = both
                kv_save.start()
                acc_s[j, 6, :, :LANES] += fold(both.astype(F32))
                dh1_s[...] += dot_nt(both, wkv[...])

            got["g"].wait()
            for copy in loads["h"] + loads["i"]:
                copy.wait()

            def hidden(t):
                for k in range(2):
                    cols = pl.ds(pl.multiple_of(k * hid + t * width, width), width)
                    back = dot_nt(db_s[j], wh[k][w, block_of(t, width), :])
                    back = (back * g_s[j, :, cols].astype(F32)).astype(BF16)
                    du_s[j, :, cols] = back
                    accu_s[j, k * tiles + t] += fold(back.astype(F32))

            steps(tiles, hidden)
            save["du"].start()
            dh2_s[...] = dot_nt(du_s[j, :, :hid], wi[0][w]) + dot_nt(du_s[j, :, hid:], wi[1][w])
            got["x"].wait()

            def norm(r):
                span = block_of(r, NORM_ROWS)
                hat, spread = normalized(x_s[j, span, :])
                first, second = dh1_s[span, :], dh2_s[span, :]
                for i, v in enumerate((first * hat, first, second * hat, second)):
                    acc_s[j, 1 + i] += fold(v)
                inside = first * small[j, 0:1, :] + second * small[j, 1:2, :]
                shift = jnp.mean(inside, axis=-1, keepdims=True)
                tilt = jnp.mean(inside * hat, axis=-1, keepdims=True)
                dy_s[span, :] += spread * (inside - shift - hat * tilt)

            steps(rows // NORM_ROWS, norm)

        steps(2, layer)
        in_s[...] = dy_s[...].astype(BF16)
        ends = [pltpu.make_async_copy(in_s, st["gin"].at[place], once.at[9]), pltpu.make_async_copy(in_s, hop_out, once.at[10])]
        ends += [pltpu.make_async_copy(b, st[n], once.at[4 + i]) for i, (n, b) in enumerate(running)]
        for copy in ends:
            copy.start()
        for j in range(2):
            for copy in saves(j).values():
                copy.wait()
        for copy in ends + [kv_save]:
            copy.wait()


def bwd_call(rows, chunks, state, sc, scale, hop, cot, params, weights, fwd):
    small, cos, ahead, behind, wkv = params
    length, width = cot.shape
    half, hid = weights[0].shape[2], weights[4].shape[2]
    hidden, pairs, tiles = 2 * hid, width // LANES, 2 * hid // width
    _, shapes = state_shapes(length, width, hidden)
    fresh = state is None
    n = len(BWD_STATE)
    saved = dict(zip(FWD_STATE, fwd))
    scratch = [
        pltpu.VMEM((rows, width), BF16),
        pltpu.VMEM((rows, width), F32),
        pltpu.VMEM((2, rows, width), F32),
        pltpu.VMEM((2, rows, width), BF16),
        pltpu.VMEM((2, pairs, HD, 2 * rows), BF16),
        pltpu.VMEM((2, pairs, HD, 2 * rows), F32),
        pltpu.VMEM((2, rows, hidden), BF16),
        pltpu.VMEM((2, pairs, 1, 2 * rows), F32),
        pltpu.VMEM((length, LANES), BF16),
        pltpu.VMEM((length, LANES), BF16),
        pltpu.VMEM((HD, length), BF16),
        pltpu.VMEM((2, rows, width), BF16),
        pltpu.VMEM((rows, width), BF16),
        pltpu.VMEM((2, rows, hidden), BF16),
        pltpu.VMEM((2, rows, width), BF16),
        pltpu.VMEM((2 * pairs, HD, 2 * rows), F32),
        pltpu.VMEM((rows, LANES), BF16),
        pltpu.VMEM((length, LANES), F32),
        pltpu.VMEM((rows, width), F32),
        pltpu.VMEM((rows, width), F32),
        pltpu.VMEM((2, 8, 8, width), F32),
        pltpu.VMEM((2, tiles, 8, width), F32),
        pltpu.VMEM((pairs, 4 * rows, LANES), BF16),
        pltpu.VMEM((pairs, HD, 2 * rows), BF16),
        pltpu.VMEM((pairs, 1, 2 * rows), F32),
        pltpu.VMEM((SPAN, 2 * rows), F32),
        pltpu.VMEM((SPAN, 2 * rows), F32),
        pltpu.VMEM((SPAN, 2 * rows), F32),
        pltpu.VMEM((SPAN, 2 * rows), F32),
        pltpu.VMEM((SPAN, 4 * rows), BF16),
        pltpu.VMEM((SPAN, 4 * rows), BF16),
        *weight_scratch(weights),
        pltpu.SemaphoreType.DMA((2, 6)),
        pltpu.SemaphoreType.DMA((2, 3)),
        pltpu.SemaphoreType.DMA((11,)),
        pltpu.SemaphoreType.DMA((2, N_W)),
    ]
    first_state = 9 + N_W + len(READ)
    outs = pl.pallas_call(
        functools.partial(bwd_kernel, rows, chunks, fresh),
        out_shape=[make_struct(shapes[k]) for k in BWD_STATE] + [jax.ShapeDtypeStruct((rows, width), BF16)],
        in_specs=[SMEM, SMEM, ANY, ANY] + [VMEM] * 5 + [ANY] * (N_W + len(READ) + (0 if fresh else n)),
        out_specs=[ANY] * (n + 1),
        scratch_shapes=scratch,
        input_output_aliases={} if fresh else {first_state + i: i for i in range(n)},
        compiler_params=pltpu.CompilerParams(vmem_limit_bytes=VMEM_LIMIT),
        name="section_backward",
    )(sc, scale, hop, cot, small, cos, ahead, behind, wkv, *weights, *[saved[k] for k in READ], *([] if fresh else state))
    return outs[:n], outs[n]


def turn_tables(length):
    column = jnp.arange(LANES) % HD
    half = ROT // 2
    freq = jnp.power(10000.0, -2.0 * (column % half).astype(F32) / ROT)
    angle = jnp.arange(length).astype(F32)[:, None] * freq[None, :]
    cosines = jnp.where((column < ROT)[None, :], jnp.cos(angle), 1.0)
    sines = jnp.sin(angle)
    ahead = jnp.where((column < half)[None, :], -sines, 0.0)
    behind = jnp.where(((column >= half) & (column < ROT))[None, :], sines, 0.0)
    return cosines, ahead, behind


def stage_place(stage):
    across = stage // 2
    return across, (stage % 2 if across == 0 else 1 - stage % 2)


def device(across, core, tensor):
    return (2 * across + core) * 2 + tensor


PLANE = ("section", "tensor")
SWAP = [(0, 1), (1, 0), (2, 3), (3, 2)]


def plane_routes():
    fetch, ahead = [], []
    for stage in range(4):
        across, tensor = stage_place(stage)
        for core in range(2):
            fetch.append((device(across, stage % 2, core), device(across, core, tensor)))
            if stage < 3:
                after, turned = stage_place(stage + 1)
                ahead.append((device(across, core, tensor), device(after, core, turned)))
    return fetch, [(b, a) for a, b in fetch], ahead, [(b, a) for a, b in ahead]


FETCH, DELIVER, AHEAD, BEHIND = plane_routes()


def other_core(value):
    return lax.ppermute(value, "section", SWAP)


def added(left, right):
    return (left.astype(F32) + right.astype(F32)).astype(BF16)


def after(value, *others):
    return lax.optimization_barrier((value, *others))[0]


def line_sums(pieces, make):
    position = lax.axis_index("dp")
    at_end = (position == 0) | (position == 3)
    count = len(pieces)
    own, first, second, third, done = [], [], [], [], []
    for r in range(count + 5):
        if r < count:
            ties = [chain[n] for chain, n in ((first, r - 3), (second, r - 4), (third, r - 5), (done, r - 6)) if n >= 0]
            mine, theirs = make(pieces[r], ties)
            own.append((mine, other_core(theirs)))
        if 0 <= r - 1 < count:
            term = added(*own[r - 1])
            first.append(added(term, lax.ppermute(term, "dp", [(0, 1), (3, 2)])))
        if 0 <= r - 2 < count:
            part = first[r - 2]
            second.append(added(part, lax.ppermute(part, "dp", [(1, 2), (2, 1)])))
        if 0 <= r - 3 < count:
            whole = second[r - 3]
            third.append(jnp.where(at_end, lax.ppermute(whole, "dp", [(1, 0), (2, 3)]), whole))
        if 0 <= r - 4 < count:
            done.append(lax.ppermute(third[r - 4], PLANE, DELIVER))
    return done


def local(
    inputs,
    cotangent,
    subset_ids,
    subset_weight,
    ln_gain,
    ln_bias,
    w_query,
    b_query,
    w_kv,
    b_kv,
    w_out,
    out_bias,
    w_in,
    b_in,
    w_hid_out,
):
    section, tensor = lax.axis_index("section"), lax.axis_index("tensor")
    across, core = section // 2, section % 2
    stage = 2 * across + jnp.where(across == 0, tensor, 1 - tensor)
    micro, part, width = inputs.shape
    length = part * lax.axis_size(PLANE)
    half, hid = w_query.shape[3], w_in.shape[3]
    chunks = length // ROWS
    ticks = chunks + 3

    parity = lax.axis_index("dp") % 2
    pairs = [(i, i ^ 1) for i in range(lax.axis_size("dp"))]
    halves = {}
    for name, whole in (("h", w_hid_out), ("i", w_in), ("o", w_out), ("q", w_query)):
        fetched = lax.ppermute(lax.dynamic_index_in_dim(whole[0], parity, 0, keepdims=False), PLANE, FETCH)
        swapped = lax.ppermute(fetched, "dp", pairs)
        mine = jnp.stack([fetched, swapped])
        halves[name] = [mine, other_core(mine)]
    weights = [w for name in "qoih" for w in halves[name]]
    vectors = jnp.concatenate([v.reshape(-1) for v in (ln_gain, ln_bias, out_bias, b_kv, b_query, b_in)]).reshape(-1, LANES)
    vectors = lax.ppermute(vectors, PLANE, FETCH)
    own_kv = lax.ppermute(w_kv[0], PLANE, FETCH)
    flat, flat_other = vectors.reshape(-1), other_core(vectors).reshape(-1)
    edge = 12 * width + LANES
    bkv = flat[12 * width : edge]
    bkv = jnp.pad(jnp.concatenate([bkv[:HD], bkv[:HD], bkv[HD:], bkv[HD:]]), (0, width - 2 * LANES))
    bq = jnp.concatenate([f[edge : edge + 2 * half].reshape(2, 1, half) for f in (flat, flat_other)], axis=2)
    bi = jnp.concatenate([f[edge + 2 * half :].reshape(2, hid // width, 1, width) for f in (flat, flat_other)], axis=1)
    norms = [flat[n * 4 * width : (n + 1) * 4 * width].reshape(2, 2, width) for n in range(3)]
    small = jnp.concatenate([*norms, bq, jnp.broadcast_to(bkv, (2, 1, width))], axis=1)
    wide_kv = jnp.concatenate([own_kv[:, :HD], own_kv[:, :HD], own_kv[:, HD:], own_kv[:, HD:]], axis=1)

    whole_in = lax.all_gather(inputs, PLANE, axis=1, tiled=True)
    my_in = lax.dynamic_index_in_dim(whole_in, core, 0, keepdims=False)
    my_id = lax.dynamic_index_in_dim(subset_ids, core, 0, keepdims=False)
    matches = my_id == jnp.arange(subset_weight.shape[0], dtype=jnp.int32)
    weight = jnp.sum(jnp.where(matches, subset_weight, 0.0))
    is_first, is_last = stage == 0, stage == 3
    scale = jnp.where(is_last, weight, 1.0).reshape(1)

    tables = turn_tables(length)
    forward_params = (small, bi, *tables, wide_kv)
    hop = jnp.zeros((ROWS, width), BF16)
    saved = None
    for tick in range(ticks):
        number = tick - stage
        valid = (number >= 0) & (number < chunks)
        sc = jnp.stack([valid.astype(jnp.int32), jnp.clip(number, 0, chunks - 1), is_first.astype(jnp.int32), parity])
        saved, hop = fwd_call(ROWS, saved, sc, hop, my_in, forward_params, weights)
        if tick == 0:
            whole_cot = lax.all_gather(after(cotangent, hop), PLANE, axis=1, tiled=True)
        if tick < ticks - 1:
            hop = lax.ppermute(hop, PLANE, AHEAD)
    my_cot = lax.dynamic_index_in_dim(whole_cot, core, 0, keepdims=False)
    kept = dict(zip(FWD_STATE, saved))

    def spread(mine_only, here):
        rows = jnp.where(here, mine_only, jnp.zeros_like(mine_only))[None]
        canvas = jnp.where((jnp.arange(micro) == core)[:, None, None], rows, jnp.zeros_like(rows))
        return lax.psum_scatter(canvas, PLANE, scatter_dimension=1, tiled=True)

    final = spread(kept["y"], is_last)

    backward_params = (small, *tables, own_kv)
    back = None
    for tick in range(ticks):
        number = chunks - 1 - tick + (3 - stage)
        valid = (number >= 0) & (number < chunks)
        sc = jnp.stack([valid.astype(jnp.int32), jnp.clip(number, 0, chunks - 1), is_last.astype(jnp.int32), parity])
        back, hop = bwd_call(ROWS, chunks, back, sc, scale, hop, my_cot, backward_params, weights, saved)
        if tick < ticks - 1:
            hop = lax.ppermute(hop, PLANE, BEHIND)
    got = dict(zip(BWD_STATE, back))
    input_grad = spread(got["gin"], is_first).astype(F32)

    sources = {"h": ("a", "db"), "i": ("h2", "du"), "o": ("o", "db"), "q": ("h1", "dq"), "kv": ("h1", "dkv")}

    def terms(piece, ties):
        name, slot, start, size = piece
        left, right = kept[sources[name][0]][slot], got[sources[name][1]]
        right = after(right, *ties) if ties else right
        if name == "kv":
            one = dot(left, right, ((0,), (0,))).astype(BF16)
            return one, one
        right = right[slot]
        both = []
        for k in range(2):
            if name in "ho":
                at = k * (hid if name == "h" else half) + start
                both.append(dot(left[:, at : at + size], right, ((0,), (0,))).astype(BF16))
            else:
                at = k * (hid if name == "i" else half) + start
                both.append(dot(left, right[:, at : at + size], ((0,), (0,))).astype(BF16))
        return both

    pieces = [("q", 1, 0, half)]
    for slot in (1, 0):
        for name in "hi":
            pieces += [(name, slot, at, hid // 2) for at in (0, hid // 2)]
    pieces += [("o", 1, 0, half), ("o", 0, 0, half), ("q", 0, 0, half), ("kv", 0, 0, 0)]
    if lax.axis_size("dp") == 4:
        done = line_sums(pieces, terms)
    else:
        done = []
        for piece in pieces:
            mine, theirs = terms(piece, [])
            done.append(lax.ppermute(lax.psum(added(mine, other_core(theirs)), "dp"), PLANE, DELIVER))
    done = dict(zip(pieces, done))

    def joined(name, size, axis):
        slots = []
        for slot in range(2):
            parts = [done[p].astype(F32) for p in pieces if p[:2] == (name, slot)]
            slots.append(jnp.concatenate(parts, axis=axis))
        return jnp.stack(slots)[None]

    query = jnp.sum(got["acc"], axis=2)
    inner = jnp.sum(got["accu"], axis=2)
    rolled = jnp.roll(query[:, 5], half, axis=1)
    query = query.at[:, 5].set(jnp.where(core == 0, query[:, 5], rolled))
    inner = jnp.where(core == 0, inner, jnp.roll(inner, hid // width, axis=1))
    acc = jnp.concatenate([query, inner], axis=1)
    acc = acc + other_core(acc)
    acc = lax.ppermute(lax.psum(acc, "dp"), PLANE, DELIVER)
    gain_grad = jnp.stack([acc[:, 1], acc[:, 3]], axis=1)[None]
    bias_grad = jnp.stack([acc[:, 2], acc[:, 4]], axis=1)[None]
    out_bias_grad = jnp.stack([acc[:, 0], acc[:, 0]], axis=1)[None]
    bq_grad = lax.dynamic_slice_in_dim(acc[:, 5], tensor * half, half, axis=1)[None]
    bi_grad = lax.dynamic_slice_in_dim(acc[:, 8:].reshape(2, 2 * hid), tensor * hid, hid, axis=1)[None]
    return (
        final,
        input_grad,
        gain_grad,
        bias_grad,
        joined("q", half, 1),
        bq_grad,
        done["kv", 0, 0, 0].astype(F32)[None],
        acc[0, 6, : 2 * HD][None],
        joined("o", half, 0),
        out_bias_grad,
        joined("i", hid, 1),
        bi_grad,
        joined("h", hid, 0),
    )


def solution(mesh):
    assert mesh.shape["section"] == 4 and mesh.shape["tensor"] == 2
    rows = P("dp", PLANE, None)
    weights = (
        P("section", None, None, None),
        P("section", None, None, None),
        P("section", None, None, "tensor"),
        P("section", None, "tensor"),
        P("section", None, None),
        P("section", None),
        P("section", None, "tensor", None),
        P("section", None, None, None),
        P("section", None, None, "tensor"),
        P("section", None, "tensor"),
        P("section", None, "tensor", None),
    )
    return jax.shard_map(
        local,
        mesh=mesh,
        in_specs=(rows, rows, P("dp"), P(), *weights),
        out_specs=(rows, rows, *weights),
        check_vma=False,
    )
```

```python
import functools
import jax
import jax.numpy as jnp
from jax import lax
from jax.experimental import pallas as pl
from jax.experimental.pallas import tpu as pltpu
from jax.sharding import PartitionSpec as P

HD = 64
ROT = 16
EPS = 1e-05
LANES = 128
ROWS = 256
NORM_ROWS = 64
SPAN = 512
VMEM_LIMIT = 60 * 2**20
ANY = pl.BlockSpec(memory_space=pl.ANY)
SMEM = pl.BlockSpec(memory_space=pltpu.SMEM)
VMEM = pl.BlockSpec(memory_space=pltpu.VMEM)
BF16, F32 = jnp.bfloat16, jnp.float32


def dot(left, right, dims=((1,), (0,))):
    return lax.dot_general(left, right, (dims, ((), ())), preferred_element_type=F32)


def dot_nt(left, right):
    return dot(left, right, ((1,), (1,)))


def turn(values, cosines, ahead, behind):
    return (
        values * cosines
        + pltpu.roll(values, LANES - ROT // 2, axis=1) * ahead
        + pltpu.roll(values, ROT // 2, axis=1) * behind
    )


def normalized(rows):
    centred = rows - jnp.mean(rows, axis=-1, keepdims=True)
    scale = lax.rsqrt(jnp.mean(centred * centred, axis=-1, keepdims=True) + EPS)
    return centred * scale, scale


def hidden_from(span, rows, m):
    key = lax.broadcasted_iota(jnp.int32, (SPAN, 2 * rows), 0)
    query = lax.broadcasted_iota(jnp.int32, (SPAN, 2 * rows), 1) & (rows - 1)
    return key > query + (m * rows - span * SPAN)


def side_by_side(pair):
    return jnp.concatenate([pair[:HD], pair[HD:]], axis=1)


def staged(total, stages):
    def turns(t):
        for half in range(2):
            for k, stage in enumerate(stages):
                u = 2 * t + half - k
                stage(jnp.clip(u, 0, total - 1), (half - k) % 2, u >= 0)

    steps((total + len(stages)) // 2, turns)


def fold(values):
    return jnp.sum(values.reshape(values.shape[0] // 8, 8, values.shape[1]), axis=0)


def steps(size, body):
    def step(i, _):
        body(i)
        return 0

    lax.fori_loop(0, size, step, 0)


def block_of(i, size):
    return pl.ds(pl.multiple_of(i * size, size), size)


FWD_STATE = ("x", "h1", "h2", "q", "qt", "o", "ot", "a", "g", "l", "kd", "vd", "kt", "vt", "y")
BWD_STATE = ("db", "du", "dq", "dkv", "dkw", "acc", "accu", "gin")
READ = ("x", "q", "qt", "ot", "g", "l", "kd", "vd", "kt")
N_W = 16


def state_shapes(length, width, hidden):
    pairs, tiles = width // LANES, hidden // width
    row, ff, one = ((2, length, width), BF16), ((2, length, hidden), BF16), ((length, width), BF16)
    full, chunks = ((2, length, width), F32), length // ROWS
    lse, turned = ((2, chunks, pairs, 1, 2 * ROWS), F32), (2, chunks, pairs, HD, 2 * ROWS)
    wide, tall, total = ((length, LANES), BF16), ((HD, length), BF16), ((length, LANES), F32)
    fwd = dict(x=full, h1=row, h2=row, q=row, qt=(turned, BF16), o=row, ot=(turned, F32), a=ff, g=ff, l=lse, kd=wide, vd=wide, kt=tall, vt=tall, y=one)
    bwd = dict(db=row, du=ff, dq=row, dkv=wide, dkw=total, acc=((2, 8, 8, width), F32), accu=((2, tiles, 8, width), F32), gin=one)
    return fwd, bwd


def weight_waits(stored, weights, wsems, place):
    return {
        name: [pltpu.make_async_copy(stored[4 * n + 2 * k], weights[2 * n + k].at[place], wsems.at[place, 2 * n + k]) for k in range(2)]
        for n, name in enumerate("qoih")
    }


def start_weights(stored, weights, wsems, place, names):
    for held in range(2):

        @pl.when(place == held)
        def _():
            for name in names:
                n = "qoih".index(name)
                for k in range(2):
                    pltpu.make_async_copy(stored[4 * n + 2 * k + held], weights[2 * n + k].at[held], wsems.at[held, 2 * n + k]).start()


def weight_scratch(weights):
    return [pltpu.VMEM((2, *w.shape), BF16) for w in weights[::2]]


def make_struct(item):
    return jax.ShapeDtypeStruct(*item)


def fwd_kernel(rows, fresh, *refs):
    n_state = len(FWD_STATE)
    sc, hop_in, seq_in, small, bi, cos, ahead, behind, wkv = refs[:9]
    stored = refs[9 : 9 + N_W]
    at = 9 + N_W + (0 if fresh else n_state)
    st = dict(zip(FWD_STATE, refs[at : at + n_state]))
    hop_out = refs[at + n_state]
    (x_s, xf_s, h1_s, h2_s, q_s, qt_s, o_s, ot_s, a_s, g_s, l_s, kd_s, vd_s, kt_s, vt_s, vtc_s, s0_s, s1_s, e0_s, e1_s, top_s, sum_s, part_s, *weights, sems, once, wsems) = refs[at + n_state + 1 :]
    wq, wo, wi, wh = (weights[2 * i : 2 * i + 2] for i in range(4))
    width = xf_s.shape[2]
    half, hid = wq[0].shape[2], wi[0].shape[2]
    pairs, tiles, length = width // LANES, hid // width, kd_s.shape[0]

    @pl.when(sc[0] == 1)
    def _():
        m = sc[1]
        place = block_of(m, rows)

        @pl.when(sc[2] == 1)
        def _():
            pltpu.make_async_copy(seq_in.at[sc[4], place], x_s, once.at[0]).start()

        @pl.when(sc[2] == 0)
        def _():
            pltpu.make_async_copy(hop_in, x_s, once.at[0]).start()

        for j in range(2):
            start_weights(stored, weights, wsems, j ^ sc[3], "qioh")
        kd_in = pltpu.make_async_copy(st["kd"], kd_s, once.at[1])
        vt_in = pltpu.make_async_copy(st["vt"], vt_s, once.at[2])
        kd_in.start()
        vt_in.start()
        pltpu.make_async_copy(hop_in, x_s, once.at[0]).wait()
        xf_s[0] = x_s[...].astype(F32)
        tables = (cos[place, :], ahead[place, :], behind[place, :])

        def saves(j):
            pairs_of = (("x", xf_s), ("h1", h1_s), ("h2", h2_s), ("q", q_s), ("o", o_s), ("a", a_s), ("g", g_s))
            out = {n: pltpu.make_async_copy(b.at[j], st[n].at[j, place], sems.at[j, i]) for i, (n, b) in enumerate(pairs_of)}
            for i, (n, b) in enumerate((("l", l_s), ("qt", qt_s), ("ot", ot_s))):
                out[n] = pltpu.make_async_copy(b.at[j], st[n].at[j, m], sems.at[j, 7 + i])
            return out

        kv_saves = (
            pltpu.make_async_copy(kd_s.at[place], st["kd"].at[place], once.at[3]),
            pltpu.make_async_copy(vd_s, st["vd"].at[place], once.at[4]),
            pltpu.make_async_copy(kt_s, st["kt"].at[:, place], once.at[5]),
            pltpu.make_async_copy(vtc_s, st["vt"].at[:, place], once.at[6]),
        )

        def layer(j):
            w = j ^ sc[3]
            loads = weight_waits(stored, weights, wsems, w)
            save = saves(j)
            save["x"].start()

            def norm(r):
                span = block_of(r, NORM_ROWS)
                hat, _ = normalized(xf_s[j, span, :])
                h1_s[j, span, :] = (hat * small[j, 0:1, :] + small[j, 2:3, :]).astype(BF16)
                h2_s[j, span, :] = (hat * small[j, 1:2, :] + small[j, 3:4, :]).astype(BF16)

            steps(rows // NORM_ROWS, norm)
            save["h1"].start()
            save["h2"].start()

            @pl.when(j == 0)
            def _():
                kv = dot(h1_s[j], wkv[...]) + small[j, 7:8, : 2 * LANES]
                keys, values = turn(kv[:, :LANES], *tables), kv[:, LANES:]
                kd_in.wait()
                vt_in.wait()
                kd_s[place, :] = keys.astype(BF16)
                vd_s[...] = values.astype(BF16)
                kt_s[...] = jnp.transpose(keys)[:HD].astype(BF16)
                vtc_s[...] = jnp.transpose(values)[:HD].astype(BF16)
                vt_s[:, place] = vtc_s[...]
                for c in range(1, length // rows):

                    @pl.when(m < c)
                    def _():
                        vt_s[:, c * rows : (c + 1) * rows] = jnp.zeros((HD, rows), BF16)

                for copy in kv_saves:
                    copy.start()

            for k in range(2):
                loads["q"][k].wait()
                query = dot(h1_s[j], wq[k][w]) + small[j, 6:7, k * half : (k + 1) * half]
                for b in range(half // LANES):
                    block = turn(query[:, b * LANES : (b + 1) * LANES], *tables) * HD**-0.5
                    col = k * half + b * LANES
                    q_s[j, :, col : col + LANES] = block.astype(BF16)
                    qt_s[j, col // LANES] = side_by_side(jnp.transpose(block)).astype(BF16)
            save["q"].start()
            save["qt"].start()

            many = m * rows >= SPAN

            def unit(u):
                return (u >= pairs).astype(jnp.int32), jnp.where(u >= pairs, u - pairs, u)

            def scores(u, slot, live):
                span, i = unit(u)
                (s0_s, s1_s)[slot][...] = dot(kd_s[block_of(span, SPAN), :HD], qt_s[j, i])

            def soften(u, slot, live):
                span, i = unit(u)
                score = jnp.where(hidden_from(span, rows, m), -1e30, (s0_s, s1_s)[slot][...])
                top = jnp.max(score, axis=0, keepdims=True)
                expo = jnp.exp(score - top)
                top_s[u] = top
                sum_s[u] = jnp.sum(expo, axis=0, keepdims=True)
                (e0_s, e1_s)[slot][...] = expo.astype(BF16)

            def weigh(u, slot, live):
                span, i = unit(u)
                part_s[u] = dot(vt_s[:, block_of(span, SPAN)], (e0_s, e1_s)[slot][...])

            staged(jnp.where(many, 2 * pairs, pairs), (scores, soften, weigh))

            def gather(i):
                first, second = top_s[i], jnp.where(many, top_s[pairs + i], -1e30)
                top = jnp.maximum(first, second)
                first, second = jnp.exp(first - top), jnp.exp(second - top)
                summed = first * sum_s[i] + jnp.where(many, second * sum_s[pairs + i], 0.0)
                out = first * part_s[i] + jnp.where(many, second * part_s[pairs + i], 0.0)
                out = out / summed
                l_s[j, i] = top + jnp.log(summed)
                ot_s[j, i] = out
                out = jnp.concatenate([out[:, :rows], out[:, rows:]], axis=0)
                o_s[j, :, block_of(i, LANES)] = jnp.transpose(out).astype(BF16)

            steps(pairs, gather)
            for name in ("o", "ot", "l"):
                save[name].start()

            for copy in loads["i"]:
                copy.wait()

            def hidden(t):
                for k in range(2):
                    before = dot(h2_s[j], wi[k][w, :, block_of(t, width)]) + bi[j, k * tiles + t]
                    normal = 0.5 + 0.5 * lax.erf(before * 0.5**0.5)
                    cols = pl.ds(pl.multiple_of(k * hid + t * width, width), width)
                    a_s[j, :, cols] = (before * normal).astype(BF16)
                    slope = normal + before * (jnp.exp(-0.5 * before * before) * 0.3989422804014327)
                    g_s[j, :, cols] = slope.astype(BF16)

            steps(tiles, hidden)
            save["a"].start()
            save["g"].start()
            for copy in loads["o"] + loads["h"]:
                copy.wait()
            branch = dot(a_s[j, :, :hid], wh[0][w]) + dot(a_s[j, :, hid:], wh[1][w])
            branch += dot(o_s[j, :, :half], wo[0][w]) + dot(o_s[j, :, half:], wo[1][w])
            xf_s[j + 1] = xf_s[j] + (branch + small[j, 4:5, :] + small[j, 5:6, :])

        steps(2, layer)
        x_s[...] = xf_s[2].astype(BF16)
        ends = (
            pltpu.make_async_copy(x_s, st["y"].at[place], once.at[7]),
            pltpu.make_async_copy(x_s, hop_out, once.at[8]),
        )
        for copy in ends:
            copy.start()
        for j in range(2):
            for copy in saves(j).values():
                copy.wait()
        for copy in kv_saves + ends:
            copy.wait()


def fwd_call(rows, state, sc, hop, seq, params, weights):
    small, bi, cos, ahead, behind, wkv = params
    _, length, width = seq.shape
    half, hid = weights[0].shape[1], weights[8].shape[1]
    hidden, pairs = 2 * hid, width // LANES
    shapes, _ = state_shapes(length, width, hidden)
    fresh = state is None
    n = len(FWD_STATE)
    scratch = [
        pltpu.VMEM((rows, width), BF16),
        pltpu.VMEM((3, rows, width), F32),
        pltpu.VMEM((2, rows, width), BF16),
        pltpu.VMEM((2, rows, width), BF16),
        pltpu.VMEM((2, rows, width), BF16),
        pltpu.VMEM((2, pairs, HD, 2 * rows), BF16),
        pltpu.VMEM((2, rows, width), BF16),
        pltpu.VMEM((2, pairs, HD, 2 * rows), F32),
        pltpu.VMEM((2, rows, hidden), BF16),
        pltpu.VMEM((2, rows, hidden), BF16),
        pltpu.VMEM((2, pairs, 1, 2 * rows), F32),
        pltpu.VMEM((length, LANES), BF16),
        pltpu.VMEM((rows, LANES), BF16),
        pltpu.VMEM((HD, rows), BF16),
        pltpu.VMEM((HD, length), BF16),
        pltpu.VMEM((HD, rows), BF16),
        pltpu.VMEM((SPAN, 2 * rows), F32),
        pltpu.VMEM((SPAN, 2 * rows), F32),
        pltpu.VMEM((SPAN, 2 * rows), BF16),
        pltpu.VMEM((SPAN, 2 * rows), BF16),
        pltpu.VMEM((2 * pairs, 1, 2 * rows), F32),
        pltpu.VMEM((2 * pairs, 1, 2 * rows), F32),
        pltpu.VMEM((2 * pairs, HD, 2 * rows), F32),
        *weight_scratch(weights),
        pltpu.SemaphoreType.DMA((2, 10)),
        pltpu.SemaphoreType.DMA((9,)),
        pltpu.SemaphoreType.DMA((2, N_W)),
    ]
    outs = pl.pallas_call(
        functools.partial(fwd_kernel, rows, fresh),
        out_shape=[make_struct(shapes[k]) for k in FWD_STATE] + [jax.ShapeDtypeStruct((rows, width), BF16)],
        in_specs=[SMEM, ANY, ANY] + [VMEM] * 6 + [ANY] * (N_W + (0 if fresh else n)),
        out_specs=[ANY] * (n + 1),
        scratch_shapes=scratch,
        input_output_aliases={} if fresh else {9 + N_W + i: i for i in range(n)},
        compiler_params=pltpu.CompilerParams(vmem_limit_bytes=VMEM_LIMIT),
        name="section_forward",
    )(sc, hop, seq, small, bi, cos, ahead, behind, wkv, *weights, *([] if fresh else state))
    return outs[:n], outs[n]


def bwd_kernel(rows, chunks, fresh, *refs):
    n_read, n_state = len(READ), len(BWD_STATE)
    sc, scale, hop_in, cot, small, cos, ahead, behind, wkv = refs[:9]
    stored = refs[9 : 9 + N_W]
    at = 9 + N_W
    rd = dict(zip(READ, refs[at : at + n_read]))
    at += n_read + (0 if fresh else n_state)
    st = dict(zip(BWD_STATE, refs[at : at + n_state]))
    hop_out = refs[at + n_state]
    (in_s, dy_s, x_s, q_s, qt_s, ot_s, g_s, l_s, kd_s, vd_s, kt_s, db_s, do_s, du_s, dq_s, dqt_s, dkv_s, dkw_s, dh1_s, dh2_s, acc_s, accu_s, two_s, dot_s, d_s, s0_s, s1_s, dp0_s, dp1_s, both0_s, both1_s, *weights, sems, outs, once, wsems) = refs[at + n_state + 1 :]
    wq, wo, wi, wh = (weights[2 * i : 2 * i + 2] for i in range(4))
    width = dy_s.shape[1]
    half, hid = wq[0].shape[2], wi[0].shape[2]
    pairs, tiles, length = width // LANES, hid // width, kd_s.shape[0]

    @pl.when(sc[0] == 1)
    def _():
        m = sc[1]
        place = block_of(m, rows)

        @pl.when(sc[2] == 1)
        def _():
            pltpu.make_async_copy(cot.at[sc[4], place], in_s, once.at[0]).start()

        @pl.when(sc[2] == 0)
        def _():
            pltpu.make_async_copy(hop_in, in_s, once.at[0]).start()

        def gets(j):
            named = (("g", g_s), ("q", q_s), ("x", x_s))
            got = {n: pltpu.make_async_copy(rd[n].at[j, place], b.at[j], sems.at[j, i]) for i, (n, b) in enumerate(named)}
            for i, (n, b) in enumerate((("l", l_s), ("qt", qt_s), ("ot", ot_s))):
                got[n] = pltpu.make_async_copy(rd[n].at[j, m], b.at[j], sems.at[j, 3 + i])
            return got

        shared = [pltpu.make_async_copy(rd[n], b, once.at[1 + i]) for i, (n, b) in enumerate((("kd", kd_s), ("vd", vd_s), ("kt", kt_s)))]
        for j in (1, 0):
            start_weights(stored, weights, wsems, j ^ sc[3], "o")
            for copy in list(gets(j).values()) + (shared if j == 1 else []):
                copy.start()
            start_weights(stored, weights, wsems, j ^ sc[3], "qhi")
        running = (("dkw", dkw_s), ("acc", acc_s), ("accu", accu_s))

        @pl.when(m == chunks - 1)
        def _():
            for _, buf in running:
                buf[...] = jnp.zeros_like(buf)

        @pl.when(m < chunks - 1)
        def _():
            copies = [pltpu.make_async_copy(st[n], b, once.at[4 + i]) for i, (n, b) in enumerate(running)]
            for copy in copies:
                copy.start()
            for copy in copies:
                copy.wait()

        pltpu.make_async_copy(hop_in, in_s, once.at[0]).wait()
        dy_s[...] = in_s[...].astype(F32) * scale[0]
        tables = (cos[place, :], -ahead[place, :], -behind[place, :])

        def saves(j):
            named = (("db", db_s), ("du", du_s), ("dq", dq_s))
            return {n: pltpu.make_async_copy(b.at[j], st[n].at[j, place], outs.at[j, i]) for i, (n, b) in enumerate(named)}

        kv_save = pltpu.make_async_copy(dkv_s, st["dkv"].at[place], once.at[8])

        def layer(step):
            j = 1 - step
            w = j ^ sc[3]
            loads = weight_waits(stored, weights, wsems, w)
            got, save = gets(j), saves(j)
            grad = dy_s[...]
            db_s[j] = grad.astype(BF16)
            acc_s[j, 0] += fold(grad)
            save["db"].start()
            for k in range(2):
                loads["o"][k].wait()
                do_s[:, k * half : (k + 1) * half] = dot_nt(db_s[j], wo[k][w]).astype(BF16)
            for name in ("ot", "q", "qt", "l"):
                got[name].wait()

            @pl.when(j == 1)
            def _():
                for copy in shared:
                    copy.wait()

            def ready(i):
                cols = block_of(i, LANES)
                out_grad = do_s[:, cols].astype(F32)
                turned = side_by_side(jnp.transpose(out_grad))
                d_s[i] = jnp.sum(turned * ot_s[j, i], axis=0, keepdims=True)
                dot_s[i] = turned.astype(BF16)
                query = q_s[j, :, cols].astype(F32)
                low = lax.broadcasted_iota(jnp.int32, query.shape, 1) < HD
                parts = (
                    jnp.where(low, query, 0.0),
                    jnp.where(low, pltpu.roll(query, HD, axis=1), 0.0),
                    jnp.where(low, 0.0, pltpu.roll(out_grad, HD, axis=1)),
                    jnp.where(low, 0.0, out_grad),
                )
                for n, part in enumerate(parts):
                    two_s[i, n * rows : (n + 1) * rows, :] = part.astype(BF16)

            steps(pairs, ready)

            def unit(u):
                return (u >= pairs).astype(jnp.int32), jnp.where(u >= pairs, u - pairs, u)

            def scores(u, slot, live):
                span, i = unit(u)
                (s0_s, s1_s)[slot][...] = dot(kd_s[block_of(span, SPAN), :HD], qt_s[j, i])
                (dp0_s, dp1_s)[slot][...] = dot(vd_s[block_of(span, SPAN), :HD], dot_s[i])

            def soften(u, slot, live):
                span, i = unit(u)
                probs = jnp.where(hidden_from(span, rows, m), 0.0, jnp.exp((s0_s, s1_s)[slot][...] - l_s[j, i]))
                both = (both0_s, both1_s)[slot]
                both[:, : 2 * rows] = (probs * ((dp0_s, dp1_s)[slot][...] - d_s[i])).astype(BF16)
                both[:, 2 * rows :] = probs.astype(BF16)

            def weigh(u, slot, live):
                span, i = unit(u)
                place = block_of(span, SPAN)
                dqt_s[u] = dot(kt_s[:, place], (both0_s, both1_s)[slot][:, : 2 * rows])
                part = dot((both0_s, both1_s)[slot][...], two_s[i])

                dkw_s[place, :] += jnp.where(live, part, 0.0)

            many = m * rows >= SPAN
            staged(jnp.where(many, 2 * pairs, pairs), (scores, soften, weigh))

            def finish(i):
                grad = dqt_s[i] + jnp.where(many, dqt_s[pairs + i], 0.0)
                grad = jnp.concatenate([grad[:, :rows], grad[:, rows:]], axis=0)
                turned = turn(jnp.transpose(grad) * HD**-0.5, *tables)
                dq_s[j, :, block_of(i, LANES)] = turned.astype(BF16)

            steps(pairs, finish)
            save["dq"].start()
            acc_s[j, 5] += fold(dq_s[j].astype(F32))
            for copy in loads["q"]:
                copy.wait()
            dh1_s[...] = dot_nt(dq_s[j, :, :half], wq[0][w]) + dot_nt(dq_s[j, :, half:], wq[1][w])

            @pl.when(j == 0)
            def _():
                both = dkw_s[place, :]
                low = lax.broadcasted_iota(jnp.int32, both.shape, 1) < HD
                both = jnp.where(low, turn(both, *tables), both).astype(BF16)
                dkv_s[...] = both
                kv_save.start()
                acc_s[j, 6, :, :LANES] += fold(both.astype(F32))
                dh1_s[...] += dot_nt(both, wkv[...])

            got["g"].wait()
            for copy in loads["h"] + loads["i"]:
                copy.wait()

            def hidden(t):
                for k in range(2):
                    cols = pl.ds(pl.multiple_of(k * hid + t * width, width), width)
                    back = dot_nt(db_s[j], wh[k][w, block_of(t, width), :])
                    back = (back * g_s[j, :, cols].astype(F32)).astype(BF16)
                    du_s[j, :, cols] = back
                    accu_s[j, k * tiles + t] += fold(back.astype(F32))

            steps(tiles, hidden)
            save["du"].start()
            dh2_s[...] = dot_nt(du_s[j, :, :hid], wi[0][w]) + dot_nt(du_s[j, :, hid:], wi[1][w])
            got["x"].wait()

            def norm(r):
                span = block_of(r, NORM_ROWS)
                hat, spread = normalized(x_s[j, span, :])
                first, second = dh1_s[span, :], dh2_s[span, :]
                for i, v in enumerate((first * hat, first, second * hat, second)):
                    acc_s[j, 1 + i] += fold(v)
                inside = first * small[j, 0:1, :] + second * small[j, 1:2, :]
                shift = jnp.mean(inside, axis=-1, keepdims=True)
                tilt = jnp.mean(inside * hat, axis=-1, keepdims=True)
                dy_s[span, :] += spread * (inside - shift - hat * tilt)

            steps(rows // NORM_ROWS, norm)

        steps(2, layer)
        in_s[...] = dy_s[...].astype(BF16)
        ends = [pltpu.make_async_copy(in_s, st["gin"].at[place], once.at[9]), pltpu.make_async_copy(in_s, hop_out, once.at[10])]
        ends += [pltpu.make_async_copy(b, st[n], once.at[4 + i]) for i, (n, b) in enumerate(running)]
        for copy in ends:
            copy.start()
        for j in range(2):
            for copy in saves(j).values():
                copy.wait()
        for copy in ends + [kv_save]:
            copy.wait()


def bwd_call(rows, chunks, state, sc, scale, hop, cot, params, weights, fwd):
    small, cos, ahead, behind, wkv = params
    _, length, width = cot.shape
    half, hid = weights[0].shape[1], weights[8].shape[1]
    hidden, pairs, tiles = 2 * hid, width // LANES, 2 * hid // width
    _, shapes = state_shapes(length, width, hidden)
    fresh = state is None
    n = len(BWD_STATE)
    saved = dict(zip(FWD_STATE, fwd))
    scratch = [
        pltpu.VMEM((rows, width), BF16),
        pltpu.VMEM((rows, width), F32),
        pltpu.VMEM((2, rows, width), F32),
        pltpu.VMEM((2, rows, width), BF16),
        pltpu.VMEM((2, pairs, HD, 2 * rows), BF16),
        pltpu.VMEM((2, pairs, HD, 2 * rows), F32),
        pltpu.VMEM((2, rows, hidden), BF16),
        pltpu.VMEM((2, pairs, 1, 2 * rows), F32),
        pltpu.VMEM((length, LANES), BF16),
        pltpu.VMEM((length, LANES), BF16),
        pltpu.VMEM((HD, length), BF16),
        pltpu.VMEM((2, rows, width), BF16),
        pltpu.VMEM((rows, width), BF16),
        pltpu.VMEM((2, rows, hidden), BF16),
        pltpu.VMEM((2, rows, width), BF16),
        pltpu.VMEM((2 * pairs, HD, 2 * rows), F32),
        pltpu.VMEM((rows, LANES), BF16),
        pltpu.VMEM((length, LANES), F32),
        pltpu.VMEM((rows, width), F32),
        pltpu.VMEM((rows, width), F32),
        pltpu.VMEM((2, 8, 8, width), F32),
        pltpu.VMEM((2, tiles, 8, width), F32),
        pltpu.VMEM((pairs, 4 * rows, LANES), BF16),
        pltpu.VMEM((pairs, HD, 2 * rows), BF16),
        pltpu.VMEM((pairs, 1, 2 * rows), F32),
        pltpu.VMEM((SPAN, 2 * rows), F32),
        pltpu.VMEM((SPAN, 2 * rows), F32),
        pltpu.VMEM((SPAN, 2 * rows), F32),
        pltpu.VMEM((SPAN, 2 * rows), F32),
        pltpu.VMEM((SPAN, 4 * rows), BF16),
        pltpu.VMEM((SPAN, 4 * rows), BF16),
        *weight_scratch(weights),
        pltpu.SemaphoreType.DMA((2, 6)),
        pltpu.SemaphoreType.DMA((2, 3)),
        pltpu.SemaphoreType.DMA((11,)),
        pltpu.SemaphoreType.DMA((2, N_W)),
    ]
    first_state = 9 + N_W + len(READ)
    outs = pl.pallas_call(
        functools.partial(bwd_kernel, rows, chunks, fresh),
        out_shape=[make_struct(shapes[k]) for k in BWD_STATE] + [jax.ShapeDtypeStruct((rows, width), BF16)],
        in_specs=[SMEM, SMEM, ANY, ANY] + [VMEM] * 5 + [ANY] * (N_W + len(READ) + (0 if fresh else n)),
        out_specs=[ANY] * (n + 1),
        scratch_shapes=scratch,
        input_output_aliases={} if fresh else {first_state + i: i for i in range(n)},
        compiler_params=pltpu.CompilerParams(vmem_limit_bytes=VMEM_LIMIT),
        name="section_backward",
    )(sc, scale, hop, cot, small, cos, ahead, behind, wkv, *weights, *[saved[k] for k in READ], *([] if fresh else state))
    return outs[:n], outs[n]


def turn_tables(length):
    column = jnp.arange(LANES) % HD
    half = ROT // 2
    freq = jnp.power(10000.0, -2.0 * (column % half).astype(F32) / ROT)
    angle = jnp.arange(length).astype(F32)[:, None] * freq[None, :]
    cosines = jnp.where((column < ROT)[None, :], jnp.cos(angle), 1.0)
    sines = jnp.sin(angle)
    ahead = jnp.where((column < half)[None, :], -sines, 0.0)
    behind = jnp.where(((column >= half) & (column < ROT))[None, :], sines, 0.0)
    return cosines, ahead, behind


def stage_place(stage):
    across = stage // 2
    return across, (stage % 2 if across == 0 else 1 - stage % 2)


def device(across, core, tensor):
    return (2 * across + core) * 2 + tensor


PLANE = ("section", "tensor")
SWAP = [(0, 1), (1, 0), (2, 3), (3, 2)]


def plane_routes():
    fetch, ahead = [], []
    for stage in range(4):
        across, tensor = stage_place(stage)
        for core in range(2):
            fetch.append((device(across, stage % 2, core), device(across, core, tensor)))
            if stage < 3:
                after, turned = stage_place(stage + 1)
                ahead.append((device(across, core, tensor), device(after, core, turned)))
    return fetch, [(b, a) for a, b in fetch], ahead, [(b, a) for a, b in ahead]


FETCH, DELIVER, AHEAD, BEHIND = plane_routes()


def other_core(value):
    return lax.ppermute(value, "section", SWAP)


def added(left, right):
    return (left.astype(F32) + right.astype(F32)).astype(BF16)


def after(value, *others):
    return lax.optimization_barrier((value, *others))[0]


def line_sums(count, make):
    position = lax.axis_index("dp")
    at_end = (position == 0) | (position == 3)
    own, first, second, third, done = [], [], [], [], []
    for r in range(count + 4):
        if r < count:
            ties = [chain[n] for chain, n in ((first, r - 2), (second, r - 3), (third, r - 4), (done, r - 5)) if n >= 0]
            mine, theirs = make(r, ties)
            term = added(mine, other_core(theirs))
            first.append(added(term, lax.ppermute(term, "dp", [(0, 1), (3, 2)])))
        if 0 <= r - 1 < count:
            part = first[r - 1]
            second.append(added(part, lax.ppermute(part, "dp", [(1, 2), (2, 1)])))
        if 0 <= r - 2 < count:
            whole = second[r - 2]
            third.append(jnp.where(at_end, lax.ppermute(whole, "dp", [(1, 0), (2, 3)]), whole))
        if 0 <= r - 3 < count:
            done.append(lax.ppermute(third[r - 3], PLANE, DELIVER))
    return done, first


def local(
    inputs,
    cotangent,
    subset_ids,
    subset_weight,
    ln_gain,
    ln_bias,
    w_query,
    b_query,
    w_kv,
    b_kv,
    w_out,
    out_bias,
    w_in,
    b_in,
    w_hid_out,
):
    section, tensor = lax.axis_index("section"), lax.axis_index("tensor")
    across, core = section // 2, section % 2
    stage = 2 * across + jnp.where(across == 0, tensor, 1 - tensor)
    micro, part, width = inputs.shape
    length = part * lax.axis_size(PLANE)
    half, hid = w_query.shape[3], w_in.shape[3]
    chunks = length // ROWS
    ticks = chunks + 3

    parity = lax.axis_index("dp") % 2
    pairs = [(i, i ^ 1) for i in range(lax.axis_size("dp"))]
    wholes = (w_in, w_query, w_out, w_hid_out)
    fetched = [lax.ppermute(lax.dynamic_index_in_dim(w[0], parity, 0, keepdims=False), PLANE, FETCH) for w in wholes]
    swapped = [lax.ppermute(w, "dp", pairs) for w in fetched]
    held = dict(zip("iqoh", zip(fetched, [after(w, fetched[3]) for w in fetched], swapped, [after(w, swapped[3]) for w in swapped])))
    weights = []
    for name in "qoih":
        near, tied_near, far, tied_far = held[name]
        weights += [near, far, other_core(tied_near), other_core(tied_far)]
    vectors = jnp.concatenate([v.reshape(-1) for v in (ln_gain, ln_bias, out_bias, b_kv, b_query, b_in)]).reshape(-1, LANES)
    vectors = lax.ppermute(after(vectors, fetched[3]), PLANE, FETCH)
    own_kv = lax.ppermute(after(w_kv[0], fetched[3]), PLANE, FETCH)
    flat, flat_other = vectors.reshape(-1), other_core(vectors).reshape(-1)
    edge = 12 * width + LANES
    bkv = flat[12 * width : edge]
    bkv = jnp.pad(jnp.concatenate([bkv[:HD], bkv[:HD], bkv[HD:], bkv[HD:]]), (0, width - 2 * LANES))
    bq = jnp.concatenate([f[edge : edge + 2 * half].reshape(2, 1, half) for f in (flat, flat_other)], axis=2)
    bi = jnp.concatenate([f[edge + 2 * half :].reshape(2, hid // width, 1, width) for f in (flat, flat_other)], axis=1)
    norms = [flat[n * 4 * width : (n + 1) * 4 * width].reshape(2, 2, width) for n in range(3)]
    small = jnp.concatenate([*norms, bq, jnp.broadcast_to(bkv, (2, 1, width))], axis=1)
    wide_kv = jnp.concatenate([own_kv[:, :HD], own_kv[:, :HD], own_kv[:, HD:], own_kv[:, HD:]], axis=1)

    whole_in = lax.all_gather(after(inputs, fetched[3]), PLANE, axis=1, tiled=True)
    my_id = lax.dynamic_index_in_dim(subset_ids, core, 0, keepdims=False)
    matches = my_id == jnp.arange(subset_weight.shape[0], dtype=jnp.int32)
    weight = jnp.sum(jnp.where(matches, subset_weight, 0.0))
    is_first, is_last = stage == 0, stage == 3
    scale = jnp.where(is_last, weight, 1.0).reshape(1)

    tables = turn_tables(length)
    forward_params = (small, bi, *tables, wide_kv)
    hop = jnp.zeros((ROWS, width), BF16)
    saved = None
    for tick in range(ticks):
        number = tick - stage
        valid = (number >= 0) & (number < chunks)
        sc = jnp.stack([valid.astype(jnp.int32), jnp.clip(number, 0, chunks - 1), is_first.astype(jnp.int32), parity, core])
        saved, hop = fwd_call(ROWS, saved, sc, hop, whole_in, forward_params, weights)
        if tick == 0:
            whole_cot = lax.all_gather(after(cotangent, hop), PLANE, axis=1, tiled=True)
        if tick < ticks - 1:
            hop = lax.ppermute(hop, PLANE, AHEAD)
    kept = dict(zip(FWD_STATE, saved))

    def spread(mine_only, here):
        rows = jnp.where(here, mine_only, jnp.zeros_like(mine_only))[None]
        canvas = jnp.where((jnp.arange(micro) == core)[:, None, None], rows, jnp.zeros_like(rows))
        return lax.psum_scatter(canvas, PLANE, scatter_dimension=1, tiled=True)

    final = spread(kept["y"], is_last)

    backward_params = (small, *tables, own_kv)
    back = None
    for tick in range(ticks):
        number = chunks - 1 - tick + (3 - stage)
        valid = (number >= 0) & (number < chunks)
        sc = jnp.stack([valid.astype(jnp.int32), jnp.clip(number, 0, chunks - 1), is_last.astype(jnp.int32), parity, core])
        back, hop = bwd_call(ROWS, chunks, back, sc, scale, hop, whole_cot, backward_params, weights, saved)
        if tick < ticks - 1:
            hop = lax.ppermute(hop, PLANE, BEHIND)
    got = dict(zip(BWD_STATE, back))

    def part(values, slot, start, size):
        return lax.slice(values, (slot, 0, start), (slot + 1, length, start + size)).reshape(length, size)

    def product(left, right):
        return dot(left, right, ((0,), (0,))).astype(BF16)

    def outer(slot, ties):
        grad = after(got["db"], *ties) if ties else got["db"]
        both = []
        for k in range(2):
            rows = [
                product(part(kept["o"], slot, k * half, half), part(grad, slot, 0, width)),
                product(part(got["dq"], slot, k * half, half), part(kept["h1"], slot, 0, width)),
            ]
            if slot == 0:
                rows.append(product(got["dkv"], part(kept["h1"], slot, 0, width)))
            both.append(jnp.concatenate(rows))
        return both

    def inner_out(slot, ties):
        grad = after(got["db"], *ties) if ties else got["db"]
        return [product(part(kept["a"], slot, k * hid, hid), part(grad, slot, 0, width)) for k in range(2)]

    def inner_in(slot, ties):
        grad = after(got["du"], *ties) if ties else got["du"]
        return [product(part(kept["h2"], slot, 0, width), part(grad, slot, k * hid, hid)) for k in range(2)]

    makers = (
        lambda ties: outer(1, ties),
        lambda ties: inner_out(1, ties),
        lambda ties: inner_in(1, ties),
        lambda ties: inner_out(0, ties),
        lambda ties: inner_in(0, ties),
        lambda ties: outer(0, ties),
    )
    if lax.axis_size("dp") == 4:
        done, sent = line_sums(len(makers), lambda n, ties: makers[n](ties))
        later = after(got["gin"], sent[0])
    else:
        done = []
        for make in makers:
            mine, theirs = make([])
            done.append(lax.ppermute(lax.psum(added(mine, other_core(theirs)), "dp"), PLANE, DELIVER))
        later = got["gin"]
    input_grad = spread(later, is_first).astype(F32)
    out_grad = jnp.stack([done[5][:half], done[0][:half]])[None].astype(F32)
    query_grad = jnp.stack([done[5][half : 2 * half], done[0][half : 2 * half]]).astype(F32)
    query_grad = jnp.swapaxes(query_grad, 1, 2)[None]
    kv_grad = jnp.swapaxes(done[5][2 * half :].astype(F32), 0, 1)[None]
    in_grad = jnp.stack([done[4], done[2]])[None].astype(F32)
    hid_out_grad = jnp.stack([done[3], done[1]])[None].astype(F32)

    query = jnp.sum(got["acc"], axis=2)
    inner = jnp.sum(got["accu"], axis=2)
    rolled = jnp.roll(query[:, 5], half, axis=1)
    query = query.at[:, 5].set(jnp.where(core == 0, query[:, 5], rolled))
    inner = jnp.where(core == 0, inner, jnp.roll(inner, hid // width, axis=1))
    acc = jnp.concatenate([query, inner], axis=1)
    acc = acc + other_core(acc)
    acc = lax.ppermute(lax.psum(acc, "dp"), PLANE, DELIVER)
    gain_grad = jnp.stack([acc[:, 1], acc[:, 3]], axis=1)[None]
    bias_grad = jnp.stack([acc[:, 2], acc[:, 4]], axis=1)[None]
    out_bias_grad = jnp.stack([acc[:, 0], acc[:, 0]], axis=1)[None]
    bq_grad = lax.dynamic_slice_in_dim(acc[:, 5], tensor * half, half, axis=1)[None]
    bi_grad = lax.dynamic_slice_in_dim(acc[:, 8:].reshape(2, 2 * hid), tensor * hid, hid, axis=1)[None]
    return (
        final,
        input_grad,
        gain_grad,
        bias_grad,
        query_grad,
        bq_grad,
        kv_grad,
        acc[0, 6, : 2 * HD][None],
        out_grad,
        out_bias_grad,
        in_grad,
        bi_grad,
        hid_out_grad,
    )


def solution(mesh):
    assert mesh.shape["section"] == 4 and mesh.shape["tensor"] == 2
    rows = P("dp", PLANE, None)
    weights = (
        P("section", None, None, None),
        P("section", None, None, None),
        P("section", None, None, "tensor"),
        P("section", None, "tensor"),
        P("section", None, None),
        P("section", None),
        P("section", None, "tensor", None),
        P("section", None, None, None),
        P("section", None, None, "tensor"),
        P("section", None, "tensor"),
        P("section", None, "tensor", None),
    )
    return jax.shard_map(
        local,
        mesh=mesh,
        in_specs=(rows, rows, P("dp"), P(), *weights),
        out_specs=(rows, rows, *weights),
        check_vma=False,
    )
```

```python
import functools
import jax
import jax.numpy as jnp
from jax import lax
from jax.experimental import pallas as pl
from jax.experimental.pallas import tpu as pltpu
from jax.sharding import PartitionSpec as P

HD = 64
ROT = 16
EPS = 1e-05
LANES = 128
ROWS = 256
OFFLOADED = 0
NORM_ROWS = 64
SPAN = 512
VMEM_LIMIT = 60 * 2**20
ANY = pl.BlockSpec(memory_space=pl.ANY)
SMEM = pl.BlockSpec(memory_space=pltpu.SMEM)
VMEM = pl.BlockSpec(memory_space=pltpu.VMEM)
BF16, F32 = jnp.bfloat16, jnp.float32


def dot(left, right, dims=((1,), (0,))):
    return lax.dot_general(left, right, (dims, ((), ())), preferred_element_type=F32)


def dot_nt(left, right):
    return dot(left, right, ((1,), (1,)))


def turn(values, cosines, ahead, behind):
    return (
        values * cosines
        + pltpu.roll(values, LANES - ROT // 2, axis=1) * ahead
        + pltpu.roll(values, ROT // 2, axis=1) * behind
    )


def normalized(rows):
    centred = rows - jnp.mean(rows, axis=-1, keepdims=True)
    scale = lax.rsqrt(jnp.mean(centred * centred, axis=-1, keepdims=True) + EPS)
    return centred * scale, scale


def hidden_from(span, rows, m):
    key = lax.broadcasted_iota(jnp.int32, (SPAN, 2 * rows), 0)
    query = lax.broadcasted_iota(jnp.int32, (SPAN, 2 * rows), 1) & (rows - 1)
    return key > query + (m * rows - span * SPAN)


def side_by_side(pair):
    return jnp.concatenate([pair[:HD], pair[HD:]], axis=1)


def staged(total, stages):
    def turns(t):
        for half in range(2):
            for k, stage in enumerate(stages):
                u = 2 * t + half - k
                stage(jnp.clip(u, 0, total - 1), (half - k) % 2, u >= 0)

    steps((total + len(stages)) // 2, turns)


def fold(values):
    return jnp.sum(values.reshape(values.shape[0] // 8, 8, values.shape[1]), axis=0)


def steps(size, body):
    def step(i, _):
        body(i)
        return 0

    lax.fori_loop(0, size, step, 0)


def block_of(i, size):
    return pl.ds(pl.multiple_of(i * size, size), size)


FWD_STATE = ("x", "h1", "h2", "q", "qt", "o", "ot", "a", "g", "l", "kd", "vd", "kt", "vt", "y")
BWD_STATE = ("db", "du", "dq", "dkv", "dkw", "acc", "accu", "gin")
READ = ("x", "q", "qt", "ot", "g", "l", "kd", "vd", "kt")
N_W = 16


def state_shapes(length, width, hidden):
    pairs, tiles = width // LANES, hidden // width
    row, ff, one = ((2, length, width), BF16), ((2, length, hidden), BF16), ((length, width), BF16)
    full, chunks = ((2, length, width), F32), length // ROWS
    lse, turned = ((2, chunks, pairs, 1, 2 * ROWS), F32), (2, chunks, pairs, HD, 2 * ROWS)
    wide, tall, total = ((length, LANES), BF16), ((HD, length), BF16), ((length, LANES), F32)
    fwd = dict(x=full, h1=row, h2=row, q=row, qt=(turned, BF16), o=row, ot=(turned, F32), a=ff, g=ff, l=lse, kd=wide, vd=wide, kt=tall, vt=tall, y=one)
    bwd = dict(db=row, du=ff, dq=row, dkv=wide, dkw=total, acc=((2, 8, 8, width), F32), accu=((2, tiles, 8, width), F32), gin=one)
    return fwd, bwd


def weight_waits(stored, weights, wsems, place):
    return {
        name: [pltpu.make_async_copy(stored[4 * n + 2 * k], weights[2 * n + k].at[place], wsems.at[place, 2 * n + k]) for k in range(2)]
        for n, name in enumerate("qoih")
    }


def start_weights(stored, weights, wsems, place, names):
    for held in range(2):

        @pl.when(place == held)
        def _():
            for name in names:
                n = "qoih".index(name)
                for k in range(2):
                    pltpu.make_async_copy(stored[4 * n + 2 * k + held], weights[2 * n + k].at[held], wsems.at[held, 2 * n + k]).start()


def weight_scratch(weights):
    return [pltpu.VMEM((2, *w.shape), BF16) for w in weights[::2]]


def make_struct(item):
    return jax.ShapeDtypeStruct(*item)


def fwd_kernel(rows, fresh, *refs):
    n_state = len(FWD_STATE)
    sc, hop_in, seq_in, small, bi, cos, ahead, behind, wkv = refs[:9]
    stored = refs[9 : 9 + N_W]
    at = 9 + N_W + (0 if fresh else n_state)
    st = dict(zip(FWD_STATE, refs[at : at + n_state]))
    hop_out = refs[at + n_state]
    (x_s, xf_s, h1_s, h2_s, q_s, qt_s, o_s, ot_s, a_s, g_s, l_s, kd_s, vd_s, kt_s, vt_s, vtc_s, s0_s, s1_s, e0_s, e1_s, top_s, sum_s, part_s, *weights, sems, once, wsems) = refs[at + n_state + 1 :]
    wq, wo, wi, wh = (weights[2 * i : 2 * i + 2] for i in range(4))
    width = xf_s.shape[2]
    half, hid = wq[0].shape[2], wi[0].shape[2]
    pairs, tiles, length = width // LANES, hid // width, kd_s.shape[0]

    @pl.when(sc[0] == 1)
    def _():
        m = sc[1]
        place = block_of(m, rows)

        @pl.when(sc[2] == 1)
        def _():
            pltpu.make_async_copy(seq_in.at[sc[4], place], x_s, once.at[0]).start()

        @pl.when(sc[2] == 0)
        def _():
            pltpu.make_async_copy(hop_in, x_s, once.at[0]).start()

        start_weights(stored, weights, wsems, sc[3], "q")
        kd_in = pltpu.make_async_copy(st["kd"], kd_s, once.at[1])
        vt_in = pltpu.make_async_copy(st["vt"], vt_s, once.at[2])
        kd_in.start()
        vt_in.start()
        pltpu.make_async_copy(hop_in, x_s, once.at[0]).wait()
        xf_s[0] = x_s[...].astype(F32)
        tables = (cos[place, :], ahead[place, :], behind[place, :])

        def saves(j):
            pairs_of = (("x", xf_s), ("h1", h1_s), ("h2", h2_s), ("q", q_s), ("o", o_s), ("a", a_s), ("g", g_s))
            out = {n: pltpu.make_async_copy(b.at[j], st[n].at[j, place], sems.at[j, i]) for i, (n, b) in enumerate(pairs_of)}
            for i, (n, b) in enumerate((("l", l_s), ("qt", qt_s), ("ot", ot_s))):
                out[n] = pltpu.make_async_copy(b.at[j], st[n].at[j, m], sems.at[j, 7 + i])
            return out

        kv_saves = (
            pltpu.make_async_copy(kd_s.at[place], st["kd"].at[place], once.at[3]),
            pltpu.make_async_copy(vd_s, st["vd"].at[place], once.at[4]),
            pltpu.make_async_copy(kt_s, st["kt"].at[:, place], once.at[5]),
            pltpu.make_async_copy(vtc_s, st["vt"].at[:, place], once.at[6]),
        )

        def layer(j):
            w = j ^ sc[3]
            loads = weight_waits(stored, weights, wsems, w)
            save = saves(j)
            save["x"].start()

            def norm(r):
                span = block_of(r, NORM_ROWS)
                hat, _ = normalized(xf_s[j, span, :])
                h1_s[j, span, :] = (hat * small[j, 0:1, :] + small[j, 2:3, :]).astype(BF16)
                h2_s[j, span, :] = (hat * small[j, 1:2, :] + small[j, 3:4, :]).astype(BF16)

            steps(rows // NORM_ROWS, norm)
            save["h1"].start()
            save["h2"].start()

            @pl.when(j == 0)
            def _():
                kv = dot(h1_s[j], wkv[...]) + small[j, 7:8, : 2 * LANES]
                keys, values = turn(kv[:, :LANES], *tables), kv[:, LANES:]
                kd_in.wait()
                vt_in.wait()
                kd_s[place, :] = keys.astype(BF16)
                vd_s[...] = values.astype(BF16)
                kt_s[...] = jnp.transpose(keys)[:HD].astype(BF16)
                vtc_s[...] = jnp.transpose(values)[:HD].astype(BF16)
                vt_s[:, place] = vtc_s[...]
                for c in range(1, length // rows):

                    @pl.when(m < c)
                    def _():
                        vt_s[:, c * rows : (c + 1) * rows] = jnp.zeros((HD, rows), BF16)

                for copy in kv_saves:
                    copy.start()

            for copy in loads["q"]:
                copy.wait()
            start_weights(stored, weights, wsems, w, "ioh")
            for k in range(2):
                query = dot(h1_s[j], wq[k][w]) + small[j, 6:7, k * half : (k + 1) * half]
                for b in range(half // LANES):
                    block = turn(query[:, b * LANES : (b + 1) * LANES], *tables) * HD**-0.5
                    col = k * half + b * LANES
                    q_s[j, :, col : col + LANES] = block.astype(BF16)
                    qt_s[j, col // LANES] = side_by_side(jnp.transpose(block)).astype(BF16)
            save["q"].start()
            save["qt"].start()

            many = m * rows >= SPAN

            def unit(u):
                return (u >= pairs).astype(jnp.int32), jnp.where(u >= pairs, u - pairs, u)

            def scores(u, slot, live):
                span, i = unit(u)
                (s0_s, s1_s)[slot][...] = dot(kd_s[block_of(span, SPAN), :HD], qt_s[j, i])

            def soften(u, slot, live):
                span, i = unit(u)
                score = jnp.where(hidden_from(span, rows, m), -1e30, (s0_s, s1_s)[slot][...])
                top = jnp.max(score, axis=0, keepdims=True)
                expo = jnp.exp(score - top)
                top_s[u] = top
                sum_s[u] = jnp.sum(expo, axis=0, keepdims=True)
                (e0_s, e1_s)[slot][...] = expo.astype(BF16)

            def weigh(u, slot, live):
                span, i = unit(u)
                part_s[u] = dot(vt_s[:, block_of(span, SPAN)], (e0_s, e1_s)[slot][...])

            staged(jnp.where(many, 2 * pairs, pairs), (scores, soften, weigh))

            def gather(i):
                first, second = top_s[i], jnp.where(many, top_s[pairs + i], -1e30)
                top = jnp.maximum(first, second)
                first, second = jnp.exp(first - top), jnp.exp(second - top)
                summed = first * sum_s[i] + jnp.where(many, second * sum_s[pairs + i], 0.0)
                out = first * part_s[i] + jnp.where(many, second * part_s[pairs + i], 0.0)
                out = out / summed
                l_s[j, i] = top + jnp.log(summed)
                ot_s[j, i] = out
                out = jnp.concatenate([out[:, :rows], out[:, rows:]], axis=0)
                o_s[j, :, block_of(i, LANES)] = jnp.transpose(out).astype(BF16)

            steps(pairs, gather)
            for name in ("o", "ot", "l"):
                save[name].start()

            for copy in loads["i"]:
                copy.wait()

            def hidden(t):
                for k in range(2):
                    before = dot(h2_s[j], wi[k][w, :, block_of(t, width)]) + bi[j, k * tiles + t]
                    normal = 0.5 + 0.5 * lax.erf(before * 0.5**0.5)
                    cols = pl.ds(pl.multiple_of(k * hid + t * width, width), width)
                    a_s[j, :, cols] = (before * normal).astype(BF16)
                    slope = normal + before * (jnp.exp(-0.5 * before * before) * 0.3989422804014327)
                    g_s[j, :, cols] = slope.astype(BF16)

            steps(tiles, hidden)

            @pl.when(j == 0)
            def _():
                start_weights(stored, weights, wsems, 1 ^ sc[3], "q")

            save["a"].start()
            save["g"].start()
            for copy in loads["o"] + loads["h"]:
                copy.wait()
            branch = dot(a_s[j, :, :hid], wh[0][w]) + dot(a_s[j, :, hid:], wh[1][w])
            branch += dot(o_s[j, :, :half], wo[0][w]) + dot(o_s[j, :, half:], wo[1][w])
            xf_s[j + 1] = xf_s[j] + (branch + small[j, 4:5, :] + small[j, 5:6, :])

        steps(2, layer)
        x_s[...] = xf_s[2].astype(BF16)
        ends = (
            pltpu.make_async_copy(x_s, st["y"].at[place], once.at[7]),
            pltpu.make_async_copy(x_s, hop_out, once.at[8]),
        )
        for copy in ends:
            copy.start()
        for j in range(2):
            for copy in saves(j).values():
                copy.wait()
        for copy in kv_saves + ends:
            copy.wait()


def fwd_call(rows, state, sc, hop, seq, params, weights):
    small, bi, cos, ahead, behind, wkv = params
    _, length, width = seq.shape
    half, hid = weights[0].shape[1], weights[8].shape[1]
    hidden, pairs = 2 * hid, width // LANES
    shapes, _ = state_shapes(length, width, hidden)
    fresh = state is None
    n = len(FWD_STATE)
    scratch = [
        pltpu.VMEM((rows, width), BF16),
        pltpu.VMEM((3, rows, width), F32),
        pltpu.VMEM((2, rows, width), BF16),
        pltpu.VMEM((2, rows, width), BF16),
        pltpu.VMEM((2, rows, width), BF16),
        pltpu.VMEM((2, pairs, HD, 2 * rows), BF16),
        pltpu.VMEM((2, rows, width), BF16),
        pltpu.VMEM((2, pairs, HD, 2 * rows), F32),
        pltpu.VMEM((2, rows, hidden), BF16),
        pltpu.VMEM((2, rows, hidden), BF16),
        pltpu.VMEM((2, pairs, 1, 2 * rows), F32),
        pltpu.VMEM((length, LANES), BF16),
        pltpu.VMEM((rows, LANES), BF16),
        pltpu.VMEM((HD, rows), BF16),
        pltpu.VMEM((HD, length), BF16),
        pltpu.VMEM((HD, rows), BF16),
        pltpu.VMEM((SPAN, 2 * rows), F32),
        pltpu.VMEM((SPAN, 2 * rows), F32),
        pltpu.VMEM((SPAN, 2 * rows), BF16),
        pltpu.VMEM((SPAN, 2 * rows), BF16),
        pltpu.VMEM((2 * pairs, 1, 2 * rows), F32),
        pltpu.VMEM((2 * pairs, 1, 2 * rows), F32),
        pltpu.VMEM((2 * pairs, HD, 2 * rows), F32),
        *weight_scratch(weights),
        pltpu.SemaphoreType.DMA((2, 10)),
        pltpu.SemaphoreType.DMA((9,)),
        pltpu.SemaphoreType.DMA((2, N_W)),
    ]
    outs = pl.pallas_call(
        functools.partial(fwd_kernel, rows, fresh),
        out_shape=[make_struct(shapes[k]) for k in FWD_STATE] + [jax.ShapeDtypeStruct((rows, width), BF16)],
        in_specs=[SMEM, ANY, ANY] + [VMEM] * 6 + [ANY] * (N_W + (0 if fresh else n)),
        out_specs=[ANY] * (n + 1),
        scratch_shapes=scratch,
        input_output_aliases={} if fresh else {9 + N_W + i: i for i in range(n)},
        compiler_params=pltpu.CompilerParams(vmem_limit_bytes=VMEM_LIMIT),
        name="section_forward",
    )(sc, hop, seq, small, bi, cos, ahead, behind, wkv, *weights, *([] if fresh else state))
    return outs[:n], outs[n]


def bwd_kernel(rows, chunks, fresh, *refs):
    n_read, n_state = len(READ), len(BWD_STATE)
    sc, scale, hop_in, cot, small, cos, ahead, behind, wkv = refs[:9]
    stored = refs[9 : 9 + N_W]
    at = 9 + N_W
    rd = dict(zip(READ, refs[at : at + n_read]))
    at += n_read + (0 if fresh else n_state)
    st = dict(zip(BWD_STATE, refs[at : at + n_state]))
    hop_out = refs[at + n_state]
    (in_s, dy_s, x_s, q_s, qt_s, ot_s, g_s, l_s, kd_s, vd_s, kt_s, db_s, do_s, du_s, dq_s, dqt_s, dkv_s, dkw_s, dh1_s, dh2_s, acc_s, accu_s, two_s, dot_s, d_s, s0_s, s1_s, dp0_s, dp1_s, both0_s, both1_s, *weights, sems, outs, once, wsems) = refs[at + n_state + 1 :]
    wq, wo, wi, wh = (weights[2 * i : 2 * i + 2] for i in range(4))
    width = dy_s.shape[1]
    half, hid = wq[0].shape[2], wi[0].shape[2]
    pairs, tiles, length = width // LANES, hid // width, kd_s.shape[0]

    @pl.when(sc[0] == 1)
    def _():
        m = sc[1]
        place = block_of(m, rows)

        @pl.when(sc[2] == 1)
        def _():
            pltpu.make_async_copy(cot.at[sc[4], place], in_s, once.at[0]).start()

        @pl.when(sc[2] == 0)
        def _():
            pltpu.make_async_copy(hop_in, in_s, once.at[0]).start()

        def gets(j):
            named = (("g", g_s), ("q", q_s), ("x", x_s))
            got = {n: pltpu.make_async_copy(rd[n].at[j, place], b.at[j], sems.at[j, i]) for i, (n, b) in enumerate(named)}
            for i, (n, b) in enumerate((("l", l_s), ("qt", qt_s), ("ot", ot_s))):
                got[n] = pltpu.make_async_copy(rd[n].at[j, m], b.at[j], sems.at[j, 3 + i])
            return got

        shared = [pltpu.make_async_copy(rd[n], b, once.at[1 + i]) for i, (n, b) in enumerate((("kd", kd_s), ("vd", vd_s), ("kt", kt_s)))]
        def fetch(j):
            start_weights(stored, weights, wsems, j ^ sc[3], "o")
            for copy in gets(j).values():
                copy.start()

        fetch(1)
        for copy in shared:
            copy.start()
        running = (("dkw", dkw_s), ("acc", acc_s), ("accu", accu_s))

        @pl.when(m == chunks - 1)
        def _():
            for _, buf in running:
                buf[...] = jnp.zeros_like(buf)

        @pl.when(m < chunks - 1)
        def _():
            copies = [pltpu.make_async_copy(st[n], b, once.at[4 + i]) for i, (n, b) in enumerate(running)]
            for copy in copies:
                copy.start()
            for copy in copies:
                copy.wait()

        pltpu.make_async_copy(hop_in, in_s, once.at[0]).wait()
        dy_s[...] = in_s[...].astype(F32) * scale[0]
        tables = (cos[place, :], -ahead[place, :], -behind[place, :])

        def saves(j):
            named = (("db", db_s), ("du", du_s), ("dq", dq_s))
            return {n: pltpu.make_async_copy(b.at[j], st[n].at[j, place], outs.at[j, i]) for i, (n, b) in enumerate(named)}

        kv_save = pltpu.make_async_copy(dkv_s, st["dkv"].at[place], once.at[8])

        def layer(step):
            j = 1 - step
            w = j ^ sc[3]
            loads = weight_waits(stored, weights, wsems, w)
            got, save = gets(j), saves(j)
            grad = dy_s[...]
            db_s[j] = grad.astype(BF16)
            acc_s[j, 0] += fold(grad)
            save["db"].start()
            for copy in loads["o"]:
                copy.wait()
            start_weights(stored, weights, wsems, w, "qhi")
            for k in range(2):
                do_s[:, k * half : (k + 1) * half] = dot_nt(db_s[j], wo[k][w]).astype(BF16)
            for name in ("ot", "q", "qt", "l"):
                got[name].wait()

            @pl.when(j == 1)
            def _():
                for copy in shared:
                    copy.wait()

            def ready(i):
                cols = block_of(i, LANES)
                out_grad = do_s[:, cols].astype(F32)
                turned = side_by_side(jnp.transpose(out_grad))
                d_s[i] = jnp.sum(turned * ot_s[j, i], axis=0, keepdims=True)
                dot_s[i] = turned.astype(BF16)
                query = q_s[j, :, cols].astype(F32)
                low = lax.broadcasted_iota(jnp.int32, query.shape, 1) < HD
                parts = (
                    jnp.where(low, query, 0.0),
                    jnp.where(low, pltpu.roll(query, HD, axis=1), 0.0),
                    jnp.where(low, 0.0, pltpu.roll(out_grad, HD, axis=1)),
                    jnp.where(low, 0.0, out_grad),
                )
                for n, part in enumerate(parts):
                    two_s[i, n * rows : (n + 1) * rows, :] = part.astype(BF16)

            steps(pairs, ready)

            def unit(u):
                return (u >= pairs).astype(jnp.int32), jnp.where(u >= pairs, u - pairs, u)

            def scores(u, slot, live):
                span, i = unit(u)
                (s0_s, s1_s)[slot][...] = dot(kd_s[block_of(span, SPAN), :HD], qt_s[j, i])
                (dp0_s, dp1_s)[slot][...] = dot(vd_s[block_of(span, SPAN), :HD], dot_s[i])

            def soften(u, slot, live):
                span, i = unit(u)
                probs = jnp.where(hidden_from(span, rows, m), 0.0, jnp.exp((s0_s, s1_s)[slot][...] - l_s[j, i]))
                both = (both0_s, both1_s)[slot]
                both[:, : 2 * rows] = (probs * ((dp0_s, dp1_s)[slot][...] - d_s[i])).astype(BF16)
                both[:, 2 * rows :] = probs.astype(BF16)

            def weigh(u, slot, live):
                span, i = unit(u)
                place = block_of(span, SPAN)
                dqt_s[u] = dot(kt_s[:, place], (both0_s, both1_s)[slot][:, : 2 * rows])
                part = dot((both0_s, both1_s)[slot][...], two_s[i])

                dkw_s[place, :] += jnp.where(live, part, 0.0)

            many = m * rows >= SPAN
            staged(jnp.where(many, 2 * pairs, pairs), (scores, soften, weigh))

            def finish(i):
                grad = dqt_s[i] + jnp.where(many, dqt_s[pairs + i], 0.0)
                grad = jnp.concatenate([grad[:, :rows], grad[:, rows:]], axis=0)
                turned = turn(jnp.transpose(grad) * HD**-0.5, *tables)
                dq_s[j, :, block_of(i, LANES)] = turned.astype(BF16)

            steps(pairs, finish)
            save["dq"].start()
            acc_s[j, 5] += fold(dq_s[j].astype(F32))
            for copy in loads["q"]:
                copy.wait()

            @pl.when(j == 1)
            def _():
                fetch(0)

            dh1_s[...] = dot_nt(dq_s[j, :, :half], wq[0][w]) + dot_nt(dq_s[j, :, half:], wq[1][w])

            @pl.when(j == 0)
            def _():
                both = dkw_s[place, :]
                low = lax.broadcasted_iota(jnp.int32, both.shape, 1) < HD
                both = jnp.where(low, turn(both, *tables), both).astype(BF16)
                dkv_s[...] = both
                kv_save.start()
                acc_s[j, 6, :, :LANES] += fold(both.astype(F32))
                dh1_s[...] += dot_nt(both, wkv[...])

            got["g"].wait()
            for copy in loads["h"] + loads["i"]:
                copy.wait()

            def hidden(t):
                for k in range(2):
                    cols = pl.ds(pl.multiple_of(k * hid + t * width, width), width)
                    back = dot_nt(db_s[j], wh[k][w, block_of(t, width), :])
                    back = (back * g_s[j, :, cols].astype(F32)).astype(BF16)
                    du_s[j, :, cols] = back
                    accu_s[j, k * tiles + t] += fold(back.astype(F32))

            steps(tiles, hidden)
            save["du"].start()
            dh2_s[...] = dot_nt(du_s[j, :, :hid], wi[0][w]) + dot_nt(du_s[j, :, hid:], wi[1][w])
            got["x"].wait()

            def norm(r):
                span = block_of(r, NORM_ROWS)
                hat, spread = normalized(x_s[j, span, :])
                first, second = dh1_s[span, :], dh2_s[span, :]
                for i, v in enumerate((first * hat, first, second * hat, second)):
                    acc_s[j, 1 + i] += fold(v)
                inside = first * small[j, 0:1, :] + second * small[j, 1:2, :]
                shift = jnp.mean(inside, axis=-1, keepdims=True)
                tilt = jnp.mean(inside * hat, axis=-1, keepdims=True)
                dy_s[span, :] += spread * (inside - shift - hat * tilt)

            steps(rows // NORM_ROWS, norm)

        steps(2, layer)
        in_s[...] = dy_s[...].astype(BF16)
        ends = [pltpu.make_async_copy(in_s, st["gin"].at[place], once.at[9]), pltpu.make_async_copy(in_s, hop_out, once.at[10])]
        ends += [pltpu.make_async_copy(b, st[n], once.at[4 + i]) for i, (n, b) in enumerate(running)]
        for copy in ends:
            copy.start()
        for j in range(2):
            for copy in saves(j).values():
                copy.wait()
        for copy in ends + [kv_save]:
            copy.wait()


def bwd_call(rows, chunks, state, sc, scale, hop, cot, params, weights, fwd):
    small, cos, ahead, behind, wkv = params
    _, length, width = cot.shape
    half, hid = weights[0].shape[1], weights[8].shape[1]
    hidden, pairs, tiles = 2 * hid, width // LANES, 2 * hid // width
    _, shapes = state_shapes(length, width, hidden)
    fresh = state is None
    n = len(BWD_STATE)
    saved = dict(zip(FWD_STATE, fwd))
    scratch = [
        pltpu.VMEM((rows, width), BF16),
        pltpu.VMEM((rows, width), F32),
        pltpu.VMEM((2, rows, width), F32),
        pltpu.VMEM((2, rows, width), BF16),
        pltpu.VMEM((2, pairs, HD, 2 * rows), BF16),
        pltpu.VMEM((2, pairs, HD, 2 * rows), F32),
        pltpu.VMEM((2, rows, hidden), BF16),
        pltpu.VMEM((2, pairs, 1, 2 * rows), F32),
        pltpu.VMEM((length, LANES), BF16),
        pltpu.VMEM((length, LANES), BF16),
        pltpu.VMEM((HD, length), BF16),
        pltpu.VMEM((2, rows, width), BF16),
        pltpu.VMEM((rows, width), BF16),
        pltpu.VMEM((2, rows, hidden), BF16),
        pltpu.VMEM((2, rows, width), BF16),
        pltpu.VMEM((2 * pairs, HD, 2 * rows), F32),
        pltpu.VMEM((rows, LANES), BF16),
        pltpu.VMEM((length, LANES), F32),
        pltpu.VMEM((rows, width), F32),
        pltpu.VMEM((rows, width), F32),
        pltpu.VMEM((2, 8, 8, width), F32),
        pltpu.VMEM((2, tiles, 8, width), F32),
        pltpu.VMEM((pairs, 4 * rows, LANES), BF16),
        pltpu.VMEM((pairs, HD, 2 * rows), BF16),
        pltpu.VMEM((pairs, 1, 2 * rows), F32),
        pltpu.VMEM((SPAN, 2 * rows), F32),
        pltpu.VMEM((SPAN, 2 * rows), F32),
        pltpu.VMEM((SPAN, 2 * rows), F32),
        pltpu.VMEM((SPAN, 2 * rows), F32),
        pltpu.VMEM((SPAN, 4 * rows), BF16),
        pltpu.VMEM((SPAN, 4 * rows), BF16),
        *weight_scratch(weights),
        pltpu.SemaphoreType.DMA((2, 6)),
        pltpu.SemaphoreType.DMA((2, 3)),
        pltpu.SemaphoreType.DMA((11,)),
        pltpu.SemaphoreType.DMA((2, N_W)),
    ]
    first_state = 9 + N_W + len(READ)
    outs = pl.pallas_call(
        functools.partial(bwd_kernel, rows, chunks, fresh),
        out_shape=[make_struct(shapes[k]) for k in BWD_STATE] + [jax.ShapeDtypeStruct((rows, width), BF16)],
        in_specs=[SMEM, SMEM, ANY, ANY] + [VMEM] * 5 + [ANY] * (N_W + len(READ) + (0 if fresh else n)),
        out_specs=[ANY] * (n + 1),
        scratch_shapes=scratch,
        input_output_aliases={} if fresh else {first_state + i: i for i in range(n)},
        compiler_params=pltpu.CompilerParams(vmem_limit_bytes=VMEM_LIMIT),
        name="section_backward",
    )(sc, scale, hop, cot, small, cos, ahead, behind, wkv, *weights, *[saved[k] for k in READ], *([] if fresh else state))
    return outs[:n], outs[n]


def turn_tables(length):
    column = jnp.arange(LANES) % HD
    half = ROT // 2
    freq = jnp.power(10000.0, -2.0 * (column % half).astype(F32) / ROT)
    angle = jnp.arange(length).astype(F32)[:, None] * freq[None, :]
    cosines = jnp.where((column < ROT)[None, :], jnp.cos(angle), 1.0)
    sines = jnp.sin(angle)
    ahead = jnp.where((column < half)[None, :], -sines, 0.0)
    behind = jnp.where(((column >= half) & (column < ROT))[None, :], sines, 0.0)
    return cosines, ahead, behind


def stage_place(stage):
    across = stage // 2
    return across, (stage % 2 if across == 0 else 1 - stage % 2)


def device(across, core, tensor):
    return (2 * across + core) * 2 + tensor


PLANE = ("section", "tensor")
SWAP = [(0, 1), (1, 0), (2, 3), (3, 2)]


def plane_routes():
    fetch, ahead = [], []
    for stage in range(4):
        across, tensor = stage_place(stage)
        for core in range(2):
            fetch.append((device(across, stage % 2, core), device(across, core, tensor)))
            if stage < 3:
                after, turned = stage_place(stage + 1)
                ahead.append((device(across, core, tensor), device(after, core, turned)))
    return fetch, [(b, a) for a, b in fetch], ahead, [(b, a) for a, b in ahead]


FETCH, DELIVER, AHEAD, BEHIND = plane_routes()


def end_routes():
    def place(plane_index, z):
        section, tensor = plane_index // 2, plane_index % 2
        return (section * 4 + z) * 2 + tensor

    return [(place(a, z), place(b, end)) for a, b in DELIVER for z, end in ((1, 0), (2, 3))]


def routed(value, routes):
    moved = lax.ppermute(value, PLANE, [(a, b) for a, b in routes if a != b])
    here = lax.axis_index(PLANE)
    stays = sum((here == a).astype(jnp.int32) for a, b in routes if a == b) > 0
    return jnp.where(stays, value, moved)


def other_core(value):
    return lax.ppermute(value, "section", SWAP)


def added(left, right):
    return (left.astype(F32) + right.astype(F32)).astype(BF16)


def after(value, *others):
    return lax.optimization_barrier((value, *others))[0]


def line_sums(count, offloaded, make):
    position = lax.axis_index("dp")
    at_end = (position == 0) | (position == 3)
    owners = end_routes()
    sums, terms, first, second, done = [], [], [], [], []

    def finish(n):
        whole = second[n]
        near = routed(whole, DELIVER)
        far = lax.ppermute(whole, ("section", "dp", "tensor"), owners)
        done.append(jnp.where(at_end, far, near))

    steps_left = count - offloaded

    def middle(n):
        part = first[n]
        if n >= 2:
            finish(n - 2)
        if n >= 3:
            part = after(part, done[n - 3])
        second.append(added(part, lax.ppermute(part, "dp", [(1, 2), (2, 1)])))

    for r in range(count):
        n = r - offloaded
        ties = terms[:] if n == 0 else [chain[i] for chain, i in ((first, n - 2), (second, n - 3), (done, n - 4)) if i >= 0]
        mine, theirs = make(r, ties)
        term = added(mine, other_core(theirs))
        if n < 0:
            terms.append(term)
            sums.append(lax.psum(term, "dp"))
            continue
        first.append(added(term, lax.ppermute(term, "dp", [(0, 1), (3, 2)])))
        if n >= 1:
            middle(n - 1)
    for n in range(len(second), steps_left):
        middle(n)
    while len(done) < steps_left:
        finish(len(done))
    return [routed(value, DELIVER) for value in sums] + done, first[1]


def local(
    inputs,
    cotangent,
    subset_ids,
    subset_weight,
    ln_gain,
    ln_bias,
    w_query,
    b_query,
    w_kv,
    b_kv,
    w_out,
    out_bias,
    w_in,
    b_in,
    w_hid_out,
):
    section, tensor = lax.axis_index("section"), lax.axis_index("tensor")
    across, core = section // 2, section % 2
    stage = 2 * across + jnp.where(across == 0, tensor, 1 - tensor)
    micro, part, width = inputs.shape
    length = part * lax.axis_size(PLANE)
    half, hid = w_query.shape[3], w_in.shape[3]
    chunks = length // ROWS
    ticks = chunks + 3

    parity = lax.axis_index("dp") % 2
    pairs = [(i, i ^ 1) for i in range(lax.axis_size("dp"))]
    wholes = (w_in, w_query, w_out, w_hid_out)
    fetched = [routed(lax.dynamic_index_in_dim(w[0], parity, 0, keepdims=False), FETCH) for w in wholes]
    swapped = [lax.ppermute(w, "dp", pairs) for w in fetched]
    vectors = jnp.concatenate([v.reshape(-1) for v in (ln_gain, ln_bias, out_bias, b_kv, b_query, b_in)]).reshape(-1, LANES)
    vectors, own_kv = routed(vectors, FETCH), routed(w_kv[0], FETCH)
    early = (fetched[3], vectors, own_kv)
    held = dict(zip("iqoh", zip(fetched, [after(w, *early) for w in fetched], swapped, [after(w, swapped[3]) for w in swapped])))
    weights = []
    for name in "qoih":
        near, tied_near, far, tied_far = held[name]
        weights += [near, far, other_core(tied_near), other_core(tied_far)]
    flat, flat_other = vectors.reshape(-1), other_core(vectors).reshape(-1)
    edge = 12 * width + LANES
    bkv = flat[12 * width : edge]
    bkv = jnp.pad(jnp.concatenate([bkv[:HD], bkv[:HD], bkv[HD:], bkv[HD:]]), (0, width - 2 * LANES))
    bq = jnp.concatenate([f[edge : edge + 2 * half].reshape(2, 1, half) for f in (flat, flat_other)], axis=2)
    bi = jnp.concatenate([f[edge + 2 * half :].reshape(2, hid // width, 1, width) for f in (flat, flat_other)], axis=1)
    norms = [flat[n * 4 * width : (n + 1) * 4 * width].reshape(2, 2, width) for n in range(3)]
    small = jnp.concatenate([*norms, bq, jnp.broadcast_to(bkv, (2, 1, width))], axis=1)
    wide_kv = jnp.concatenate([own_kv[:, :HD], own_kv[:, :HD], own_kv[:, HD:], own_kv[:, HD:]], axis=1)

    whole_in = lax.all_gather(after(inputs, fetched[3]), PLANE, axis=1, tiled=True)
    my_id = lax.dynamic_index_in_dim(subset_ids, core, 0, keepdims=False)
    matches = my_id == jnp.arange(subset_weight.shape[0], dtype=jnp.int32)
    weight = jnp.sum(jnp.where(matches, subset_weight, 0.0))
    is_first, is_last = stage == 0, stage == 3
    scale = jnp.where(is_last, weight, 1.0).reshape(1)

    tables = turn_tables(length)
    forward_params = (small, bi, *tables, wide_kv)
    hop = jnp.zeros((ROWS, width), BF16)
    saved = None
    for tick in range(ticks):
        number = tick - stage
        valid = (number >= 0) & (number < chunks)
        sc = jnp.stack([valid.astype(jnp.int32), jnp.clip(number, 0, chunks - 1), is_first.astype(jnp.int32), parity, core])
        saved, hop = fwd_call(ROWS, saved, sc, hop, whole_in, forward_params, weights)
        if tick == 0:
            whole_cot = lax.all_gather(after(cotangent, hop), PLANE, axis=1, tiled=True)
        if tick < ticks - 1:
            hop = lax.ppermute(hop, PLANE, AHEAD)
    kept = dict(zip(FWD_STATE, saved))

    def spread(mine_only, here):
        rows = jnp.where(here, mine_only, jnp.zeros_like(mine_only))[None]
        canvas = jnp.where((jnp.arange(micro) == core)[:, None, None], rows, jnp.zeros_like(rows))
        return lax.psum_scatter(canvas, PLANE, scatter_dimension=1, tiled=True)

    final = spread(kept["y"], is_last)

    backward_params = (small, *tables, own_kv)
    back = None
    for tick in range(ticks):
        number = chunks - 1 - tick + (3 - stage)
        valid = (number >= 0) & (number < chunks)
        sc = jnp.stack([valid.astype(jnp.int32), jnp.clip(number, 0, chunks - 1), is_last.astype(jnp.int32), parity, core])
        back, hop = bwd_call(ROWS, chunks, back, sc, scale, hop, whole_cot, backward_params, weights, saved)
        if tick < ticks - 1:
            hop = lax.ppermute(hop, PLANE, BEHIND)
    got = dict(zip(BWD_STATE, back))

    def part(values, slot, start, size):
        return lax.slice(values, (slot, 0, start), (slot + 1, length, start + size)).reshape(length, size)

    def product(left, right):
        return dot(left, right, ((0,), (0,))).astype(BF16)

    def outer(slot, ties):
        grad = after(got["db"], *ties) if ties else got["db"]
        both = []
        for k in range(2):
            rows = [
                product(part(kept["o"], slot, k * half, half), part(grad, slot, 0, width)),
                product(part(got["dq"], slot, k * half, half), part(kept["h1"], slot, 0, width)),
            ]
            if slot == 0:
                rows.append(product(got["dkv"], part(kept["h1"], slot, 0, width)))
            both.append(jnp.concatenate(rows))
        return both

    def inner_out(slot, ties):
        grad = after(got["db"], *ties) if ties else got["db"]
        return [product(part(kept["a"], slot, k * hid, hid), part(grad, slot, 0, width)) for k in range(2)]

    def inner_in(slot, ties):
        grad = after(got["du"], *ties) if ties else got["du"]
        return [product(part(kept["h2"], slot, 0, width), part(grad, slot, k * hid, hid)) for k in range(2)]

    makers = (
        lambda ties: inner_out(1, ties),
        lambda ties: inner_in(1, ties),
        lambda ties: inner_out(0, ties),
        lambda ties: inner_in(0, ties),
        lambda ties: outer(1, ties),
        lambda ties: outer(0, ties),
    )
    if lax.axis_size("dp") == 4:
        done, sent = line_sums(len(makers), OFFLOADED, lambda n, ties: makers[n](ties))
        later = after(got["gin"], sent)
    else:
        done = []
        for make in makers:
            mine, theirs = make([])
            done.append(lax.ppermute(lax.psum(added(mine, other_core(theirs)), "dp"), PLANE, DELIVER))
        later = got["gin"]
    input_grad = spread(later, is_first).astype(F32)
    hid_out_grad = jnp.stack([done[2], done[0]])[None].astype(F32)
    in_grad = jnp.stack([done[3], done[1]])[None].astype(F32)
    out_grad = jnp.stack([done[5][:half], done[4][:half]])[None].astype(F32)
    query_grad = jnp.stack([done[5][half : 2 * half], done[4][half : 2 * half]]).astype(F32)
    query_grad = jnp.swapaxes(query_grad, 1, 2)[None]
    kv_grad = jnp.swapaxes(done[5][2 * half :].astype(F32), 0, 1)[None]

    query = jnp.sum(got["acc"], axis=2)
    inner = jnp.sum(got["accu"], axis=2)
    rolled = jnp.roll(query[:, 5], half, axis=1)
    query = query.at[:, 5].set(jnp.where(core == 0, query[:, 5], rolled))
    inner = jnp.where(core == 0, inner, jnp.roll(inner, hid // width, axis=1))
    acc = jnp.concatenate([query, inner], axis=1)
    acc = acc + other_core(acc)
    acc = lax.ppermute(lax.psum(acc, "dp"), PLANE, DELIVER)
    gain_grad = jnp.stack([acc[:, 1], acc[:, 3]], axis=1)[None]
    bias_grad = jnp.stack([acc[:, 2], acc[:, 4]], axis=1)[None]
    out_bias_grad = jnp.stack([acc[:, 0], acc[:, 0]], axis=1)[None]
    bq_grad = lax.dynamic_slice_in_dim(acc[:, 5], tensor * half, half, axis=1)[None]
    bi_grad = lax.dynamic_slice_in_dim(acc[:, 8:].reshape(2, 2 * hid), tensor * hid, hid, axis=1)[None]
    return (
        final,
        input_grad,
        gain_grad,
        bias_grad,
        query_grad,
        bq_grad,
        kv_grad,
        acc[0, 6, : 2 * HD][None],
        out_grad,
        out_bias_grad,
        in_grad,
        bi_grad,
        hid_out_grad,
    )


def solution(mesh):
    assert mesh.shape["section"] == 4 and mesh.shape["tensor"] == 2
    rows = P("dp", PLANE, None)
    weights = (
        P("section", None, None, None),
        P("section", None, None, None),
        P("section", None, None, "tensor"),
        P("section", None, "tensor"),
        P("section", None, None),
        P("section", None),
        P("section", None, "tensor", None),
        P("section", None, None, None),
        P("section", None, None, "tensor"),
        P("section", None, "tensor"),
        P("section", None, "tensor", None),
    )
    return jax.shard_map(
        local,
        mesh=mesh,
        in_specs=(rows, rows, P("dp"), P(), *weights),
        out_specs=(rows, rows, *weights),
        check_vma=False,
    )
```

```python
import functools
import jax
import jax.numpy as jnp
from jax import lax
from jax.experimental import pallas as pl
from jax.experimental.pallas import tpu as pltpu
from jax.sharding import PartitionSpec as P

HD = 64
ROT = 16
EPS = 1e-05
LANES = 128
ROWS = 256
NORM_ROWS = 64
SPAN = 512
VMEM_LIMIT = 60 * 2**20
ANY = pl.BlockSpec(memory_space=pl.ANY)
SMEM = pl.BlockSpec(memory_space=pltpu.SMEM)
VMEM = pl.BlockSpec(memory_space=pltpu.VMEM)
BF16, F32 = jnp.bfloat16, jnp.float32


def dot(left, right, dims=((1,), (0,))):
    return lax.dot_general(left, right, (dims, ((), ())), preferred_element_type=F32)


def dot_nt(left, right):
    return dot(left, right, ((1,), (1,)))


def turn(values, cosines, ahead, behind):
    return (
        values * cosines
        + pltpu.roll(values, LANES - ROT // 2, axis=1) * ahead
        + pltpu.roll(values, ROT // 2, axis=1) * behind
    )


def normalized(rows):
    centred = rows - jnp.mean(rows, axis=-1, keepdims=True)
    scale = lax.rsqrt(jnp.mean(centred * centred, axis=-1, keepdims=True) + EPS)
    return centred * scale, scale


def hidden_from(span, rows, m):
    key = lax.broadcasted_iota(jnp.int32, (SPAN, 2 * rows), 0)
    query = lax.broadcasted_iota(jnp.int32, (SPAN, 2 * rows), 1) & (rows - 1)
    return key > query + (m * rows - span * SPAN)


def side_by_side(pair):
    return jnp.concatenate([pair[:HD], pair[HD:]], axis=1)


def staged(total, stages):
    def turns(t):
        for half in range(2):
            for k, stage in enumerate(stages):
                u = 2 * t + half - k
                stage(jnp.clip(u, 0, total - 1), (half - k) % 2, u >= 0)

    steps((total + len(stages)) // 2, turns)


def fold(values):
    return jnp.sum(values.reshape(values.shape[0] // 8, 8, values.shape[1]), axis=0)


def steps(size, body):
    def step(i, _):
        body(i)
        return 0

    lax.fori_loop(0, size, step, 0)


def block_of(i, size):
    return pl.ds(pl.multiple_of(i * size, size), size)


FWD_STATE = ("x", "h1", "h2", "q", "qt", "o", "ot", "a", "g", "l", "kd", "vd", "kt", "vt", "y")
BWD_STATE = ("db", "du", "dq", "dkv", "dkw", "acc", "accu", "gin")
READ = ("x", "q", "qt", "ot", "g", "l", "kd", "vd", "kt")
N_W = 16


def state_shapes(length, width, hidden):
    pairs, tiles = width // LANES, hidden // width
    row, ff, one = ((2, length, width), BF16), ((2, length, hidden), BF16), ((length, width), BF16)
    full, chunks = ((2, length, width), F32), length // ROWS
    lse, turned = ((2, chunks, pairs, 1, 2 * ROWS), F32), (2, chunks, pairs, HD, 2 * ROWS)
    wide, tall, total = ((length, LANES), BF16), ((HD, length), BF16), ((length, LANES), F32)
    fwd = dict(x=full, h1=row, h2=row, q=row, qt=(turned, BF16), o=row, ot=(turned, F32), a=ff, g=ff, l=lse, kd=wide, vd=wide, kt=tall, vt=tall, y=one)
    bwd = dict(db=row, du=ff, dq=row, dkv=wide, dkw=total, acc=((2, 8, 8, width), F32), accu=((2, tiles, 8, width), F32), gin=one)
    return fwd, bwd


def weight_waits(stored, weights, wsems, place):
    return {
        name: [pltpu.make_async_copy(stored[4 * n + 2 * k], weights[2 * n + k].at[place], wsems.at[place, 2 * n + k]) for k in range(2)]
        for n, name in enumerate("qoih")
    }


def start_weights(stored, weights, wsems, place, names):
    for held in range(2):

        @pl.when(place == held)
        def _():
            for name in names:
                n = "qoih".index(name)
                for k in range(2):
                    pltpu.make_async_copy(stored[4 * n + 2 * k + held], weights[2 * n + k].at[held], wsems.at[held, 2 * n + k]).start()


def weight_scratch(weights):
    return [pltpu.VMEM((2, *w.shape), BF16) for w in weights[::2]]


def make_struct(item):
    return jax.ShapeDtypeStruct(*item)


def fwd_kernel(rows, fresh, *refs):
    n_state = len(FWD_STATE)
    sc, hop_in, seq_in, small, bi, cos, ahead, behind, wkv = refs[:9]
    stored = refs[9 : 9 + N_W]
    at = 9 + N_W + (0 if fresh else n_state)
    st = dict(zip(FWD_STATE, refs[at : at + n_state]))
    hop_out = refs[at + n_state]
    (x_s, xf_s, h1_s, h2_s, q_s, qt_s, o_s, ot_s, a_s, g_s, l_s, kd_s, vd_s, kt_s, vt_s, vtc_s, s0_s, s1_s, e0_s, e1_s, top_s, sum_s, part_s, *weights, sems, once, wsems) = refs[at + n_state + 1 :]
    wq, wo, wi, wh = (weights[2 * i : 2 * i + 2] for i in range(4))
    width = xf_s.shape[2]
    half, hid = wq[0].shape[2], wi[0].shape[2]
    pairs, tiles, length = width // LANES, hid // width, kd_s.shape[0]

    @pl.when(sc[0] == 1)
    def _():
        m = sc[1]
        place = block_of(m, rows)

        @pl.when(sc[2] == 1)
        def _():
            pltpu.make_async_copy(seq_in.at[sc[4], place], x_s, once.at[0]).start()

        @pl.when(sc[2] == 0)
        def _():
            pltpu.make_async_copy(hop_in, x_s, once.at[0]).start()

        start_weights(stored, weights, wsems, sc[3], "q")
        kd_in = pltpu.make_async_copy(st["kd"], kd_s, once.at[1])
        vt_in = pltpu.make_async_copy(st["vt"], vt_s, once.at[2])
        kd_in.start()
        vt_in.start()
        pltpu.make_async_copy(hop_in, x_s, once.at[0]).wait()
        xf_s[0] = x_s[...].astype(F32)
        tables = (cos[place, :], ahead[place, :], behind[place, :])

        def saves(j):
            pairs_of = (("x", xf_s), ("h1", h1_s), ("h2", h2_s), ("q", q_s), ("o", o_s), ("a", a_s), ("g", g_s))
            out = {n: pltpu.make_async_copy(b.at[j], st[n].at[j, place], sems.at[j, i]) for i, (n, b) in enumerate(pairs_of)}
            for i, (n, b) in enumerate((("l", l_s), ("qt", qt_s), ("ot", ot_s))):
                out[n] = pltpu.make_async_copy(b.at[j], st[n].at[j, m], sems.at[j, 7 + i])
            return out

        kv_saves = (
            pltpu.make_async_copy(kd_s.at[place], st["kd"].at[place], once.at[3]),
            pltpu.make_async_copy(vd_s, st["vd"].at[place], once.at[4]),
            pltpu.make_async_copy(kt_s, st["kt"].at[:, place], once.at[5]),
            pltpu.make_async_copy(vtc_s, st["vt"].at[:, place], once.at[6]),
        )

        def layer(j):
            w = j ^ sc[3]
            loads = weight_waits(stored, weights, wsems, w)
            save = saves(j)
            save["x"].start()

            def norm(r):
                span = block_of(r, NORM_ROWS)
                hat, _ = normalized(xf_s[j, span, :])
                h1_s[j, span, :] = (hat * small[j, 0:1, :] + small[j, 2:3, :]).astype(BF16)
                h2_s[j, span, :] = (hat * small[j, 1:2, :] + small[j, 3:4, :]).astype(BF16)

            steps(rows // NORM_ROWS, norm)
            save["h1"].start()
            save["h2"].start()

            @pl.when(j == 0)
            def _():
                kv = dot(h1_s[j], wkv[...]) + small[j, 7:8, : 2 * LANES]
                keys, values = turn(kv[:, :LANES], *tables), kv[:, LANES:]
                kd_in.wait()
                vt_in.wait()
                kd_s[place, :] = keys.astype(BF16)
                vd_s[...] = values.astype(BF16)
                kt_s[...] = jnp.transpose(keys)[:HD].astype(BF16)
                vtc_s[...] = jnp.transpose(values)[:HD].astype(BF16)
                vt_s[:, place] = vtc_s[...]
                for c in range(1, length // rows):

                    @pl.when(m < c)
                    def _():
                        vt_s[:, c * rows : (c + 1) * rows] = jnp.zeros((HD, rows), BF16)

                for copy in kv_saves:
                    copy.start()

            for copy in loads["q"]:
                copy.wait()
            start_weights(stored, weights, wsems, w, "ioh")
            for k in range(2):
                query = dot(h1_s[j], wq[k][w]) + small[j, 6:7, k * half : (k + 1) * half]
                for b in range(half // LANES):
                    block = turn(query[:, b * LANES : (b + 1) * LANES], *tables) * HD**-0.5
                    col = k * half + b * LANES
                    q_s[j, :, col : col + LANES] = block.astype(BF16)
                    qt_s[j, col // LANES] = side_by_side(jnp.transpose(block)).astype(BF16)
            save["q"].start()
            save["qt"].start()

            many = m * rows >= SPAN

            def unit(u):
                return (u >= pairs).astype(jnp.int32), jnp.where(u >= pairs, u - pairs, u)

            def scores(u, slot, live):
                span, i = unit(u)
                (s0_s, s1_s)[slot][...] = dot(kd_s[block_of(span, SPAN), :HD], qt_s[j, i])

            def soften(u, slot, live):
                span, i = unit(u)
                score = jnp.where(hidden_from(span, rows, m), -1e30, (s0_s, s1_s)[slot][...])
                top = jnp.max(score, axis=0, keepdims=True)
                expo = jnp.exp(score - top)
                top_s[u] = top
                sum_s[u] = jnp.sum(expo, axis=0, keepdims=True)
                (e0_s, e1_s)[slot][...] = expo.astype(BF16)

            def weigh(u, slot, live):
                span, i = unit(u)
                part_s[u] = dot(vt_s[:, block_of(span, SPAN)], (e0_s, e1_s)[slot][...])

            staged(jnp.where(many, 2 * pairs, pairs), (scores, soften, weigh))

            def gather(i):
                first, second = top_s[i], jnp.where(many, top_s[pairs + i], -1e30)
                top = jnp.maximum(first, second)
                first, second = jnp.exp(first - top), jnp.exp(second - top)
                summed = first * sum_s[i] + jnp.where(many, second * sum_s[pairs + i], 0.0)
                out = first * part_s[i] + jnp.where(many, second * part_s[pairs + i], 0.0)
                out = out / summed
                l_s[j, i] = top + jnp.log(summed)
                ot_s[j, i] = out
                out = jnp.concatenate([out[:, :rows], out[:, rows:]], axis=0)
                o_s[j, :, block_of(i, LANES)] = jnp.transpose(out).astype(BF16)

            steps(pairs, gather)
            for name in ("o", "ot", "l"):
                save[name].start()

            for copy in loads["i"]:
                copy.wait()

            def hidden(t):
                for k in range(2):
                    before = dot(h2_s[j], wi[k][w, :, block_of(t, width)]) + bi[j, k * tiles + t]
                    normal = 0.5 + 0.5 * lax.erf(before * 0.5**0.5)
                    cols = pl.ds(pl.multiple_of(k * hid + t * width, width), width)
                    a_s[j, :, cols] = (before * normal).astype(BF16)
                    slope = normal + before * (jnp.exp(-0.5 * before * before) * 0.3989422804014327)
                    g_s[j, :, cols] = slope.astype(BF16)

            steps(tiles, hidden)

            @pl.when(j == 0)
            def _():
                start_weights(stored, weights, wsems, 1 ^ sc[3], "q")

            save["a"].start()
            save["g"].start()
            for copy in loads["o"] + loads["h"]:
                copy.wait()
            branch = dot(a_s[j, :, :hid], wh[0][w]) + dot(a_s[j, :, hid:], wh[1][w])
            branch += dot(o_s[j, :, :half], wo[0][w]) + dot(o_s[j, :, half:], wo[1][w])
            xf_s[j + 1] = xf_s[j] + (branch + small[j, 4:5, :] + small[j, 5:6, :])

        steps(2, layer)
        x_s[...] = xf_s[2].astype(BF16)
        ends = (
            pltpu.make_async_copy(x_s, st["y"].at[place], once.at[7]),
            pltpu.make_async_copy(x_s, hop_out, once.at[8]),
        )
        for copy in ends:
            copy.start()
        for j in range(2):
            for copy in saves(j).values():
                copy.wait()
        for copy in kv_saves + ends:
            copy.wait()


def fwd_call(rows, state, sc, hop, seq, params, weights):
    small, bi, cos, ahead, behind, wkv = params
    _, length, width = seq.shape
    half, hid = weights[0].shape[1], weights[8].shape[1]
    hidden, pairs = 2 * hid, width // LANES
    shapes, _ = state_shapes(length, width, hidden)
    fresh = state is None
    n = len(FWD_STATE)
    scratch = [
        pltpu.VMEM((rows, width), BF16),
        pltpu.VMEM((3, rows, width), F32),
        pltpu.VMEM((2, rows, width), BF16),
        pltpu.VMEM((2, rows, width), BF16),
        pltpu.VMEM((2, rows, width), BF16),
        pltpu.VMEM((2, pairs, HD, 2 * rows), BF16),
        pltpu.VMEM((2, rows, width), BF16),
        pltpu.VMEM((2, pairs, HD, 2 * rows), F32),
        pltpu.VMEM((2, rows, hidden), BF16),
        pltpu.VMEM((2, rows, hidden), BF16),
        pltpu.VMEM((2, pairs, 1, 2 * rows), F32),
        pltpu.VMEM((length, LANES), BF16),
        pltpu.VMEM((rows, LANES), BF16),
        pltpu.VMEM((HD, rows), BF16),
        pltpu.VMEM((HD, length), BF16),
        pltpu.VMEM((HD, rows), BF16),
        pltpu.VMEM((SPAN, 2 * rows), F32),
        pltpu.VMEM((SPAN, 2 * rows), F32),
        pltpu.VMEM((SPAN, 2 * rows), BF16),
        pltpu.VMEM((SPAN, 2 * rows), BF16),
        pltpu.VMEM((2 * pairs, 1, 2 * rows), F32),
        pltpu.VMEM((2 * pairs, 1, 2 * rows), F32),
        pltpu.VMEM((2 * pairs, HD, 2 * rows), F32),
        *weight_scratch(weights),
        pltpu.SemaphoreType.DMA((2, 10)),
        pltpu.SemaphoreType.DMA((9,)),
        pltpu.SemaphoreType.DMA((2, N_W)),
    ]
    outs = pl.pallas_call(
        functools.partial(fwd_kernel, rows, fresh),
        out_shape=[make_struct(shapes[k]) for k in FWD_STATE] + [jax.ShapeDtypeStruct((rows, width), BF16)],
        in_specs=[SMEM, ANY, ANY] + [VMEM] * 6 + [ANY] * (N_W + (0 if fresh else n)),
        out_specs=[ANY] * (n + 1),
        scratch_shapes=scratch,
        input_output_aliases={} if fresh else {9 + N_W + i: i for i in range(n)},
        compiler_params=pltpu.CompilerParams(vmem_limit_bytes=VMEM_LIMIT),
        name="section_forward",
    )(sc, hop, seq, small, bi, cos, ahead, behind, wkv, *weights, *([] if fresh else state))
    return outs[:n], outs[n]


def bwd_kernel(rows, chunks, fresh, *refs):
    n_read, n_state = len(READ), len(BWD_STATE)
    sc, scale, hop_in, cot, small, cos, ahead, behind, wkv = refs[:9]
    stored = refs[9 : 9 + N_W]
    at = 9 + N_W
    rd = dict(zip(READ, refs[at : at + n_read]))
    at += n_read + (0 if fresh else n_state)
    st = dict(zip(BWD_STATE, refs[at : at + n_state]))
    hop_out = refs[at + n_state]
    (in_s, dy_s, x_s, q_s, qt_s, ot_s, g_s, l_s, kd_s, vd_s, kt_s, db_s, do_s, du_s, dq_s, dqt_s, dkv_s, dkw_s, dh1_s, dh2_s, acc_s, accu_s, two_s, dot_s, d_s, s0_s, s1_s, dp0_s, dp1_s, both0_s, both1_s, *weights, sems, outs, once, wsems) = refs[at + n_state + 1 :]
    wq, wo, wi, wh = (weights[2 * i : 2 * i + 2] for i in range(4))
    width = dy_s.shape[1]
    half, hid = wq[0].shape[2], wi[0].shape[2]
    pairs, tiles, length = width // LANES, hid // width, kd_s.shape[0]

    @pl.when(sc[0] == 1)
    def _():
        m = sc[1]
        place = block_of(m, rows)

        @pl.when(sc[2] == 1)
        def _():
            pltpu.make_async_copy(cot.at[sc[4], place], in_s, once.at[0]).start()

        @pl.when(sc[2] == 0)
        def _():
            pltpu.make_async_copy(hop_in, in_s, once.at[0]).start()

        def gets(j):
            named = (("g", g_s), ("q", q_s), ("x", x_s))
            got = {n: pltpu.make_async_copy(rd[n].at[j, place], b.at[j], sems.at[j, i]) for i, (n, b) in enumerate(named)}
            for i, (n, b) in enumerate((("l", l_s), ("qt", qt_s), ("ot", ot_s))):
                got[n] = pltpu.make_async_copy(rd[n].at[j, m], b.at[j], sems.at[j, 3 + i])
            return got

        shared = [pltpu.make_async_copy(rd[n], b, once.at[1 + i]) for i, (n, b) in enumerate((("kd", kd_s), ("vd", vd_s), ("kt", kt_s)))]
        def fetch(j):
            start_weights(stored, weights, wsems, j ^ sc[3], "o")
            for copy in gets(j).values():
                copy.start()

        fetch(1)
        for copy in shared:
            copy.start()
        running = (("dkw", dkw_s), ("acc", acc_s), ("accu", accu_s))

        @pl.when(m == chunks - 1)
        def _():
            for _, buf in running:
                buf[...] = jnp.zeros_like(buf)

        @pl.when(m < chunks - 1)
        def _():
            copies = [pltpu.make_async_copy(st[n], b, once.at[4 + i]) for i, (n, b) in enumerate(running)]
            for copy in copies:
                copy.start()
            for copy in copies:
                copy.wait()

        pltpu.make_async_copy(hop_in, in_s, once.at[0]).wait()
        dy_s[...] = in_s[...].astype(F32) * scale[0]
        tables = (cos[place, :], -ahead[place, :], -behind[place, :])

        def saves(j):
            named = (("db", db_s), ("du", du_s), ("dq", dq_s))
            return {n: pltpu.make_async_copy(b.at[j], st[n].at[j, place], outs.at[j, i]) for i, (n, b) in enumerate(named)}

        kv_save = pltpu.make_async_copy(dkv_s, st["dkv"].at[place], once.at[8])

        def layer(step):
            j = 1 - step
            w = j ^ sc[3]
            loads = weight_waits(stored, weights, wsems, w)
            got, save = gets(j), saves(j)
            grad = dy_s[...]
            db_s[j] = grad.astype(BF16)
            acc_s[j, 0] += fold(grad)
            save["db"].start()
            for copy in loads["o"]:
                copy.wait()
            start_weights(stored, weights, wsems, w, "qhi")
            for k in range(2):
                do_s[:, k * half : (k + 1) * half] = dot_nt(db_s[j], wo[k][w]).astype(BF16)
            for name in ("ot", "q", "qt", "l"):
                got[name].wait()

            @pl.when(j == 1)
            def _():
                for copy in shared:
                    copy.wait()

            def ready(i):
                cols = block_of(i, LANES)
                out_grad = do_s[:, cols].astype(F32)
                turned = side_by_side(jnp.transpose(out_grad))
                d_s[i] = jnp.sum(turned * ot_s[j, i], axis=0, keepdims=True)
                dot_s[i] = turned.astype(BF16)
                query = q_s[j, :, cols].astype(F32)
                low = lax.broadcasted_iota(jnp.int32, query.shape, 1) < HD
                parts = (
                    jnp.where(low, query, 0.0),
                    jnp.where(low, pltpu.roll(query, HD, axis=1), 0.0),
                    jnp.where(low, 0.0, pltpu.roll(out_grad, HD, axis=1)),
                    jnp.where(low, 0.0, out_grad),
                )
                for n, part in enumerate(parts):
                    two_s[i, n * rows : (n + 1) * rows, :] = part.astype(BF16)

            steps(pairs, ready)

            def unit(u):
                return (u >= pairs).astype(jnp.int32), jnp.where(u >= pairs, u - pairs, u)

            def scores(u, slot, live):
                span, i = unit(u)
                (s0_s, s1_s)[slot][...] = dot(kd_s[block_of(span, SPAN), :HD], qt_s[j, i])
                (dp0_s, dp1_s)[slot][...] = dot(vd_s[block_of(span, SPAN), :HD], dot_s[i])

            def soften(u, slot, live):
                span, i = unit(u)
                probs = jnp.where(hidden_from(span, rows, m), 0.0, jnp.exp((s0_s, s1_s)[slot][...] - l_s[j, i]))
                both = (both0_s, both1_s)[slot]
                both[:, : 2 * rows] = (probs * ((dp0_s, dp1_s)[slot][...] - d_s[i])).astype(BF16)
                both[:, 2 * rows :] = probs.astype(BF16)

            def weigh(u, slot, live):
                span, i = unit(u)
                place = block_of(span, SPAN)
                dqt_s[u] = dot(kt_s[:, place], (both0_s, both1_s)[slot][:, : 2 * rows])
                part = dot((both0_s, both1_s)[slot][...], two_s[i])

                dkw_s[place, :] += jnp.where(live, part, 0.0)

            many = m * rows >= SPAN
            staged(jnp.where(many, 2 * pairs, pairs), (scores, soften, weigh))

            def finish(i):
                grad = dqt_s[i] + jnp.where(many, dqt_s[pairs + i], 0.0)
                grad = jnp.concatenate([grad[:, :rows], grad[:, rows:]], axis=0)
                turned = turn(jnp.transpose(grad) * HD**-0.5, *tables)
                dq_s[j, :, block_of(i, LANES)] = turned.astype(BF16)

            steps(pairs, finish)
            save["dq"].start()
            acc_s[j, 5] += fold(dq_s[j].astype(F32))
            for copy in loads["q"]:
                copy.wait()

            @pl.when(j == 1)
            def _():
                fetch(0)

            dh1_s[...] = dot_nt(dq_s[j, :, :half], wq[0][w]) + dot_nt(dq_s[j, :, half:], wq[1][w])

            @pl.when(j == 0)
            def _():
                both = dkw_s[place, :]
                low = lax.broadcasted_iota(jnp.int32, both.shape, 1) < HD
                both = jnp.where(low, turn(both, *tables), both).astype(BF16)
                dkv_s[...] = both
                kv_save.start()
                acc_s[j, 6, :, :LANES] += fold(both.astype(F32))
                dh1_s[...] += dot_nt(both, wkv[...])

            got["g"].wait()
            for copy in loads["h"] + loads["i"]:
                copy.wait()

            def hidden(t):
                for k in range(2):
                    cols = pl.ds(pl.multiple_of(k * hid + t * width, width), width)
                    back = dot_nt(db_s[j], wh[k][w, block_of(t, width), :])
                    back = (back * g_s[j, :, cols].astype(F32)).astype(BF16)
                    du_s[j, :, cols] = back
                    accu_s[j, k * tiles + t] += fold(back.astype(F32))

            steps(tiles, hidden)
            save["du"].start()
            dh2_s[...] = dot_nt(du_s[j, :, :hid], wi[0][w]) + dot_nt(du_s[j, :, hid:], wi[1][w])
            got["x"].wait()

            def norm(r):
                span = block_of(r, NORM_ROWS)
                hat, spread = normalized(x_s[j, span, :])
                first, second = dh1_s[span, :], dh2_s[span, :]
                for i, v in enumerate((first * hat, first, second * hat, second)):
                    acc_s[j, 1 + i] += fold(v)
                inside = first * small[j, 0:1, :] + second * small[j, 1:2, :]
                shift = jnp.mean(inside, axis=-1, keepdims=True)
                tilt = jnp.mean(inside * hat, axis=-1, keepdims=True)
                dy_s[span, :] += spread * (inside - shift - hat * tilt)

            steps(rows // NORM_ROWS, norm)

        steps(2, layer)
        in_s[...] = dy_s[...].astype(BF16)
        ends = [pltpu.make_async_copy(in_s, st["gin"].at[place], once.at[9]), pltpu.make_async_copy(in_s, hop_out, once.at[10])]
        ends += [pltpu.make_async_copy(b, st[n], once.at[4 + i]) for i, (n, b) in enumerate(running)]
        for copy in ends:
            copy.start()
        for j in range(2):
            for copy in saves(j).values():
                copy.wait()
        for copy in ends + [kv_save]:
            copy.wait()


def bwd_call(rows, chunks, state, sc, scale, hop, cot, params, weights, fwd):
    small, cos, ahead, behind, wkv = params
    _, length, width = cot.shape
    half, hid = weights[0].shape[1], weights[8].shape[1]
    hidden, pairs, tiles = 2 * hid, width // LANES, 2 * hid // width
    _, shapes = state_shapes(length, width, hidden)
    fresh = state is None
    n = len(BWD_STATE)
    saved = dict(zip(FWD_STATE, fwd))
    scratch = [
        pltpu.VMEM((rows, width), BF16),
        pltpu.VMEM((rows, width), F32),
        pltpu.VMEM((2, rows, width), F32),
        pltpu.VMEM((2, rows, width), BF16),
        pltpu.VMEM((2, pairs, HD, 2 * rows), BF16),
        pltpu.VMEM((2, pairs, HD, 2 * rows), F32),
        pltpu.VMEM((2, rows, hidden), BF16),
        pltpu.VMEM((2, pairs, 1, 2 * rows), F32),
        pltpu.VMEM((length, LANES), BF16),
        pltpu.VMEM((length, LANES), BF16),
        pltpu.VMEM((HD, length), BF16),
        pltpu.VMEM((2, rows, width), BF16),
        pltpu.VMEM((rows, width), BF16),
        pltpu.VMEM((2, rows, hidden), BF16),
        pltpu.VMEM((2, rows, width), BF16),
        pltpu.VMEM((2 * pairs, HD, 2 * rows), F32),
        pltpu.VMEM((rows, LANES), BF16),
        pltpu.VMEM((length, LANES), F32),
        pltpu.VMEM((rows, width), F32),
        pltpu.VMEM((rows, width), F32),
        pltpu.VMEM((2, 8, 8, width), F32),
        pltpu.VMEM((2, tiles, 8, width), F32),
        pltpu.VMEM((pairs, 4 * rows, LANES), BF16),
        pltpu.VMEM((pairs, HD, 2 * rows), BF16),
        pltpu.VMEM((pairs, 1, 2 * rows), F32),
        pltpu.VMEM((SPAN, 2 * rows), F32),
        pltpu.VMEM((SPAN, 2 * rows), F32),
        pltpu.VMEM((SPAN, 2 * rows), F32),
        pltpu.VMEM((SPAN, 2 * rows), F32),
        pltpu.VMEM((SPAN, 4 * rows), BF16),
        pltpu.VMEM((SPAN, 4 * rows), BF16),
        *weight_scratch(weights),
        pltpu.SemaphoreType.DMA((2, 6)),
        pltpu.SemaphoreType.DMA((2, 3)),
        pltpu.SemaphoreType.DMA((11,)),
        pltpu.SemaphoreType.DMA((2, N_W)),
    ]
    first_state = 9 + N_W + len(READ)
    outs = pl.pallas_call(
        functools.partial(bwd_kernel, rows, chunks, fresh),
        out_shape=[make_struct(shapes[k]) for k in BWD_STATE] + [jax.ShapeDtypeStruct((rows, width), BF16)],
        in_specs=[SMEM, SMEM, ANY, ANY] + [VMEM] * 5 + [ANY] * (N_W + len(READ) + (0 if fresh else n)),
        out_specs=[ANY] * (n + 1),
        scratch_shapes=scratch,
        input_output_aliases={} if fresh else {first_state + i: i for i in range(n)},
        compiler_params=pltpu.CompilerParams(vmem_limit_bytes=VMEM_LIMIT),
        name="section_backward",
    )(sc, scale, hop, cot, small, cos, ahead, behind, wkv, *weights, *[saved[k] for k in READ], *([] if fresh else state))
    return outs[:n], outs[n]


def turn_tables(length):
    column = jnp.arange(LANES) % HD
    half = ROT // 2
    freq = jnp.power(10000.0, -2.0 * (column % half).astype(F32) / ROT)
    angle = jnp.arange(length).astype(F32)[:, None] * freq[None, :]
    cosines = jnp.where((column < ROT)[None, :], jnp.cos(angle), 1.0)
    sines = jnp.sin(angle)
    ahead = jnp.where((column < half)[None, :], -sines, 0.0)
    behind = jnp.where(((column >= half) & (column < ROT))[None, :], sines, 0.0)
    return cosines, ahead, behind


def stage_place(stage):
    across = stage // 2
    return across, (stage % 2 if across == 0 else 1 - stage % 2)


def device(across, core, tensor):
    return (2 * across + core) * 2 + tensor


PLANE = ("section", "tensor")
SWAP = [(0, 1), (1, 0), (2, 3), (3, 2)]


def plane_routes():
    fetch, ahead = [], []
    for stage in range(4):
        across, tensor = stage_place(stage)
        for core in range(2):
            fetch.append((device(across, stage % 2, core), device(across, core, tensor)))
            if stage < 3:
                after, turned = stage_place(stage + 1)
                ahead.append((device(across, core, tensor), device(after, core, turned)))
    return fetch, [(b, a) for a, b in fetch], ahead, [(b, a) for a, b in ahead]


FETCH, DELIVER, AHEAD, BEHIND = plane_routes()


def same_chip(a, b):
    return a // 4 == b // 4 and a % 2 == b % 2


def among(places):
    here = lax.axis_index(PLANE)
    return sum((here == a).astype(jnp.int32) for a in places) > 0


def both_slots(whole, parity):
    own, other = (lax.dynamic_index_in_dim(whole, p, 0, keepdims=False) for p in (parity, 1 - parity))
    near = routed(own, FETCH)
    size = lax.axis_size("dp")
    linked = [b for a, b in FETCH if not same_chip(a, b)]

    def place(b, z):
        return (b // 2 * size + z) * 2 + b % 2

    passed = lax.ppermute(near, ("section", "dp", "tensor"), [(place(b, z ^ 1), place(b, z)) for b in linked for z in range(size)])
    moved = lax.ppermute(other, PLANE, [(a, b) for a, b in FETCH if a != b and same_chip(a, b)])
    far = jnp.where(among([b for a, b in FETCH if a == b]), other, jnp.where(among(linked), passed, moved))
    return near, far


def routed(value, routes):
    moved = lax.ppermute(value, PLANE, [(a, b) for a, b in routes if a != b])
    return jnp.where(among([a for a, b in routes if a == b]), value, moved)


def other_core(value):
    return lax.ppermute(value, "section", SWAP)


def added(left, right):
    return (left.astype(F32) + right.astype(F32)).astype(BF16)


def after(value, *others):
    return lax.optimization_barrier((value, *others))[0]


def line_sums(count, make):
    position = lax.axis_index("dp")
    at_end = (position == 0) | (position == 3)
    terms, arrived, first, second, third, done = [], [], [], [], [], []

    def tied(value, *links):
        values = [chain[n] for chain, n in links if n >= 0]
        return after(value, *values) if values else value

    def advance(n):
        first.append(added(tied(terms[n], (second, n - 1)), arrived[n]))
        across = lax.ppermute(first[n], "dp", [(1, 2), (2, 1)])
        second.append(added(tied(first[n], (third, n - 1), (done, n - 2)), across))
        third.append(jnp.where(at_end, lax.ppermute(second[n], "dp", [(1, 0), (2, 3)]), second[n]))
        done.append(routed(third[n], DELIVER))

    for n in range(count):
        if n >= 3:
            advance(n - 3)
        mine, theirs = make(n, terms[-2:-1])
        terms.append(tied(added(mine, other_core(theirs)), (first, n - 3), (second, n - 3)))
        arrived.append(lax.ppermute(terms[n], "dp", [(0, 1), (3, 2)]))
    for n in range(max(count - 3, 0), count):
        advance(n)
    return done, first[1]


def local(
    inputs,
    cotangent,
    subset_ids,
    subset_weight,
    ln_gain,
    ln_bias,
    w_query,
    b_query,
    w_kv,
    b_kv,
    w_out,
    out_bias,
    w_in,
    b_in,
    w_hid_out,
):
    section, tensor = lax.axis_index("section"), lax.axis_index("tensor")
    across, core = section // 2, section % 2
    stage = 2 * across + jnp.where(across == 0, tensor, 1 - tensor)
    micro, part, width = inputs.shape
    length = part * lax.axis_size(PLANE)
    half, hid = w_query.shape[3], w_in.shape[3]
    chunks = length // ROWS
    ticks = chunks + 3

    parity = lax.axis_index("dp") % 2
    wholes = (w_in, w_query, w_out, w_hid_out)
    fetched, swapped = zip(*(both_slots(w[0], parity) for w in wholes))
    vectors = jnp.concatenate([v.reshape(-1) for v in (ln_gain, ln_bias, out_bias, b_kv, b_query, b_in)]).reshape(-1, LANES)
    vectors, own_kv = routed(vectors, FETCH), routed(w_kv[0], FETCH)
    early = (fetched[3], vectors, own_kv)
    held = dict(zip("iqoh", zip(fetched, [after(w, *early) for w in fetched], swapped, [after(w, swapped[3]) for w in swapped])))
    weights = []
    for name in "qoih":
        near, tied_near, far, tied_far = held[name]
        weights += [near, far, other_core(tied_near), other_core(tied_far)]
    flat, flat_other = vectors.reshape(-1), other_core(vectors).reshape(-1)
    edge = 12 * width + LANES
    bkv = flat[12 * width : edge]
    bkv = jnp.pad(jnp.concatenate([bkv[:HD], bkv[:HD], bkv[HD:], bkv[HD:]]), (0, width - 2 * LANES))
    bq = jnp.concatenate([f[edge : edge + 2 * half].reshape(2, 1, half) for f in (flat, flat_other)], axis=2)
    bi = jnp.concatenate([f[edge + 2 * half :].reshape(2, hid // width, 1, width) for f in (flat, flat_other)], axis=1)
    norms = [flat[n * 4 * width : (n + 1) * 4 * width].reshape(2, 2, width) for n in range(3)]
    small = jnp.concatenate([*norms, bq, jnp.broadcast_to(bkv, (2, 1, width))], axis=1)
    wide_kv = jnp.concatenate([own_kv[:, :HD], own_kv[:, :HD], own_kv[:, HD:], own_kv[:, HD:]], axis=1)

    whole_in = lax.all_gather(after(inputs, fetched[3]), PLANE, axis=1, tiled=True)
    my_id = lax.dynamic_index_in_dim(subset_ids, core, 0, keepdims=False)
    matches = my_id == jnp.arange(subset_weight.shape[0], dtype=jnp.int32)
    weight = jnp.sum(jnp.where(matches, subset_weight, 0.0))
    is_first, is_last = stage == 0, stage == 3
    scale = jnp.where(is_last, weight, 1.0).reshape(1)

    tables = turn_tables(length)
    forward_params = (small, bi, *tables, wide_kv)
    hop = jnp.zeros((ROWS, width), BF16)
    saved = None
    for tick in range(ticks):
        number = tick - stage
        valid = (number >= 0) & (number < chunks)
        sc = jnp.stack([valid.astype(jnp.int32), jnp.clip(number, 0, chunks - 1), is_first.astype(jnp.int32), parity, core])
        saved, hop = fwd_call(ROWS, saved, sc, hop, whole_in, forward_params, weights)
        if tick == 0:
            whole_cot = lax.all_gather(after(cotangent, hop), PLANE, axis=1, tiled=True)
        if tick < ticks - 1:
            hop = lax.ppermute(hop, PLANE, AHEAD)
    kept = dict(zip(FWD_STATE, saved))

    def spread(mine_only, here):
        rows = jnp.where(here, mine_only, jnp.zeros_like(mine_only))[None]
        canvas = jnp.where((jnp.arange(micro) == core)[:, None, None], rows, jnp.zeros_like(rows))
        return lax.psum_scatter(canvas, PLANE, scatter_dimension=1, tiled=True)

    final = spread(kept["y"], is_last)

    backward_params = (small, *tables, own_kv)
    back = None
    for tick in range(ticks):
        number = chunks - 1 - tick + (3 - stage)
        valid = (number >= 0) & (number < chunks)
        sc = jnp.stack([valid.astype(jnp.int32), jnp.clip(number, 0, chunks - 1), is_last.astype(jnp.int32), parity, core])
        back, hop = bwd_call(ROWS, chunks, back, sc, scale, hop, whole_cot, backward_params, weights, saved)
        if tick < ticks - 1:
            hop = lax.ppermute(hop, PLANE, BEHIND)
    got = dict(zip(BWD_STATE, back))

    def part(values, slot, start, size):
        return lax.slice(values, (slot, 0, start), (slot + 1, length, start + size)).reshape(length, size)

    def product(left, right):
        return dot(left, right, ((0,), (0,))).astype(BF16)

    def outer(slot, ties):
        grad = after(got["db"], *ties) if ties else got["db"]
        both = []
        for k in range(2):
            rows = [
                product(part(kept["o"], slot, k * half, half), part(grad, slot, 0, width)),
                product(part(got["dq"], slot, k * half, half), part(kept["h1"], slot, 0, width)),
            ]
            if slot == 0:
                rows.append(product(got["dkv"], part(kept["h1"], slot, 0, width)))
            both.append(jnp.concatenate(rows))
        return both

    def inner_out(slot, ties):
        grad = after(got["db"], *ties) if ties else got["db"]
        return [product(part(kept["a"], slot, k * hid, hid), part(grad, slot, 0, width)) for k in range(2)]

    def inner_in(slot, ties):
        grad = after(got["du"], *ties) if ties else got["du"]
        return [product(part(kept["h2"], slot, 0, width), part(grad, slot, k * hid, hid)) for k in range(2)]

    makers = (
        lambda ties: outer(1, ties),
        lambda ties: inner_out(1, ties),
        lambda ties: inner_in(1, ties),
        lambda ties: inner_out(0, ties),
        lambda ties: inner_in(0, ties),
        lambda ties: outer(0, ties),
    )
    if lax.axis_size("dp") == 4:
        done, sent = line_sums(len(makers), lambda n, ties: makers[n](ties))
        later = after(got["gin"], sent)
    else:
        done = []
        for make in makers:
            mine, theirs = make([])
            done.append(lax.ppermute(lax.psum(added(mine, other_core(theirs)), "dp"), PLANE, DELIVER))
        later = got["gin"]
    input_grad = spread(later, is_first).astype(F32)
    hid_out_grad = jnp.stack([done[3], done[1]])[None].astype(F32)
    in_grad = jnp.stack([done[4], done[2]])[None].astype(F32)
    out_grad = jnp.stack([done[5][:half], done[0][:half]])[None].astype(F32)
    query_grad = jnp.stack([done[5][half : 2 * half], done[0][half : 2 * half]]).astype(F32)
    query_grad = jnp.swapaxes(query_grad, 1, 2)[None]
    kv_grad = jnp.swapaxes(done[5][2 * half :].astype(F32), 0, 1)[None]

    query = jnp.sum(got["acc"], axis=2)
    inner = jnp.sum(got["accu"], axis=2)
    rolled = jnp.roll(query[:, 5], half, axis=1)
    query = query.at[:, 5].set(jnp.where(core == 0, query[:, 5], rolled))
    inner = jnp.where(core == 0, inner, jnp.roll(inner, hid // width, axis=1))
    acc = jnp.concatenate([query, inner], axis=1)
    acc = acc + other_core(acc)
    acc = lax.ppermute(lax.psum(acc, "dp"), PLANE, DELIVER)
    gain_grad = jnp.stack([acc[:, 1], acc[:, 3]], axis=1)[None]
    bias_grad = jnp.stack([acc[:, 2], acc[:, 4]], axis=1)[None]
    out_bias_grad = jnp.stack([acc[:, 0], acc[:, 0]], axis=1)[None]
    bq_grad = lax.dynamic_slice_in_dim(acc[:, 5], tensor * half, half, axis=1)[None]
    bi_grad = lax.dynamic_slice_in_dim(acc[:, 8:].reshape(2, 2 * hid), tensor * hid, hid, axis=1)[None]
    return (
        final,
        input_grad,
        gain_grad,
        bias_grad,
        query_grad,
        bq_grad,
        kv_grad,
        acc[0, 6, : 2 * HD][None],
        out_grad,
        out_bias_grad,
        in_grad,
        bi_grad,
        hid_out_grad,
    )


def solution(mesh):
    assert mesh.shape["section"] == 4 and mesh.shape["tensor"] == 2
    rows = P("dp", PLANE, None)
    weights = (
        P("section", None, None, None),
        P("section", None, None, None),
        P("section", None, None, "tensor"),
        P("section", None, "tensor"),
        P("section", None, None),
        P("section", None),
        P("section", None, "tensor", None),
        P("section", None, None, None),
        P("section", None, None, "tensor"),
        P("section", None, "tensor"),
        P("section", None, "tensor", None),
    )
    return jax.shard_map(
        local,
        mesh=mesh,
        in_specs=(rows, rows, P("dp"), P(), *weights),
        out_specs=(rows, rows, *weights),
        check_vma=False,
    )
```

```python
import functools
import jax
import jax.numpy as jnp
from jax import lax
from jax.experimental import pallas as pl
from jax.experimental.pallas import tpu as pltpu
from jax.sharding import PartitionSpec as P

HD = 64
ROT = 16
EPS = 1e-05
LANES = 128
ROWS = 256
NORM_ROWS = 64
SPAN = 512
WAYS = 3
VMEM_LIMIT = 60 * 2**20
ANY = pl.BlockSpec(memory_space=pl.ANY)
SMEM = pl.BlockSpec(memory_space=pltpu.SMEM)
VMEM = pl.BlockSpec(memory_space=pltpu.VMEM)
BF16, F32 = jnp.bfloat16, jnp.float32


def dot(left, right, dims=((1,), (0,))):
    return lax.dot_general(left, right, (dims, ((), ())), preferred_element_type=F32)


def dot_nt(left, right):
    return dot(left, right, ((1,), (1,)))


def turn(values, cosines, ahead, behind):
    return (
        values * cosines
        + pltpu.roll(values, LANES - ROT // 2, axis=1) * ahead
        + pltpu.roll(values, ROT // 2, axis=1) * behind
    )


def normalized(rows):
    centred = rows - jnp.mean(rows, axis=-1, keepdims=True)
    scale = lax.rsqrt(jnp.mean(centred * centred, axis=-1, keepdims=True) + EPS)
    return centred * scale, scale


def hidden_from(span, rows, m):
    key = lax.broadcasted_iota(jnp.int32, (SPAN, 2 * rows), 0)
    query = lax.broadcasted_iota(jnp.int32, (SPAN, 2 * rows), 1) & (rows - 1)
    return key > query + (m * rows - span * SPAN)


def side_by_side(pair):
    return jnp.concatenate([pair[:HD], pair[HD:]], axis=1)


def staged(total, stages):
    def turns(t):
        for stage in stages:
            for way in range(WAYS):
                stage(WAYS * t + way, way)

    steps(total // WAYS, turns)


def fold(values):
    return jnp.sum(values.reshape(values.shape[0] // 8, 8, values.shape[1]), axis=0)


def steps(size, body):
    def step(i, _):
        body(i)
        return 0

    lax.fori_loop(0, size, step, 0)


def block_of(i, size):
    return pl.ds(pl.multiple_of(i * size, size), size)


FWD_STATE = ("x", "h1", "h2", "q", "qt", "o", "ot", "a", "g", "l", "kd", "vd", "kt", "vt", "y")
BWD_STATE = ("db", "du", "dq", "dkv", "dkw", "acc", "accu", "gin")
READ = ("x", "q", "qt", "ot", "g", "l", "kd", "vd", "kt")
N_W = 16


def state_shapes(length, width, hidden):
    pairs, tiles = width // LANES, hidden // width
    row, ff, one = ((2, length, width), BF16), ((2, length, hidden), BF16), ((length, width), BF16)
    full, chunks = ((2, length, width), F32), length // ROWS
    lse, turned = ((2, chunks, pairs, 1, 2 * ROWS), F32), (2, chunks, pairs, HD, 2 * ROWS)
    wide, tall, total = ((length, LANES), BF16), ((HD, length), BF16), ((length, LANES), F32)
    fwd = dict(x=full, h1=row, h2=row, q=row, qt=(turned, BF16), o=row, ot=(turned, F32), a=ff, g=ff, l=lse, kd=wide, vd=wide, kt=tall, vt=tall, y=one)
    bwd = dict(db=row, du=ff, dq=row, dkv=wide, dkw=total, acc=((2, 8, 8, width), F32), accu=((2, tiles, 8, width), F32), gin=one)
    return fwd, bwd


def weight_waits(stored, weights, wsems, place):
    return {
        name: [pltpu.make_async_copy(stored[4 * n + 2 * k], weights[2 * n + k].at[place], wsems.at[place, 2 * n + k]) for k in range(2)]
        for n, name in enumerate("qoih")
    }


def start_weights(stored, weights, wsems, place, names):
    for held in range(2):

        @pl.when(place == held)
        def _():
            for name in names:
                n = "qoih".index(name)
                for k in range(2):
                    pltpu.make_async_copy(stored[4 * n + 2 * k + held], weights[2 * n + k].at[held], wsems.at[held, 2 * n + k]).start()


def weight_scratch(weights):
    return [pltpu.VMEM((2, *w.shape), BF16) for w in weights[::2]]


def make_struct(item):
    return jax.ShapeDtypeStruct(*item)


def fwd_kernel(rows, fresh, *refs):
    n_state = len(FWD_STATE)
    sc, hop_in, seq_in, small, bi, cos, ahead, behind, wkv = refs[:9]
    stored = refs[9 : 9 + N_W]
    at = 9 + N_W + (0 if fresh else n_state)
    st = dict(zip(FWD_STATE, refs[at : at + n_state]))
    hop_out = refs[at + n_state]
    (x_s, xf_s, h1_s, h2_s, q_s, qt_s, o_s, ot_s, a_s, g_s, l_s, kd_s, vd_s, kt_s, vt_s, vtc_s, s0_s, s1_s, s2_s, e0_s, e1_s, e2_s, top_s, sum_s, part_s, *weights, sems, once, wsems) = refs[at + n_state + 1 :]
    wq, wo, wi, wh = (weights[2 * i : 2 * i + 2] for i in range(4))
    width = xf_s.shape[2]
    half, hid = wq[0].shape[2], wi[0].shape[2]
    pairs, tiles, length = width // LANES, hid // width, kd_s.shape[0]

    @pl.when(sc[0] == 1)
    def _():
        m = sc[1]
        place = block_of(m, rows)

        @pl.when(sc[2] == 1)
        def _():
            pltpu.make_async_copy(seq_in.at[sc[4], place], x_s, once.at[0]).start()

        @pl.when(sc[2] == 0)
        def _():
            pltpu.make_async_copy(hop_in, x_s, once.at[0]).start()

        start_weights(stored, weights, wsems, sc[3], "q")
        kd_in = pltpu.make_async_copy(st["kd"], kd_s, once.at[1])
        vt_in = pltpu.make_async_copy(st["vt"], vt_s, once.at[2])
        kd_in.start()
        vt_in.start()
        pltpu.make_async_copy(hop_in, x_s, once.at[0]).wait()
        xf_s[0] = x_s[...].astype(F32)
        tables = (cos[place, :], ahead[place, :], behind[place, :])

        def saves(j):
            pairs_of = (("x", xf_s), ("h1", h1_s), ("h2", h2_s), ("q", q_s), ("o", o_s), ("a", a_s), ("g", g_s))
            out = {n: pltpu.make_async_copy(b.at[j], st[n].at[j, place], sems.at[j, i]) for i, (n, b) in enumerate(pairs_of)}
            for i, (n, b) in enumerate((("l", l_s), ("qt", qt_s), ("ot", ot_s))):
                out[n] = pltpu.make_async_copy(b.at[j], st[n].at[j, m], sems.at[j, 7 + i])
            return out

        kv_saves = (
            pltpu.make_async_copy(kd_s.at[place], st["kd"].at[place], once.at[3]),
            pltpu.make_async_copy(vd_s, st["vd"].at[place], once.at[4]),
            pltpu.make_async_copy(kt_s, st["kt"].at[:, place], once.at[5]),
            pltpu.make_async_copy(vtc_s, st["vt"].at[:, place], once.at[6]),
        )

        def layer(j):
            w = j ^ sc[3]
            loads = weight_waits(stored, weights, wsems, w)
            save = saves(j)
            save["x"].start()

            def norm(r):
                span = block_of(r, NORM_ROWS)
                hat, _ = normalized(xf_s[j, span, :])
                h1_s[j, span, :] = (hat * small[j, 0:1, :] + small[j, 2:3, :]).astype(BF16)
                h2_s[j, span, :] = (hat * small[j, 1:2, :] + small[j, 3:4, :]).astype(BF16)

            steps(rows // NORM_ROWS, norm)
            save["h1"].start()
            save["h2"].start()

            @pl.when(j == 0)
            def _():
                kv = dot(h1_s[j], wkv[...]) + small[j, 7:8, : 2 * LANES]
                keys, values = turn(kv[:, :LANES], *tables), kv[:, LANES:]
                kd_in.wait()
                vt_in.wait()
                kd_s[place, :] = keys.astype(BF16)
                vd_s[...] = values.astype(BF16)
                kt_s[...] = jnp.transpose(keys)[:HD].astype(BF16)
                vtc_s[...] = jnp.transpose(values)[:HD].astype(BF16)
                vt_s[:, place] = vtc_s[...]
                for c in range(1, length // rows):

                    @pl.when(m < c)
                    def _():
                        vt_s[:, c * rows : (c + 1) * rows] = jnp.zeros((HD, rows), BF16)

                for copy in kv_saves:
                    copy.start()

            for copy in loads["q"]:
                copy.wait()
            start_weights(stored, weights, wsems, w, "ioh")
            for k in range(2):
                query = dot(h1_s[j], wq[k][w]) + small[j, 6:7, k * half : (k + 1) * half]
                for b in range(half // LANES):
                    block = turn(query[:, b * LANES : (b + 1) * LANES], *tables) * HD**-0.5
                    col = k * half + b * LANES
                    q_s[j, :, col : col + LANES] = block.astype(BF16)
                    qt_s[j, col // LANES] = side_by_side(jnp.transpose(block)).astype(BF16)
            save["q"].start()
            save["qt"].start()

            many = m * rows >= SPAN

            def unit(u):
                return (u >= pairs).astype(jnp.int32), jnp.where(u >= pairs, u - pairs, u)

            def scores(u, slot):
                span, i = unit(u)
                (s0_s, s1_s, s2_s)[slot][...] = dot(kd_s[block_of(span, SPAN), :HD], qt_s[j, i])

            def soften(u, slot):
                span, i = unit(u)
                score = jnp.where(hidden_from(span, rows, m), -1e30, (s0_s, s1_s, s2_s)[slot][...])
                top = jnp.max(score, axis=0, keepdims=True)
                expo = jnp.exp(score - top)
                top_s[u] = top
                sum_s[u] = jnp.sum(expo, axis=0, keepdims=True)
                (e0_s, e1_s, e2_s)[slot][...] = expo.astype(BF16)

            def weigh(u, slot):
                span, i = unit(u)
                part_s[u] = dot(vt_s[:, block_of(span, SPAN)], (e0_s, e1_s, e2_s)[slot][...])

            staged(jnp.where(many, 2 * pairs, pairs), (scores, soften, weigh))

            def gather(i):
                first, second = top_s[i], jnp.where(many, top_s[pairs + i], -1e30)
                top = jnp.maximum(first, second)
                first, second = jnp.exp(first - top), jnp.exp(second - top)
                summed = first * sum_s[i] + jnp.where(many, second * sum_s[pairs + i], 0.0)
                out = first * part_s[i] + jnp.where(many, second * part_s[pairs + i], 0.0)
                out = out / summed
                l_s[j, i] = top + jnp.log(summed)
                ot_s[j, i] = out
                out = jnp.concatenate([out[:, :rows], out[:, rows:]], axis=0)
                o_s[j, :, block_of(i, LANES)] = jnp.transpose(out).astype(BF16)

            steps(pairs, gather)
            for name in ("o", "ot", "l"):
                save[name].start()

            for copy in loads["i"]:
                copy.wait()

            def hidden(t):
                for k in range(2):
                    before = dot(h2_s[j], wi[k][w, :, block_of(t, width)]) + bi[j, k * tiles + t]
                    normal = 0.5 + 0.5 * lax.erf(before * 0.5**0.5)
                    cols = pl.ds(pl.multiple_of(k * hid + t * width, width), width)
                    a_s[j, :, cols] = (before * normal).astype(BF16)
                    slope = normal + before * (jnp.exp(-0.5 * before * before) * 0.3989422804014327)
                    g_s[j, :, cols] = slope.astype(BF16)

            steps(tiles, hidden)

            @pl.when(j == 0)
            def _():
                start_weights(stored, weights, wsems, 1 ^ sc[3], "q")

            save["a"].start()
            save["g"].start()
            for copy in loads["o"] + loads["h"]:
                copy.wait()
            branch = dot(a_s[j, :, :hid], wh[0][w]) + dot(a_s[j, :, hid:], wh[1][w])
            branch += dot(o_s[j, :, :half], wo[0][w]) + dot(o_s[j, :, half:], wo[1][w])
            xf_s[j + 1] = xf_s[j] + (branch + small[j, 4:5, :] + small[j, 5:6, :])

        steps(2, layer)
        x_s[...] = xf_s[2].astype(BF16)
        ends = (
            pltpu.make_async_copy(x_s, st["y"].at[place], once.at[7]),
            pltpu.make_async_copy(x_s, hop_out, once.at[8]),
        )
        for copy in ends:
            copy.start()
        for j in range(2):
            for copy in saves(j).values():
                copy.wait()
        for copy in kv_saves + ends:
            copy.wait()


def fwd_call(rows, state, sc, hop, seq, params, weights):
    small, bi, cos, ahead, behind, wkv = params
    _, length, width = seq.shape
    half, hid = weights[0].shape[1], weights[8].shape[1]
    hidden, pairs = 2 * hid, width // LANES
    shapes, _ = state_shapes(length, width, hidden)
    fresh = state is None
    n = len(FWD_STATE)
    scratch = [
        pltpu.VMEM((rows, width), BF16),
        pltpu.VMEM((3, rows, width), F32),
        pltpu.VMEM((2, rows, width), BF16),
        pltpu.VMEM((2, rows, width), BF16),
        pltpu.VMEM((2, rows, width), BF16),
        pltpu.VMEM((2, pairs, HD, 2 * rows), BF16),
        pltpu.VMEM((2, rows, width), BF16),
        pltpu.VMEM((2, pairs, HD, 2 * rows), F32),
        pltpu.VMEM((2, rows, hidden), BF16),
        pltpu.VMEM((2, rows, hidden), BF16),
        pltpu.VMEM((2, pairs, 1, 2 * rows), F32),
        pltpu.VMEM((length, LANES), BF16),
        pltpu.VMEM((rows, LANES), BF16),
        pltpu.VMEM((HD, rows), BF16),
        pltpu.VMEM((HD, length), BF16),
        pltpu.VMEM((HD, rows), BF16),
        pltpu.VMEM((SPAN, 2 * rows), F32),
        pltpu.VMEM((SPAN, 2 * rows), F32),
        pltpu.VMEM((SPAN, 2 * rows), F32),
        pltpu.VMEM((SPAN, 2 * rows), BF16),
        pltpu.VMEM((SPAN, 2 * rows), BF16),
        pltpu.VMEM((SPAN, 2 * rows), BF16),
        pltpu.VMEM((2 * pairs, 1, 2 * rows), F32),
        pltpu.VMEM((2 * pairs, 1, 2 * rows), F32),
        pltpu.VMEM((2 * pairs, HD, 2 * rows), F32),
        *weight_scratch(weights),
        pltpu.SemaphoreType.DMA((2, 10)),
        pltpu.SemaphoreType.DMA((9,)),
        pltpu.SemaphoreType.DMA((2, N_W)),
    ]
    outs = pl.pallas_call(
        functools.partial(fwd_kernel, rows, fresh),
        out_shape=[make_struct(shapes[k]) for k in FWD_STATE] + [jax.ShapeDtypeStruct((rows, width), BF16)],
        in_specs=[SMEM, ANY, ANY] + [VMEM] * 6 + [ANY] * (N_W + (0 if fresh else n)),
        out_specs=[ANY] * (n + 1),
        scratch_shapes=scratch,
        input_output_aliases={} if fresh else {9 + N_W + i: i for i in range(n)},
        compiler_params=pltpu.CompilerParams(vmem_limit_bytes=VMEM_LIMIT),
        name="section_forward",
    )(sc, hop, seq, small, bi, cos, ahead, behind, wkv, *weights, *([] if fresh else state))
    return outs[:n], outs[n]


def bwd_kernel(rows, chunks, fresh, *refs):
    n_read, n_state = len(READ), len(BWD_STATE)
    sc, scale, hop_in, cot, small, cos, ahead, behind, wkv = refs[:9]
    stored = refs[9 : 9 + N_W]
    at = 9 + N_W
    rd = dict(zip(READ, refs[at : at + n_read]))
    at += n_read + (0 if fresh else n_state)
    st = dict(zip(BWD_STATE, refs[at : at + n_state]))
    hop_out = refs[at + n_state]
    (in_s, dy_s, x_s, q_s, qt_s, ot_s, g_s, l_s, kd_s, vd_s, kt_s, db_s, do_s, du_s, dq_s, dqt_s, dkv_s, dkw_s, dh1_s, dh2_s, acc_s, accu_s, two_s, dot_s, d_s, s0_s, s1_s, s2_s, dp0_s, dp1_s, dp2_s, both0_s, both1_s, both2_s, *weights, sems, outs, once, wsems) = refs[at + n_state + 1 :]
    wq, wo, wi, wh = (weights[2 * i : 2 * i + 2] for i in range(4))
    width = dy_s.shape[1]
    half, hid = wq[0].shape[2], wi[0].shape[2]
    pairs, tiles, length = width // LANES, hid // width, kd_s.shape[0]

    @pl.when(sc[0] == 1)
    def _():
        m = sc[1]
        place = block_of(m, rows)

        @pl.when(sc[2] == 1)
        def _():
            pltpu.make_async_copy(cot.at[sc[4], place], in_s, once.at[0]).start()

        @pl.when(sc[2] == 0)
        def _():
            pltpu.make_async_copy(hop_in, in_s, once.at[0]).start()

        def gets(j):
            named = (("g", g_s), ("q", q_s), ("x", x_s))
            got = {n: pltpu.make_async_copy(rd[n].at[j, place], b.at[j], sems.at[j, i]) for i, (n, b) in enumerate(named)}
            for i, (n, b) in enumerate((("l", l_s), ("qt", qt_s), ("ot", ot_s))):
                got[n] = pltpu.make_async_copy(rd[n].at[j, m], b.at[j], sems.at[j, 3 + i])
            return got

        shared = [pltpu.make_async_copy(rd[n], b, once.at[1 + i]) for i, (n, b) in enumerate((("kd", kd_s), ("vd", vd_s), ("kt", kt_s)))]
        def fetch(j):
            start_weights(stored, weights, wsems, j ^ sc[3], "o")
            for copy in gets(j).values():
                copy.start()

        fetch(1)
        for copy in shared:
            copy.start()
        running = (("dkw", dkw_s), ("acc", acc_s), ("accu", accu_s))

        @pl.when(m == chunks - 1)
        def _():
            for _, buf in running:
                buf[...] = jnp.zeros_like(buf)

        @pl.when(m < chunks - 1)
        def _():
            copies = [pltpu.make_async_copy(st[n], b, once.at[4 + i]) for i, (n, b) in enumerate(running)]
            for copy in copies:
                copy.start()
            for copy in copies:
                copy.wait()

        pltpu.make_async_copy(hop_in, in_s, once.at[0]).wait()
        dy_s[...] = in_s[...].astype(F32) * scale[0]
        tables = (cos[place, :], -ahead[place, :], -behind[place, :])

        def saves(j):
            named = (("db", db_s), ("du", du_s), ("dq", dq_s))
            return {n: pltpu.make_async_copy(b.at[j], st[n].at[j, place], outs.at[j, i]) for i, (n, b) in enumerate(named)}

        kv_save = pltpu.make_async_copy(dkv_s, st["dkv"].at[place], once.at[8])

        def layer(step):
            j = 1 - step
            w = j ^ sc[3]
            loads = weight_waits(stored, weights, wsems, w)
            got, save = gets(j), saves(j)
            grad = dy_s[...]
            db_s[j] = grad.astype(BF16)
            acc_s[j, 0] += fold(grad)
            save["db"].start()
            for copy in loads["o"]:
                copy.wait()
            start_weights(stored, weights, wsems, w, "qhi")
            for k in range(2):
                do_s[:, k * half : (k + 1) * half] = dot_nt(db_s[j], wo[k][w]).astype(BF16)
            for name in ("ot", "q", "qt", "l"):
                got[name].wait()

            @pl.when(j == 1)
            def _():
                for copy in shared:
                    copy.wait()

            def ready(i):
                cols = block_of(i, LANES)
                out_grad = do_s[:, cols].astype(F32)
                turned = side_by_side(jnp.transpose(out_grad))
                d_s[i] = jnp.sum(turned * ot_s[j, i], axis=0, keepdims=True)
                dot_s[i] = turned.astype(BF16)
                query = q_s[j, :, cols].astype(F32)
                low = lax.broadcasted_iota(jnp.int32, query.shape, 1) < HD
                parts = (
                    jnp.where(low, query, 0.0),
                    jnp.where(low, pltpu.roll(query, HD, axis=1), 0.0),
                    jnp.where(low, 0.0, pltpu.roll(out_grad, HD, axis=1)),
                    jnp.where(low, 0.0, out_grad),
                )
                for n, part in enumerate(parts):
                    two_s[i, n * rows : (n + 1) * rows, :] = part.astype(BF16)

            steps(pairs, ready)

            def unit(u):
                return (u >= pairs).astype(jnp.int32), jnp.where(u >= pairs, u - pairs, u)

            def scores(u, slot):
                span, i = unit(u)
                (s0_s, s1_s, s2_s)[slot][...] = dot(kd_s[block_of(span, SPAN), :HD], qt_s[j, i])
                (dp0_s, dp1_s, dp2_s)[slot][...] = dot(vd_s[block_of(span, SPAN), :HD], dot_s[i])

            def soften(u, slot):
                span, i = unit(u)
                probs = jnp.where(hidden_from(span, rows, m), 0.0, jnp.exp((s0_s, s1_s, s2_s)[slot][...] - l_s[j, i]))
                both = (both0_s, both1_s, both2_s)[slot]
                both[:, : 2 * rows] = (probs * ((dp0_s, dp1_s, dp2_s)[slot][...] - d_s[i])).astype(BF16)
                both[:, 2 * rows :] = probs.astype(BF16)

            def weigh(u, slot):
                span, i = unit(u)
                place = block_of(span, SPAN)
                dqt_s[u] = dot(kt_s[:, place], (both0_s, both1_s, both2_s)[slot][:, : 2 * rows])
                part = dot((both0_s, both1_s, both2_s)[slot][...], two_s[i])

                dkw_s[place, :] += part

            many = m * rows >= SPAN
            staged(jnp.where(many, 2 * pairs, pairs), (scores, soften, weigh))

            def finish(i):
                grad = dqt_s[i] + jnp.where(many, dqt_s[pairs + i], 0.0)
                grad = jnp.concatenate([grad[:, :rows], grad[:, rows:]], axis=0)
                turned = turn(jnp.transpose(grad) * HD**-0.5, *tables)
                dq_s[j, :, block_of(i, LANES)] = turned.astype(BF16)

            steps(pairs, finish)
            save["dq"].start()
            acc_s[j, 5] += fold(dq_s[j].astype(F32))
            for copy in loads["q"]:
                copy.wait()

            @pl.when(j == 1)
            def _():
                fetch(0)

            dh1_s[...] = dot_nt(dq_s[j, :, :half], wq[0][w]) + dot_nt(dq_s[j, :, half:], wq[1][w])

            @pl.when(j == 0)
            def _():
                both = dkw_s[place, :]
                low = lax.broadcasted_iota(jnp.int32, both.shape, 1) < HD
                both = jnp.where(low, turn(both, *tables), both).astype(BF16)
                dkv_s[...] = both
                kv_save.start()
                acc_s[j, 6, :, :LANES] += fold(both.astype(F32))
                dh1_s[...] += dot_nt(both, wkv[...])

            got["g"].wait()
            for copy in loads["h"] + loads["i"]:
                copy.wait()

            def hidden(t):
                for k in range(2):
                    cols = pl.ds(pl.multiple_of(k * hid + t * width, width), width)
                    back = dot_nt(db_s[j], wh[k][w, block_of(t, width), :])
                    back = (back * g_s[j, :, cols].astype(F32)).astype(BF16)
                    du_s[j, :, cols] = back
                    accu_s[j, k * tiles + t] += fold(back.astype(F32))

            steps(tiles, hidden)
            save["du"].start()
            dh2_s[...] = dot_nt(du_s[j, :, :hid], wi[0][w]) + dot_nt(du_s[j, :, hid:], wi[1][w])
            got["x"].wait()

            def norm(r):
                span = block_of(r, NORM_ROWS)
                hat, spread = normalized(x_s[j, span, :])
                first, second = dh1_s[span, :], dh2_s[span, :]
                for i, v in enumerate((first * hat, first, second * hat, second)):
                    acc_s[j, 1 + i] += fold(v)
                inside = first * small[j, 0:1, :] + second * small[j, 1:2, :]
                shift = jnp.mean(inside, axis=-1, keepdims=True)
                tilt = jnp.mean(inside * hat, axis=-1, keepdims=True)
                dy_s[span, :] += spread * (inside - shift - hat * tilt)

            steps(rows // NORM_ROWS, norm)

        steps(2, layer)
        in_s[...] = dy_s[...].astype(BF16)
        ends = [pltpu.make_async_copy(in_s, st["gin"].at[place], once.at[9]), pltpu.make_async_copy(in_s, hop_out, once.at[10])]
        ends += [pltpu.make_async_copy(b, st[n], once.at[4 + i]) for i, (n, b) in enumerate(running)]
        for copy in ends:
            copy.start()
        for j in range(2):
            for copy in saves(j).values():
                copy.wait()
        for copy in ends + [kv_save]:
            copy.wait()


def bwd_call(rows, chunks, state, sc, scale, hop, cot, params, weights, fwd):
    small, cos, ahead, behind, wkv = params
    _, length, width = cot.shape
    half, hid = weights[0].shape[1], weights[8].shape[1]
    hidden, pairs, tiles = 2 * hid, width // LANES, 2 * hid // width
    _, shapes = state_shapes(length, width, hidden)
    fresh = state is None
    n = len(BWD_STATE)
    saved = dict(zip(FWD_STATE, fwd))
    scratch = [
        pltpu.VMEM((rows, width), BF16),
        pltpu.VMEM((rows, width), F32),
        pltpu.VMEM((2, rows, width), F32),
        pltpu.VMEM((2, rows, width), BF16),
        pltpu.VMEM((2, pairs, HD, 2 * rows), BF16),
        pltpu.VMEM((2, pairs, HD, 2 * rows), F32),
        pltpu.VMEM((2, rows, hidden), BF16),
        pltpu.VMEM((2, pairs, 1, 2 * rows), F32),
        pltpu.VMEM((length, LANES), BF16),
        pltpu.VMEM((length, LANES), BF16),
        pltpu.VMEM((HD, length), BF16),
        pltpu.VMEM((2, rows, width), BF16),
        pltpu.VMEM((rows, width), BF16),
        pltpu.VMEM((2, rows, hidden), BF16),
        pltpu.VMEM((2, rows, width), BF16),
        pltpu.VMEM((2 * pairs, HD, 2 * rows), F32),
        pltpu.VMEM((rows, LANES), BF16),
        pltpu.VMEM((length, LANES), F32),
        pltpu.VMEM((rows, width), F32),
        pltpu.VMEM((rows, width), F32),
        pltpu.VMEM((2, 8, 8, width), F32),
        pltpu.VMEM((2, tiles, 8, width), F32),
        pltpu.VMEM((pairs, 4 * rows, LANES), BF16),
        pltpu.VMEM((pairs, HD, 2 * rows), BF16),
        pltpu.VMEM((pairs, 1, 2 * rows), F32),
        pltpu.VMEM((SPAN, 2 * rows), F32),
        pltpu.VMEM((SPAN, 2 * rows), F32),
        pltpu.VMEM((SPAN, 2 * rows), F32),
        pltpu.VMEM((SPAN, 2 * rows), F32),
        pltpu.VMEM((SPAN, 2 * rows), F32),
        pltpu.VMEM((SPAN, 2 * rows), F32),
        pltpu.VMEM((SPAN, 4 * rows), BF16),
        pltpu.VMEM((SPAN, 4 * rows), BF16),
        pltpu.VMEM((SPAN, 4 * rows), BF16),
        *weight_scratch(weights),
        pltpu.SemaphoreType.DMA((2, 6)),
        pltpu.SemaphoreType.DMA((2, 3)),
        pltpu.SemaphoreType.DMA((11,)),
        pltpu.SemaphoreType.DMA((2, N_W)),
    ]
    first_state = 9 + N_W + len(READ)
    outs = pl.pallas_call(
        functools.partial(bwd_kernel, rows, chunks, fresh),
        out_shape=[make_struct(shapes[k]) for k in BWD_STATE] + [jax.ShapeDtypeStruct((rows, width), BF16)],
        in_specs=[SMEM, SMEM, ANY, ANY] + [VMEM] * 5 + [ANY] * (N_W + len(READ) + (0 if fresh else n)),
        out_specs=[ANY] * (n + 1),
        scratch_shapes=scratch,
        input_output_aliases={} if fresh else {first_state + i: i for i in range(n)},
        compiler_params=pltpu.CompilerParams(vmem_limit_bytes=VMEM_LIMIT),
        name="section_backward",
    )(sc, scale, hop, cot, small, cos, ahead, behind, wkv, *weights, *[saved[k] for k in READ], *([] if fresh else state))
    return outs[:n], outs[n]


def turn_tables(length):
    column = jnp.arange(LANES) % HD
    half = ROT // 2
    freq = jnp.power(10000.0, -2.0 * (column % half).astype(F32) / ROT)
    angle = jnp.arange(length).astype(F32)[:, None] * freq[None, :]
    cosines = jnp.where((column < ROT)[None, :], jnp.cos(angle), 1.0)
    sines = jnp.sin(angle)
    ahead = jnp.where((column < half)[None, :], -sines, 0.0)
    behind = jnp.where(((column >= half) & (column < ROT))[None, :], sines, 0.0)
    return cosines, ahead, behind


def stage_place(stage):
    across = stage // 2
    return across, (stage % 2 if across == 0 else 1 - stage % 2)


def device(across, core, tensor):
    return (2 * across + core) * 2 + tensor


PLANE = ("section", "tensor")
SWAP = [(0, 1), (1, 0), (2, 3), (3, 2)]


def plane_routes():
    fetch, ahead = [], []
    for stage in range(4):
        across, tensor = stage_place(stage)
        for core in range(2):
            fetch.append((device(across, stage % 2, core), device(across, core, tensor)))
            if stage < 3:
                after, turned = stage_place(stage + 1)
                ahead.append((device(across, core, tensor), device(after, core, turned)))
    return fetch, [(b, a) for a, b in fetch], ahead, [(b, a) for a, b in ahead]


FETCH, DELIVER, AHEAD, BEHIND = plane_routes()


def same_chip(a, b):
    return a // 4 == b // 4 and a % 2 == b % 2


def among(places):
    here = lax.axis_index(PLANE)
    return sum((here == a).astype(jnp.int32) for a in places) > 0


def both_slots(whole, parity):
    own, other = (lax.dynamic_index_in_dim(whole, p, 0, keepdims=False) for p in (parity, 1 - parity))
    near = routed(own, FETCH)
    size = lax.axis_size("dp")
    linked = [b for a, b in FETCH if not same_chip(a, b)]

    def place(b, z):
        return (b // 2 * size + z) * 2 + b % 2

    passed = lax.ppermute(near, ("section", "dp", "tensor"), [(place(b, z ^ 1), place(b, z)) for b in linked for z in range(size)])
    moved = lax.ppermute(other, PLANE, [(a, b) for a, b in FETCH if a != b and same_chip(a, b)])
    far = jnp.where(among([b for a, b in FETCH if a == b]), other, jnp.where(among(linked), passed, moved))
    return near, far


def routed(value, routes):
    moved = lax.ppermute(value, PLANE, [(a, b) for a, b in routes if a != b])
    return jnp.where(among([a for a, b in routes if a == b]), value, moved)


def other_core(value):
    return lax.ppermute(value, "section", SWAP)


def added(left, right):
    return (left.astype(F32) + right.astype(F32)).astype(BF16)


def after(value, *others):
    return lax.optimization_barrier((value, *others))[0]


def line_sums(count, make):
    position = lax.axis_index("dp")
    at_end = (position == 0) | (position == 3)
    terms, arrived, first, second, third, done = [], [], [], [], [], []

    def tied(value, *links):
        values = [chain[n] for chain, n in links if n >= 0]
        return after(value, *values) if values else value

    def advance(n):
        first.append(added(tied(terms[n], (second, n - 1)), arrived[n]))
        across = lax.ppermute(first[n], "dp", [(1, 2), (2, 1)])
        second.append(added(tied(first[n], (third, n - 1), (done, n - 2)), across))
        third.append(jnp.where(at_end, lax.ppermute(second[n], "dp", [(1, 0), (2, 3)]), second[n]))
        done.append(routed(third[n], DELIVER))

    for n in range(count):
        if n >= 3:
            advance(n - 3)
        mine, theirs = make(n, terms[-2:-1])
        terms.append(tied(added(mine, other_core(theirs)), (first, n - 3), (second, n - 3)))
        arrived.append(lax.ppermute(terms[n], "dp", [(0, 1), (3, 2)]))
    for n in range(max(count - 3, 0), count):
        advance(n)
    return done, first[1]


def local(
    inputs,
    cotangent,
    subset_ids,
    subset_weight,
    ln_gain,
    ln_bias,
    w_query,
    b_query,
    w_kv,
    b_kv,
    w_out,
    out_bias,
    w_in,
    b_in,
    w_hid_out,
):
    section, tensor = lax.axis_index("section"), lax.axis_index("tensor")
    across, core = section // 2, section % 2
    stage = 2 * across + jnp.where(across == 0, tensor, 1 - tensor)
    micro, part, width = inputs.shape
    length = part * lax.axis_size(PLANE)
    half, hid = w_query.shape[3], w_in.shape[3]
    chunks = length // ROWS
    ticks = chunks + 3

    parity = lax.axis_index("dp") % 2
    wholes = (w_in, w_query, w_out, w_hid_out)
    fetched, swapped = zip(*(both_slots(w[0], parity) for w in wholes))
    vectors = jnp.concatenate([v.reshape(-1) for v in (ln_gain, ln_bias, out_bias, b_kv, b_query, b_in)]).reshape(-1, LANES)
    vectors, own_kv = routed(vectors, FETCH), routed(w_kv[0], FETCH)
    early = (fetched[3], vectors, own_kv)
    held = dict(zip("iqoh", zip(fetched, [after(w, *early) for w in fetched], swapped, [after(w, swapped[3]) for w in swapped])))
    weights = []
    for name in "qoih":
        near, tied_near, far, tied_far = held[name]
        weights += [near, far, other_core(tied_near), other_core(tied_far)]
    flat, flat_other = vectors.reshape(-1), other_core(vectors).reshape(-1)
    edge = 12 * width + LANES
    bkv = flat[12 * width : edge]
    bkv = jnp.pad(jnp.concatenate([bkv[:HD], bkv[:HD], bkv[HD:], bkv[HD:]]), (0, width - 2 * LANES))
    bq = jnp.concatenate([f[edge : edge + 2 * half].reshape(2, 1, half) for f in (flat, flat_other)], axis=2)
    bi = jnp.concatenate([f[edge + 2 * half :].reshape(2, hid // width, 1, width) for f in (flat, flat_other)], axis=1)
    norms = [flat[n * 4 * width : (n + 1) * 4 * width].reshape(2, 2, width) for n in range(3)]
    small = jnp.concatenate([*norms, bq, jnp.broadcast_to(bkv, (2, 1, width))], axis=1)
    wide_kv = jnp.concatenate([own_kv[:, :HD], own_kv[:, :HD], own_kv[:, HD:], own_kv[:, HD:]], axis=1)

    whole_in = lax.all_gather(after(inputs, fetched[3]), PLANE, axis=1, tiled=True)
    my_id = lax.dynamic_index_in_dim(subset_ids, core, 0, keepdims=False)
    matches = my_id == jnp.arange(subset_weight.shape[0], dtype=jnp.int32)
    weight = jnp.sum(jnp.where(matches, subset_weight, 0.0))
    is_first, is_last = stage == 0, stage == 3
    scale = jnp.where(is_last, weight, 1.0).reshape(1)

    tables = turn_tables(length)
    forward_params = (small, bi, *tables, wide_kv)
    hop = jnp.zeros((ROWS, width), BF16)
    saved = None
    for tick in range(ticks):
        number = tick - stage
        valid = (number >= 0) & (number < chunks)
        sc = jnp.stack([valid.astype(jnp.int32), jnp.clip(number, 0, chunks - 1), is_first.astype(jnp.int32), parity, core])
        saved, hop = fwd_call(ROWS, saved, sc, hop, whole_in, forward_params, weights)
        if tick == 0:
            whole_cot = lax.all_gather(after(cotangent, hop), PLANE, axis=1, tiled=True)
        if tick < ticks - 1:
            hop = lax.ppermute(hop, PLANE, AHEAD)
    kept = dict(zip(FWD_STATE, saved))

    def spread(mine_only, here):
        rows = jnp.where(here, mine_only, jnp.zeros_like(mine_only))[None]
        canvas = jnp.where((jnp.arange(micro) == core)[:, None, None], rows, jnp.zeros_like(rows))
        return lax.psum_scatter(canvas, PLANE, scatter_dimension=1, tiled=True)

    final = spread(kept["y"], is_last)

    backward_params = (small, *tables, own_kv)
    back = None
    for tick in range(ticks):
        number = chunks - 1 - tick + (3 - stage)
        valid = (number >= 0) & (number < chunks)
        sc = jnp.stack([valid.astype(jnp.int32), jnp.clip(number, 0, chunks - 1), is_last.astype(jnp.int32), parity, core])
        back, hop = bwd_call(ROWS, chunks, back, sc, scale, hop, whole_cot, backward_params, weights, saved)
        if tick < ticks - 1:
            hop = lax.ppermute(hop, PLANE, BEHIND)
    got = dict(zip(BWD_STATE, back))

    def part(values, slot, start, size):
        return lax.slice(values, (slot, 0, start), (slot + 1, length, start + size)).reshape(length, size)

    def product(left, right):
        return dot(left, right, ((0,), (0,))).astype(BF16)

    def outer(slot, ties):
        grad = after(got["db"], *ties) if ties else got["db"]
        both = []
        for k in range(2):
            rows = [
                product(part(kept["o"], slot, k * half, half), part(grad, slot, 0, width)),
                product(part(got["dq"], slot, k * half, half), part(kept["h1"], slot, 0, width)),
            ]
            if slot == 0:
                rows.append(product(got["dkv"], part(kept["h1"], slot, 0, width)))
            both.append(jnp.concatenate(rows))
        return both

    def inner_out(slot, ties):
        grad = after(got["db"], *ties) if ties else got["db"]
        return [product(part(kept["a"], slot, k * hid, hid), part(grad, slot, 0, width)) for k in range(2)]

    def inner_in(slot, ties):
        grad = after(got["du"], *ties) if ties else got["du"]
        return [product(part(kept["h2"], slot, 0, width), part(grad, slot, k * hid, hid)) for k in range(2)]

    makers = (
        lambda ties: outer(1, ties),
        lambda ties: inner_out(1, ties),
        lambda ties: inner_in(1, ties),
        lambda ties: inner_out(0, ties),
        lambda ties: inner_in(0, ties),
        lambda ties: outer(0, ties),
    )
    if lax.axis_size("dp") == 4:
        done, sent = line_sums(len(makers), lambda n, ties: makers[n](ties))
        later = after(got["gin"], sent)
    else:
        done = []
        for make in makers:
            mine, theirs = make([])
            done.append(lax.ppermute(lax.psum(added(mine, other_core(theirs)), "dp"), PLANE, DELIVER))
        later = got["gin"]
    input_grad = spread(later, is_first).astype(F32)
    hid_out_grad = jnp.stack([done[3], done[1]])[None].astype(F32)
    in_grad = jnp.stack([done[4], done[2]])[None].astype(F32)
    out_grad = jnp.stack([done[5][:half], done[0][:half]])[None].astype(F32)
    query_grad = jnp.stack([done[5][half : 2 * half], done[0][half : 2 * half]]).astype(F32)
    query_grad = jnp.swapaxes(query_grad, 1, 2)[None]
    kv_grad = jnp.swapaxes(done[5][2 * half :].astype(F32), 0, 1)[None]

    query = jnp.sum(got["acc"], axis=2)
    inner = jnp.sum(got["accu"], axis=2)
    rolled = jnp.roll(query[:, 5], half, axis=1)
    query = query.at[:, 5].set(jnp.where(core == 0, query[:, 5], rolled))
    inner = jnp.where(core == 0, inner, jnp.roll(inner, hid // width, axis=1))
    acc = jnp.concatenate([query, inner], axis=1)
    acc = acc + other_core(acc)
    acc = lax.ppermute(lax.psum(acc, "dp"), PLANE, DELIVER)
    gain_grad = jnp.stack([acc[:, 1], acc[:, 3]], axis=1)[None]
    bias_grad = jnp.stack([acc[:, 2], acc[:, 4]], axis=1)[None]
    out_bias_grad = jnp.stack([acc[:, 0], acc[:, 0]], axis=1)[None]
    bq_grad = lax.dynamic_slice_in_dim(acc[:, 5], tensor * half, half, axis=1)[None]
    bi_grad = lax.dynamic_slice_in_dim(acc[:, 8:].reshape(2, 2 * hid), tensor * hid, hid, axis=1)[None]
    return (
        final,
        input_grad,
        gain_grad,
        bias_grad,
        query_grad,
        bq_grad,
        kv_grad,
        acc[0, 6, : 2 * HD][None],
        out_grad,
        out_bias_grad,
        in_grad,
        bi_grad,
        hid_out_grad,
    )


def solution(mesh):
    assert mesh.shape["section"] == 4 and mesh.shape["tensor"] == 2
    rows = P("dp", PLANE, None)
    weights = (
        P("section", None, None, None),
        P("section", None, None, None),
        P("section", None, None, "tensor"),
        P("section", None, "tensor"),
        P("section", None, None),
        P("section", None),
        P("section", None, "tensor", None),
        P("section", None, None, None),
        P("section", None, None, "tensor"),
        P("section", None, "tensor"),
        P("section", None, "tensor", None),
    )
    return jax.shard_map(
        local,
        mesh=mesh,
        in_specs=(rows, rows, P("dp"), P(), *weights),
        out_specs=(rows, rows, *weights),
        check_vma=False,
    )
```

```python
import functools
import jax
import jax.numpy as jnp
from jax import lax
from jax.experimental import pallas as pl
from jax.experimental.pallas import tpu as pltpu
from jax.sharding import PartitionSpec as P

HD = 64
ROT = 16
EPS = 1e-05
LANES = 128
ROWS = 256
NORM_ROWS = 256
SPAN = 512
WAYS = 3
VMEM_LIMIT = 60 * 2**20
ANY = pl.BlockSpec(memory_space=pl.ANY)
SMEM = pl.BlockSpec(memory_space=pltpu.SMEM)
VMEM = pl.BlockSpec(memory_space=pltpu.VMEM)
BF16, F32 = jnp.bfloat16, jnp.float32


def dot(left, right, dims=((1,), (0,))):
    return lax.dot_general(left, right, (dims, ((), ())), preferred_element_type=F32)


def dot_nt(left, right):
    return dot(left, right, ((1,), (1,)))


def turn(values, cosines, ahead, behind):
    return (
        values * cosines
        + pltpu.roll(values, LANES - ROT // 2, axis=1) * ahead
        + pltpu.roll(values, ROT // 2, axis=1) * behind
    )


def normalized(rows):
    centred = rows - jnp.mean(rows, axis=-1, keepdims=True)
    scale = lax.rsqrt(jnp.mean(centred * centred, axis=-1, keepdims=True) + EPS)
    return centred * scale, scale


def hidden_from(span, rows, m):
    key = lax.broadcasted_iota(jnp.int32, (SPAN, 2 * rows), 0)
    query = lax.broadcasted_iota(jnp.int32, (SPAN, 2 * rows), 1) & (rows - 1)
    return key > query + (m * rows - span * SPAN)


def side_by_side(pair):
    return jnp.concatenate([pair[:HD], pair[HD:]], axis=1)


def staged(total, stages):
    def turns(t):
        for stage in stages:
            for way in range(WAYS):
                stage(WAYS * t + way, way)

    steps(total // WAYS, turns)


def fold(values):
    return jnp.sum(values.reshape(values.shape[0] // 8, 8, values.shape[1]), axis=0)


def steps(size, body):
    def step(i, _):
        body(i)
        return 0

    lax.fori_loop(0, size, step, 0)


def block_of(i, size):
    return pl.ds(pl.multiple_of(i * size, size), size)


FWD_STATE = ("x", "h1", "h2", "q", "qt", "o", "ot", "a", "g", "l", "kd", "vd", "kt", "vt", "y")
BWD_STATE = ("db", "du", "dq", "dkv", "dkw", "acc", "accu", "gin")
READ = ("x", "q", "qt", "ot", "g", "l", "kd", "vd", "kt")
N_W = 16


def state_shapes(length, width, hidden):
    pairs, tiles = width // LANES, hidden // width
    row, ff, one = ((2, length, width), BF16), ((2, length, hidden), BF16), ((length, width), BF16)
    full, chunks = ((2, length, width), F32), length // ROWS
    lse, turned = ((2, chunks, pairs, 1, 2 * ROWS), F32), (2, chunks, pairs, HD, 2 * ROWS)
    wide, tall, total = ((length, LANES), BF16), ((HD, length), BF16), ((length, LANES), F32)
    fwd = dict(x=full, h1=row, h2=row, q=row, qt=(turned, BF16), o=row, ot=(turned, F32), a=ff, g=ff, l=lse, kd=wide, vd=wide, kt=tall, vt=tall, y=one)
    bwd = dict(db=row, du=ff, dq=row, dkv=wide, dkw=total, acc=((2, 8, 8, width), F32), accu=((2, tiles, 8, width), F32), gin=one)
    return fwd, bwd


def weight_waits(stored, weights, wsems, place):
    return {
        name: [pltpu.make_async_copy(stored[4 * n + 2 * k], weights[2 * n + k].at[place], wsems.at[place, 2 * n + k]) for k in range(2)]
        for n, name in enumerate("qoih")
    }


def start_weights(stored, weights, wsems, place, names):
    for held in range(2):

        @pl.when(place == held)
        def _():
            for name in names:
                n = "qoih".index(name)
                for k in range(2):
                    pltpu.make_async_copy(stored[4 * n + 2 * k + held], weights[2 * n + k].at[held], wsems.at[held, 2 * n + k]).start()


def weight_scratch(weights):
    return [pltpu.VMEM((2, *w.shape), BF16) for w in weights[::2]]


def make_struct(item):
    return jax.ShapeDtypeStruct(*item)


def fwd_kernel(rows, fresh, *refs):
    n_state = len(FWD_STATE)
    sc, hop_in, seq_in, small, bi, cos, ahead, behind, wkv = refs[:9]
    stored = refs[9 : 9 + N_W]
    at = 9 + N_W + (0 if fresh else n_state)
    st = dict(zip(FWD_STATE, refs[at : at + n_state]))
    hop_out = refs[at + n_state]
    (x_s, xf_s, h1_s, h2_s, q_s, qt_s, o_s, ot_s, a_s, g_s, l_s, kd_s, vd_s, kt_s, vt_s, vtc_s, s0_s, s1_s, s2_s, e0_s, e1_s, e2_s, top_s, sum_s, part_s, *weights, sems, once, wsems) = refs[at + n_state + 1 :]
    wq, wo, wi, wh = (weights[2 * i : 2 * i + 2] for i in range(4))
    width = xf_s.shape[2]
    half, hid = wq[0].shape[2], wi[0].shape[2]
    pairs, tiles, length = width // LANES, hid // width, kd_s.shape[0]

    @pl.when(sc[0] == 1)
    def _():
        m = sc[1]
        place = block_of(m, rows)

        @pl.when(sc[2] == 1)
        def _():
            pltpu.make_async_copy(seq_in.at[sc[4], place], x_s, once.at[0]).start()

        @pl.when(sc[2] == 0)
        def _():
            pltpu.make_async_copy(hop_in, x_s, once.at[0]).start()

        start_weights(stored, weights, wsems, sc[3], "q")
        kd_in = pltpu.make_async_copy(st["kd"], kd_s, once.at[1])
        vt_in = pltpu.make_async_copy(st["vt"], vt_s, once.at[2])
        kd_in.start()
        vt_in.start()
        pltpu.make_async_copy(hop_in, x_s, once.at[0]).wait()
        xf_s[0] = x_s[...].astype(F32)
        tables = (cos[place, :], ahead[place, :], behind[place, :])

        def saves(j):
            pairs_of = (("x", xf_s), ("h1", h1_s), ("h2", h2_s), ("q", q_s), ("o", o_s), ("a", a_s), ("g", g_s))
            out = {n: pltpu.make_async_copy(b.at[j], st[n].at[j, place], sems.at[j, i]) for i, (n, b) in enumerate(pairs_of)}
            for i, (n, b) in enumerate((("l", l_s), ("qt", qt_s), ("ot", ot_s))):
                out[n] = pltpu.make_async_copy(b.at[j], st[n].at[j, m], sems.at[j, 7 + i])
            return out

        kv_saves = (
            pltpu.make_async_copy(kd_s.at[place], st["kd"].at[place], once.at[3]),
            pltpu.make_async_copy(vd_s, st["vd"].at[place], once.at[4]),
            pltpu.make_async_copy(kt_s, st["kt"].at[:, place], once.at[5]),
            pltpu.make_async_copy(vtc_s, st["vt"].at[:, place], once.at[6]),
        )

        def layer(j):
            w = j ^ sc[3]
            loads = weight_waits(stored, weights, wsems, w)
            save = saves(j)
            save["x"].start()

            def norm(r):
                span = block_of(r, NORM_ROWS)
                hat, _ = normalized(xf_s[j, span, :])
                h1_s[j, span, :] = (hat * small[j, 0:1, :] + small[j, 2:3, :]).astype(BF16)
                h2_s[j, span, :] = (hat * small[j, 1:2, :] + small[j, 3:4, :]).astype(BF16)

            steps(rows // NORM_ROWS, norm)
            save["h1"].start()
            save["h2"].start()

            @pl.when(j == 0)
            def _():
                kv = dot(h1_s[j], wkv[...]) + small[j, 7:8, : 2 * LANES]
                keys, values = turn(kv[:, :LANES], *tables), kv[:, LANES:]
                kd_in.wait()
                vt_in.wait()
                kd_s[place, :] = keys.astype(BF16)
                vd_s[...] = values.astype(BF16)
                kt_s[...] = jnp.transpose(keys)[:HD].astype(BF16)
                vtc_s[...] = jnp.transpose(values)[:HD].astype(BF16)
                vt_s[:, place] = vtc_s[...]
                for c in range(1, length // rows):

                    @pl.when(m < c)
                    def _():
                        vt_s[:, c * rows : (c + 1) * rows] = jnp.zeros((HD, rows), BF16)

                for copy in kv_saves:
                    copy.start()

            for copy in loads["q"]:
                copy.wait()
            start_weights(stored, weights, wsems, w, "ioh")
            for k in range(2):
                query = dot(h1_s[j], wq[k][w]) + small[j, 6:7, k * half : (k + 1) * half]
                for b in range(half // LANES):
                    block = turn(query[:, b * LANES : (b + 1) * LANES], *tables) * HD**-0.5
                    col = k * half + b * LANES
                    q_s[j, :, col : col + LANES] = block.astype(BF16)
                    qt_s[j, col // LANES] = side_by_side(jnp.transpose(block)).astype(BF16)
            save["q"].start()
            save["qt"].start()

            many = m * rows >= SPAN

            def unit(u):
                return (u >= pairs).astype(jnp.int32), jnp.where(u >= pairs, u - pairs, u)

            def scores(u, slot):
                span, i = unit(u)
                (s0_s, s1_s, s2_s)[slot][...] = dot(kd_s[block_of(span, SPAN), :HD], qt_s[j, i])

            def soften(u, slot):
                span, i = unit(u)
                score = jnp.where(hidden_from(span, rows, m), -1e30, (s0_s, s1_s, s2_s)[slot][...])
                top = jnp.max(score, axis=0, keepdims=True)
                expo = jnp.exp(score - top)
                top_s[u] = top
                sum_s[u] = jnp.sum(expo, axis=0, keepdims=True)
                (e0_s, e1_s, e2_s)[slot][...] = expo.astype(BF16)

            def weigh(u, slot):
                span, i = unit(u)
                part_s[u] = dot(vt_s[:, block_of(span, SPAN)], (e0_s, e1_s, e2_s)[slot][...])

            staged(jnp.where(many, 2 * pairs, pairs), (scores, soften, weigh))

            def gather(i):
                first, second = top_s[i], jnp.where(many, top_s[pairs + i], -1e30)
                top = jnp.maximum(first, second)
                first, second = jnp.exp(first - top), jnp.exp(second - top)
                summed = first * sum_s[i] + jnp.where(many, second * sum_s[pairs + i], 0.0)
                out = first * part_s[i] + jnp.where(many, second * part_s[pairs + i], 0.0)
                out = out / summed
                l_s[j, i] = top + jnp.log(summed)
                ot_s[j, i] = out
                out = jnp.concatenate([out[:, :rows], out[:, rows:]], axis=0)
                o_s[j, :, block_of(i, LANES)] = jnp.transpose(out).astype(BF16)

            steps(pairs, gather)
            for name in ("o", "ot", "l"):
                save[name].start()

            for copy in loads["i"]:
                copy.wait()

            def hidden(t):
                for k in range(2):
                    before = dot(h2_s[j], wi[k][w, :, block_of(t, width)]) + bi[j, k * tiles + t]
                    normal = 0.5 + 0.5 * lax.erf(before * 0.5**0.5)
                    cols = pl.ds(pl.multiple_of(k * hid + t * width, width), width)
                    a_s[j, :, cols] = (before * normal).astype(BF16)
                    slope = normal + before * (jnp.exp(-0.5 * before * before) * 0.3989422804014327)
                    g_s[j, :, cols] = slope.astype(BF16)

            steps(tiles, hidden)

            @pl.when(j == 0)
            def _():
                start_weights(stored, weights, wsems, 1 ^ sc[3], "q")

            save["a"].start()
            save["g"].start()
            for copy in loads["o"] + loads["h"]:
                copy.wait()
            branch = dot(a_s[j, :, :hid], wh[0][w]) + dot(a_s[j, :, hid:], wh[1][w])
            branch += dot(o_s[j, :, :half], wo[0][w]) + dot(o_s[j, :, half:], wo[1][w])
            xf_s[j + 1] = xf_s[j] + (branch + small[j, 4:5, :] + small[j, 5:6, :])

        steps(2, layer)
        x_s[...] = xf_s[2].astype(BF16)
        ends = (
            pltpu.make_async_copy(x_s, st["y"].at[place], once.at[7]),
            pltpu.make_async_copy(x_s, hop_out, once.at[8]),
        )
        for copy in ends:
            copy.start()
        for j in range(2):
            for copy in saves(j).values():
                copy.wait()
        for copy in kv_saves + ends:
            copy.wait()


def fwd_call(rows, state, sc, hop, seq, params, weights):
    small, bi, cos, ahead, behind, wkv = params
    _, length, width = seq.shape
    half, hid = weights[0].shape[1], weights[8].shape[1]
    hidden, pairs = 2 * hid, width // LANES
    shapes, _ = state_shapes(length, width, hidden)
    fresh = state is None
    n = len(FWD_STATE)
    scratch = [
        pltpu.VMEM((rows, width), BF16),
        pltpu.VMEM((3, rows, width), F32),
        pltpu.VMEM((2, rows, width), BF16),
        pltpu.VMEM((2, rows, width), BF16),
        pltpu.VMEM((2, rows, width), BF16),
        pltpu.VMEM((2, pairs, HD, 2 * rows), BF16),
        pltpu.VMEM((2, rows, width), BF16),
        pltpu.VMEM((2, pairs, HD, 2 * rows), F32),
        pltpu.VMEM((2, rows, hidden), BF16),
        pltpu.VMEM((2, rows, hidden), BF16),
        pltpu.VMEM((2, pairs, 1, 2 * rows), F32),
        pltpu.VMEM((length, LANES), BF16),
        pltpu.VMEM((rows, LANES), BF16),
        pltpu.VMEM((HD, rows), BF16),
        pltpu.VMEM((HD, length), BF16),
        pltpu.VMEM((HD, rows), BF16),
        pltpu.VMEM((SPAN, 2 * rows), F32),
        pltpu.VMEM((SPAN, 2 * rows), F32),
        pltpu.VMEM((SPAN, 2 * rows), F32),
        pltpu.VMEM((SPAN, 2 * rows), BF16),
        pltpu.VMEM((SPAN, 2 * rows), BF16),
        pltpu.VMEM((SPAN, 2 * rows), BF16),
        pltpu.VMEM((2 * pairs, 1, 2 * rows), F32),
        pltpu.VMEM((2 * pairs, 1, 2 * rows), F32),
        pltpu.VMEM((2 * pairs, HD, 2 * rows), F32),
        *weight_scratch(weights),
        pltpu.SemaphoreType.DMA((2, 10)),
        pltpu.SemaphoreType.DMA((9,)),
        pltpu.SemaphoreType.DMA((2, N_W)),
    ]
    outs = pl.pallas_call(
        functools.partial(fwd_kernel, rows, fresh),
        out_shape=[make_struct(shapes[k]) for k in FWD_STATE] + [jax.ShapeDtypeStruct((rows, width), BF16)],
        in_specs=[SMEM, ANY, ANY] + [VMEM] * 6 + [ANY] * (N_W + (0 if fresh else n)),
        out_specs=[ANY] * (n + 1),
        scratch_shapes=scratch,
        input_output_aliases={} if fresh else {9 + N_W + i: i for i in range(n)},
        compiler_params=pltpu.CompilerParams(vmem_limit_bytes=VMEM_LIMIT),
        name="section_forward",
    )(sc, hop, seq, small, bi, cos, ahead, behind, wkv, *weights, *([] if fresh else state))
    return outs[:n], outs[n]


def bwd_kernel(rows, chunks, fresh, *refs):
    n_read, n_state = len(READ), len(BWD_STATE)
    sc, scale, hop_in, cot, small, cos, ahead, behind, wkv = refs[:9]
    stored = refs[9 : 9 + N_W]
    at = 9 + N_W
    rd = dict(zip(READ, refs[at : at + n_read]))
    at += n_read + (0 if fresh else n_state)
    st = dict(zip(BWD_STATE, refs[at : at + n_state]))
    hop_out = refs[at + n_state]
    (in_s, dy_s, x_s, q_s, qt_s, ot_s, g_s, l_s, kd_s, vd_s, kt_s, db_s, do_s, du_s, dq_s, dqt_s, dkv_s, dkw_s, dh1_s, dh2_s, acc_s, accu_s, two_s, dot_s, d_s, s0_s, s1_s, s2_s, dp0_s, dp1_s, dp2_s, both0_s, both1_s, both2_s, *weights, sems, outs, once, wsems) = refs[at + n_state + 1 :]
    wq, wo, wi, wh = (weights[2 * i : 2 * i + 2] for i in range(4))
    width = dy_s.shape[1]
    half, hid = wq[0].shape[2], wi[0].shape[2]
    pairs, tiles, length = width // LANES, hid // width, kd_s.shape[0]

    @pl.when(sc[0] == 1)
    def _():
        m = sc[1]
        place = block_of(m, rows)

        @pl.when(sc[2] == 1)
        def _():
            pltpu.make_async_copy(cot.at[sc[4], place], in_s, once.at[0]).start()

        @pl.when(sc[2] == 0)
        def _():
            pltpu.make_async_copy(hop_in, in_s, once.at[0]).start()

        def gets(j):
            named = (("g", g_s), ("q", q_s), ("x", x_s))
            got = {n: pltpu.make_async_copy(rd[n].at[j, place], b.at[j], sems.at[j, i]) for i, (n, b) in enumerate(named)}
            for i, (n, b) in enumerate((("l", l_s), ("qt", qt_s), ("ot", ot_s))):
                got[n] = pltpu.make_async_copy(rd[n].at[j, m], b.at[j], sems.at[j, 3 + i])
            return got

        shared = [pltpu.make_async_copy(rd[n], b, once.at[1 + i]) for i, (n, b) in enumerate((("kd", kd_s), ("vd", vd_s), ("kt", kt_s)))]
        def fetch(j):
            start_weights(stored, weights, wsems, j ^ sc[3], "o")
            for copy in gets(j).values():
                copy.start()

        fetch(1)
        for copy in shared:
            copy.start()
        running = (("dkw", dkw_s), ("acc", acc_s), ("accu", accu_s))

        @pl.when(m == chunks - 1)
        def _():
            for _, buf in running:
                buf[...] = jnp.zeros_like(buf)

        @pl.when(m < chunks - 1)
        def _():
            copies = [pltpu.make_async_copy(st[n], b, once.at[4 + i]) for i, (n, b) in enumerate(running)]
            for copy in copies:
                copy.start()
            for copy in copies:
                copy.wait()

        pltpu.make_async_copy(hop_in, in_s, once.at[0]).wait()
        dy_s[...] = in_s[...].astype(F32) * scale[0]
        tables = (cos[place, :], -ahead[place, :], -behind[place, :])

        def saves(j):
            named = (("db", db_s), ("du", du_s), ("dq", dq_s))
            return {n: pltpu.make_async_copy(b.at[j], st[n].at[j, place], outs.at[j, i]) for i, (n, b) in enumerate(named)}

        kv_save = pltpu.make_async_copy(dkv_s, st["dkv"].at[place], once.at[8])

        def layer(step):
            j = 1 - step
            w = j ^ sc[3]
            loads = weight_waits(stored, weights, wsems, w)
            got, save = gets(j), saves(j)
            grad = dy_s[...]
            db_s[j] = grad.astype(BF16)
            acc_s[j, 0] += fold(grad)
            save["db"].start()
            for copy in loads["o"]:
                copy.wait()
            start_weights(stored, weights, wsems, w, "qhi")
            for k in range(2):
                do_s[:, k * half : (k + 1) * half] = dot_nt(db_s[j], wo[k][w]).astype(BF16)
            for name in ("ot", "q", "qt", "l"):
                got[name].wait()

            @pl.when(j == 1)
            def _():
                for copy in shared:
                    copy.wait()

            def ready(i):
                cols = block_of(i, LANES)
                out_grad = do_s[:, cols].astype(F32)
                turned = side_by_side(jnp.transpose(out_grad))
                d_s[i] = jnp.sum(turned * ot_s[j, i], axis=0, keepdims=True)
                dot_s[i] = turned.astype(BF16)
                query = q_s[j, :, cols].astype(F32)
                low = lax.broadcasted_iota(jnp.int32, query.shape, 1) < HD
                parts = (
                    jnp.where(low, query, 0.0),
                    jnp.where(low, pltpu.roll(query, HD, axis=1), 0.0),
                    jnp.where(low, 0.0, pltpu.roll(out_grad, HD, axis=1)),
                    jnp.where(low, 0.0, out_grad),
                )
                for n, part in enumerate(parts):
                    two_s[i, n * rows : (n + 1) * rows, :] = part.astype(BF16)

            steps(pairs, ready)

            def unit(u):
                return (u >= pairs).astype(jnp.int32), jnp.where(u >= pairs, u - pairs, u)

            def scores(u, slot):
                span, i = unit(u)
                (s0_s, s1_s, s2_s)[slot][...] = dot(kd_s[block_of(span, SPAN), :HD], qt_s[j, i])
                (dp0_s, dp1_s, dp2_s)[slot][...] = dot(vd_s[block_of(span, SPAN), :HD], dot_s[i])

            def soften(u, slot):
                span, i = unit(u)
                probs = jnp.where(hidden_from(span, rows, m), 0.0, jnp.exp((s0_s, s1_s, s2_s)[slot][...] - l_s[j, i]))
                both = (both0_s, both1_s, both2_s)[slot]
                both[:, : 2 * rows] = (probs * ((dp0_s, dp1_s, dp2_s)[slot][...] - d_s[i])).astype(BF16)
                both[:, 2 * rows :] = probs.astype(BF16)

            def weigh(u, slot):
                span, i = unit(u)
                place = block_of(span, SPAN)
                dqt_s[u] = dot(kt_s[:, place], (both0_s, both1_s, both2_s)[slot][:, : 2 * rows])
                part = dot((both0_s, both1_s, both2_s)[slot][...], two_s[i])

                dkw_s[place, :] += part

            many = m * rows >= SPAN
            staged(jnp.where(many, 2 * pairs, pairs), (scores, soften, weigh))

            def finish(i):
                grad = dqt_s[i] + jnp.where(many, dqt_s[pairs + i], 0.0)
                grad = jnp.concatenate([grad[:, :rows], grad[:, rows:]], axis=0)
                turned = turn(jnp.transpose(grad) * HD**-0.5, *tables)
                dq_s[j, :, block_of(i, LANES)] = turned.astype(BF16)

            steps(pairs, finish)
            save["dq"].start()
            acc_s[j, 5] += fold(dq_s[j].astype(F32))
            for copy in loads["q"]:
                copy.wait()

            @pl.when(j == 1)
            def _():
                fetch(0)

            dh1_s[...] = dot_nt(dq_s[j, :, :half], wq[0][w]) + dot_nt(dq_s[j, :, half:], wq[1][w])

            @pl.when(j == 0)
            def _():
                both = dkw_s[place, :]
                low = lax.broadcasted_iota(jnp.int32, both.shape, 1) < HD
                both = jnp.where(low, turn(both, *tables), both).astype(BF16)
                dkv_s[...] = both
                kv_save.start()
                acc_s[j, 6, :, :LANES] += fold(both.astype(F32))
                dh1_s[...] += dot_nt(both, wkv[...])

            got["g"].wait()
            for copy in loads["h"] + loads["i"]:
                copy.wait()

            def hidden(t):
                for k in range(2):
                    cols = pl.ds(pl.multiple_of(k * hid + t * width, width), width)
                    back = dot_nt(db_s[j], wh[k][w, block_of(t, width), :])
                    back = (back * g_s[j, :, cols].astype(F32)).astype(BF16)
                    du_s[j, :, cols] = back
                    accu_s[j, k * tiles + t] += fold(back.astype(F32))

            steps(tiles, hidden)
            save["du"].start()
            dh2_s[...] = dot_nt(du_s[j, :, :hid], wi[0][w]) + dot_nt(du_s[j, :, hid:], wi[1][w])
            got["x"].wait()

            def norm(r):
                span = block_of(r, NORM_ROWS)
                hat, spread = normalized(x_s[j, span, :])
                first, second = dh1_s[span, :], dh2_s[span, :]
                for i, v in enumerate((first * hat, first, second * hat, second)):
                    acc_s[j, 1 + i] += fold(v)
                inside = first * small[j, 0:1, :] + second * small[j, 1:2, :]
                shift = jnp.mean(inside, axis=-1, keepdims=True)
                tilt = jnp.mean(inside * hat, axis=-1, keepdims=True)
                dy_s[span, :] += spread * (inside - shift - hat * tilt)

            steps(rows // NORM_ROWS, norm)

        steps(2, layer)
        in_s[...] = dy_s[...].astype(BF16)
        ends = [pltpu.make_async_copy(in_s, st["gin"].at[place], once.at[9]), pltpu.make_async_copy(in_s, hop_out, once.at[10])]
        ends += [pltpu.make_async_copy(b, st[n], once.at[4 + i]) for i, (n, b) in enumerate(running)]
        for copy in ends:
            copy.start()
        for j in range(2):
            for copy in saves(j).values():
                copy.wait()
        for copy in ends + [kv_save]:
            copy.wait()


def bwd_call(rows, chunks, state, sc, scale, hop, cot, params, weights, fwd):
    small, cos, ahead, behind, wkv = params
    _, length, width = cot.shape
    half, hid = weights[0].shape[1], weights[8].shape[1]
    hidden, pairs, tiles = 2 * hid, width // LANES, 2 * hid // width
    _, shapes = state_shapes(length, width, hidden)
    fresh = state is None
    n = len(BWD_STATE)
    saved = dict(zip(FWD_STATE, fwd))
    scratch = [
        pltpu.VMEM((rows, width), BF16),
        pltpu.VMEM((rows, width), F32),
        pltpu.VMEM((2, rows, width), F32),
        pltpu.VMEM((2, rows, width), BF16),
        pltpu.VMEM((2, pairs, HD, 2 * rows), BF16),
        pltpu.VMEM((2, pairs, HD, 2 * rows), F32),
        pltpu.VMEM((2, rows, hidden), BF16),
        pltpu.VMEM((2, pairs, 1, 2 * rows), F32),
        pltpu.VMEM((length, LANES), BF16),
        pltpu.VMEM((length, LANES), BF16),
        pltpu.VMEM((HD, length), BF16),
        pltpu.VMEM((2, rows, width), BF16),
        pltpu.VMEM((rows, width), BF16),
        pltpu.VMEM((2, rows, hidden), BF16),
        pltpu.VMEM((2, rows, width), BF16),
        pltpu.VMEM((2 * pairs, HD, 2 * rows), F32),
        pltpu.VMEM((rows, LANES), BF16),
        pltpu.VMEM((length, LANES), F32),
        pltpu.VMEM((rows, width), F32),
        pltpu.VMEM((rows, width), F32),
        pltpu.VMEM((2, 8, 8, width), F32),
        pltpu.VMEM((2, tiles, 8, width), F32),
        pltpu.VMEM((pairs, 4 * rows, LANES), BF16),
        pltpu.VMEM((pairs, HD, 2 * rows), BF16),
        pltpu.VMEM((pairs, 1, 2 * rows), F32),
        pltpu.VMEM((SPAN, 2 * rows), F32),
        pltpu.VMEM((SPAN, 2 * rows), F32),
        pltpu.VMEM((SPAN, 2 * rows), F32),
        pltpu.VMEM((SPAN, 2 * rows), F32),
        pltpu.VMEM((SPAN, 2 * rows), F32),
        pltpu.VMEM((SPAN, 2 * rows), F32),
        pltpu.VMEM((SPAN, 4 * rows), BF16),
        pltpu.VMEM((SPAN, 4 * rows), BF16),
        pltpu.VMEM((SPAN, 4 * rows), BF16),
        *weight_scratch(weights),
        pltpu.SemaphoreType.DMA((2, 6)),
        pltpu.SemaphoreType.DMA((2, 3)),
        pltpu.SemaphoreType.DMA((11,)),
        pltpu.SemaphoreType.DMA((2, N_W)),
    ]
    first_state = 9 + N_W + len(READ)
    outs = pl.pallas_call(
        functools.partial(bwd_kernel, rows, chunks, fresh),
        out_shape=[make_struct(shapes[k]) for k in BWD_STATE] + [jax.ShapeDtypeStruct((rows, width), BF16)],
        in_specs=[SMEM, SMEM, ANY, ANY] + [VMEM] * 5 + [ANY] * (N_W + len(READ) + (0 if fresh else n)),
        out_specs=[ANY] * (n + 1),
        scratch_shapes=scratch,
        input_output_aliases={} if fresh else {first_state + i: i for i in range(n)},
        compiler_params=pltpu.CompilerParams(vmem_limit_bytes=VMEM_LIMIT),
        name="section_backward",
    )(sc, scale, hop, cot, small, cos, ahead, behind, wkv, *weights, *[saved[k] for k in READ], *([] if fresh else state))
    return outs[:n], outs[n]


def turn_tables(length):
    column = jnp.arange(LANES) % HD
    half = ROT // 2
    freq = jnp.power(10000.0, -2.0 * (column % half).astype(F32) / ROT)
    angle = jnp.arange(length).astype(F32)[:, None] * freq[None, :]
    cosines = jnp.where((column < ROT)[None, :], jnp.cos(angle), 1.0)
    sines = jnp.sin(angle)
    ahead = jnp.where((column < half)[None, :], -sines, 0.0)
    behind = jnp.where(((column >= half) & (column < ROT))[None, :], sines, 0.0)
    return cosines, ahead, behind


def stage_place(stage):
    across = stage // 2
    return across, (stage % 2 if across == 0 else 1 - stage % 2)


def device(across, core, tensor):
    return (2 * across + core) * 2 + tensor


PLANE = ("section", "tensor")
SWAP = [(0, 1), (1, 0), (2, 3), (3, 2)]


def plane_routes():
    fetch, ahead = [], []
    for stage in range(4):
        across, tensor = stage_place(stage)
        for core in range(2):
            fetch.append((device(across, stage % 2, core), device(across, core, tensor)))
            if stage < 3:
                after, turned = stage_place(stage + 1)
                ahead.append((device(across, core, tensor), device(after, core, turned)))
    return fetch, [(b, a) for a, b in fetch], ahead, [(b, a) for a, b in ahead]


FETCH, DELIVER, AHEAD, BEHIND = plane_routes()


def same_chip(a, b):
    return a // 4 == b // 4 and a % 2 == b % 2


def among(places):
    here = lax.axis_index(PLANE)
    return sum((here == a).astype(jnp.int32) for a in places) > 0


def both_slots(whole, parity):
    own, other = (lax.dynamic_index_in_dim(whole, p, 0, keepdims=False) for p in (parity, 1 - parity))
    near = routed(own, FETCH)
    size = lax.axis_size("dp")
    linked = [b for a, b in FETCH if not same_chip(a, b)]

    def place(b, z):
        return (b // 2 * size + z) * 2 + b % 2

    passed = lax.ppermute(near, ("section", "dp", "tensor"), [(place(b, z ^ 1), place(b, z)) for b in linked for z in range(size)])
    moved = lax.ppermute(other, PLANE, [(a, b) for a, b in FETCH if a != b and same_chip(a, b)])
    far = jnp.where(among([b for a, b in FETCH if a == b]), other, jnp.where(among(linked), passed, moved))
    return near, far


def routed(value, routes):
    moved = lax.ppermute(value, PLANE, [(a, b) for a, b in routes if a != b])
    return jnp.where(among([a for a, b in routes if a == b]), value, moved)


def other_core(value):
    return lax.ppermute(value, "section", SWAP)


def added(left, right):
    return (left.astype(F32) + right.astype(F32)).astype(BF16)


def after(value, *others):
    return lax.optimization_barrier((value, *others))[0]


def line_sums(count, make):
    position = lax.axis_index("dp")
    at_end = (position == 0) | (position == 3)
    terms, arrived, first, second, third, done = [], [], [], [], [], []

    def tied(value, *links):
        values = [chain[n] for chain, n in links if n >= 0]
        return after(value, *values) if values else value

    def advance(n):
        first.append(added(tied(terms[n], (second, n - 1)), arrived[n]))
        across = lax.ppermute(first[n], "dp", [(1, 2), (2, 1)])
        second.append(added(tied(first[n], (third, n - 1), (done, n - 2)), across))
        third.append(jnp.where(at_end, lax.ppermute(second[n], "dp", [(1, 0), (2, 3)]), second[n]))
        done.append(routed(third[n], DELIVER))

    for n in range(count):
        if n >= 3:
            advance(n - 3)
        mine, theirs = make(n, terms[-2:-1])
        terms.append(tied(added(mine, other_core(theirs)), (first, n - 3), (second, n - 3)))
        arrived.append(lax.ppermute(terms[n], "dp", [(0, 1), (3, 2)]))
    for n in range(max(count - 3, 0), count):
        advance(n)
    return done, first[1]


def local(
    inputs,
    cotangent,
    subset_ids,
    subset_weight,
    ln_gain,
    ln_bias,
    w_query,
    b_query,
    w_kv,
    b_kv,
    w_out,
    out_bias,
    w_in,
    b_in,
    w_hid_out,
):
    section, tensor = lax.axis_index("section"), lax.axis_index("tensor")
    across, core = section // 2, section % 2
    stage = 2 * across + jnp.where(across == 0, tensor, 1 - tensor)
    micro, part, width = inputs.shape
    length = part * lax.axis_size(PLANE)
    half, hid = w_query.shape[3], w_in.shape[3]
    chunks = length // ROWS
    ticks = chunks + 3

    parity = lax.axis_index("dp") % 2
    wholes = (w_in, w_query, w_out, w_hid_out)
    fetched, swapped = zip(*(both_slots(w[0], parity) for w in wholes))
    vectors = jnp.concatenate([v.reshape(-1) for v in (ln_gain, ln_bias, out_bias, b_kv, b_query, b_in)]).reshape(-1, LANES)
    vectors, own_kv = routed(vectors, FETCH), routed(w_kv[0], FETCH)
    early = (fetched[3], vectors, own_kv)
    held = dict(zip("iqoh", zip(fetched, [after(w, *early) for w in fetched], swapped, [after(w, swapped[3]) for w in swapped])))
    weights = []
    for name in "qoih":
        near, tied_near, far, tied_far = held[name]
        weights += [near, far, other_core(tied_near), other_core(tied_far)]
    flat, flat_other = vectors.reshape(-1), other_core(vectors).reshape(-1)
    edge = 12 * width + LANES
    bkv = flat[12 * width : edge]
    bkv = jnp.pad(jnp.concatenate([bkv[:HD], bkv[:HD], bkv[HD:], bkv[HD:]]), (0, width - 2 * LANES))
    bq = jnp.concatenate([f[edge : edge + 2 * half].reshape(2, 1, half) for f in (flat, flat_other)], axis=2)
    bi = jnp.concatenate([f[edge + 2 * half :].reshape(2, hid // width, 1, width) for f in (flat, flat_other)], axis=1)
    norms = [flat[n * 4 * width : (n + 1) * 4 * width].reshape(2, 2, width) for n in range(3)]
    small = jnp.concatenate([*norms, bq, jnp.broadcast_to(bkv, (2, 1, width))], axis=1)
    wide_kv = jnp.concatenate([own_kv[:, :HD], own_kv[:, :HD], own_kv[:, HD:], own_kv[:, HD:]], axis=1)

    whole_in = lax.all_gather(after(inputs, fetched[3]), PLANE, axis=1, tiled=True)
    my_id = lax.dynamic_index_in_dim(subset_ids, core, 0, keepdims=False)
    matches = my_id == jnp.arange(subset_weight.shape[0], dtype=jnp.int32)
    weight = jnp.sum(jnp.where(matches, subset_weight, 0.0))
    is_first, is_last = stage == 0, stage == 3
    scale = jnp.where(is_last, weight, 1.0).reshape(1)

    tables = turn_tables(length)
    forward_params = (small, bi, *tables, wide_kv)
    hop = jnp.zeros((ROWS, width), BF16)
    saved = None
    for tick in range(ticks):
        number = tick - stage
        valid = (number >= 0) & (number < chunks)
        sc = jnp.stack([valid.astype(jnp.int32), jnp.clip(number, 0, chunks - 1), is_first.astype(jnp.int32), parity, core])
        saved, hop = fwd_call(ROWS, saved, sc, hop, whole_in, forward_params, weights)
        if tick == 0:
            whole_cot = lax.all_gather(after(cotangent, hop), PLANE, axis=1, tiled=True)
        if tick < ticks - 1:
            hop = lax.ppermute(hop, PLANE, AHEAD)
    kept = dict(zip(FWD_STATE, saved))

    def spread(mine_only, here):
        rows = jnp.where(here, mine_only, jnp.zeros_like(mine_only))[None]
        canvas = jnp.where((jnp.arange(micro) == core)[:, None, None], rows, jnp.zeros_like(rows))
        return lax.psum_scatter(canvas, PLANE, scatter_dimension=1, tiled=True)

    final = spread(kept["y"], is_last)

    backward_params = (small, *tables, own_kv)
    back = None
    for tick in range(ticks):
        number = chunks - 1 - tick + (3 - stage)
        valid = (number >= 0) & (number < chunks)
        sc = jnp.stack([valid.astype(jnp.int32), jnp.clip(number, 0, chunks - 1), is_last.astype(jnp.int32), parity, core])
        back, hop = bwd_call(ROWS, chunks, back, sc, scale, hop, whole_cot, backward_params, weights, saved)
        if tick < ticks - 1:
            hop = lax.ppermute(hop, PLANE, BEHIND)
    got = dict(zip(BWD_STATE, back))

    def part(values, slot, start, size):
        return lax.slice(values, (slot, 0, start), (slot + 1, length, start + size)).reshape(length, size)

    def product(left, right):
        return dot(left, right, ((0,), (0,))).astype(BF16)

    def outer(slot, ties):
        grad = after(got["db"], *ties) if ties else got["db"]
        both = []
        for k in range(2):
            rows = [
                product(part(kept["o"], slot, k * half, half), part(grad, slot, 0, width)),
                product(part(got["dq"], slot, k * half, half), part(kept["h1"], slot, 0, width)),
            ]
            if slot == 0:
                rows.append(product(got["dkv"], part(kept["h1"], slot, 0, width)))
            both.append(jnp.concatenate(rows))
        return both

    def inner_out(slot, ties):
        grad = after(got["db"], *ties) if ties else got["db"]
        return [product(part(kept["a"], slot, k * hid, hid), part(grad, slot, 0, width)) for k in range(2)]

    def inner_in(slot, ties):
        grad = after(got["du"], *ties) if ties else got["du"]
        return [product(part(kept["h2"], slot, 0, width), part(grad, slot, k * hid, hid)) for k in range(2)]

    makers = (
        lambda ties: outer(1, ties),
        lambda ties: inner_out(1, ties),
        lambda ties: inner_in(1, ties),
        lambda ties: inner_out(0, ties),
        lambda ties: inner_in(0, ties),
        lambda ties: outer(0, ties),
    )
    if lax.axis_size("dp") == 4:
        done, sent = line_sums(len(makers), lambda n, ties: makers[n](ties))
        later = after(got["gin"], sent)
    else:
        done = []
        for make in makers:
            mine, theirs = make([])
            done.append(lax.ppermute(lax.psum(added(mine, other_core(theirs)), "dp"), PLANE, DELIVER))
        later = got["gin"]
    input_grad = spread(later, is_first).astype(F32)
    hid_out_grad = jnp.stack([done[3], done[1]])[None].astype(F32)
    in_grad = jnp.stack([done[4], done[2]])[None].astype(F32)
    out_grad = jnp.stack([done[5][:half], done[0][:half]])[None].astype(F32)
    query_grad = jnp.stack([done[5][half : 2 * half], done[0][half : 2 * half]]).astype(F32)
    query_grad = jnp.swapaxes(query_grad, 1, 2)[None]
    kv_grad = jnp.swapaxes(done[5][2 * half :].astype(F32), 0, 1)[None]

    query = jnp.sum(got["acc"], axis=2)
    inner = jnp.sum(got["accu"], axis=2)
    rolled = jnp.roll(query[:, 5], half, axis=1)
    query = query.at[:, 5].set(jnp.where(core == 0, query[:, 5], rolled))
    inner = jnp.where(core == 0, inner, jnp.roll(inner, hid // width, axis=1))
    acc = jnp.concatenate([query, inner], axis=1)
    acc = acc + other_core(acc)
    acc = lax.ppermute(lax.psum(acc, "dp"), PLANE, DELIVER)
    gain_grad = jnp.stack([acc[:, 1], acc[:, 3]], axis=1)[None]
    bias_grad = jnp.stack([acc[:, 2], acc[:, 4]], axis=1)[None]
    out_bias_grad = jnp.stack([acc[:, 0], acc[:, 0]], axis=1)[None]
    bq_grad = lax.dynamic_slice_in_dim(acc[:, 5], tensor * half, half, axis=1)[None]
    bi_grad = lax.dynamic_slice_in_dim(acc[:, 8:].reshape(2, 2 * hid), tensor * hid, hid, axis=1)[None]
    return (
        final,
        input_grad,
        gain_grad,
        bias_grad,
        query_grad,
        bq_grad,
        kv_grad,
        acc[0, 6, : 2 * HD][None],
        out_grad,
        out_bias_grad,
        in_grad,
        bi_grad,
        hid_out_grad,
    )


def solution(mesh):
    assert mesh.shape["section"] == 4 and mesh.shape["tensor"] == 2
    rows = P("dp", PLANE, None)
    weights = (
        P("section", None, None, None),
        P("section", None, None, None),
        P("section", None, None, "tensor"),
        P("section", None, "tensor"),
        P("section", None, None),
        P("section", None),
        P("section", None, "tensor", None),
        P("section", None, None, None),
        P("section", None, None, "tensor"),
        P("section", None, "tensor"),
        P("section", None, "tensor", None),
    )
    return jax.shard_map(
        local,
        mesh=mesh,
        in_specs=(rows, rows, P("dp"), P(), *weights),
        out_specs=(rows, rows, *weights),
        check_vma=False,
    )
```
